32 devices in a mesh: dp: 4 (over y, x), row: 4 (over z), col: 2 (over core).
Axes of the slice: x: 2, y: 2, z: 4, core: 2. Of those that a mesh axis runs over, the one named last changes fastest.
Arguments:
- tokens_in: bfloat16 [16384, 1024], P(('dp', 'row'), 'col'), may hold values from -6 to 6
- cotangent: bfloat16 [16384, 1024], P(('dp', 'row'), 'col'), may hold values from -6 to 6
- prefix_length: int32 [16], P(('dp', 'row')), may hold values from 102 to 512
- first_gain: float32 [1024], P('col'), may hold values from 0.1 to 1.9
- first_shift: float32 [1024], P('col'), may hold values from -4 to 4
- joint_weight: bfloat16 [1024, 3072], P('row', 'col'), may hold values from -0.1875 to 0.1875
- joint_bias: float32 [2048], P('col'), may hold values from -6 to 6
- output_weight: bfloat16 [1024, 1024], P('col', 'row'), may hold values from -3 to 3
- output_bias: float32 [1024], P('col'), may hold values from -4 to 4
- second_gain: float32 [1024], P('col'), may hold values from 0.1 to 1.9
- second_shift: float32 [1024], P('col'), may hold values from -4 to 4
- up_weight: bfloat16 [1024, 4096], P('row', 'col'), may hold values from -0.1875 to 0.1875
- up_bias: float32 [4096], P('col'), may hold values from -6 to 6
- down_weight: bfloat16 [4096, 1024], P('col', 'row'), may hold values from -0.09375 to 0.09375
- down_bias: float32 [1024], P('col'), may hold values from -4 to 4
Outputs:
- layer_out: bfloat16 [16384, 1024], P(('dp', 'row'), 'col')
- tokens_grad: bfloat16 [16384, 1024], P(('dp', 'row'), 'col')
- grad_first_gain: float32 [1024], P('col')
- grad_first_shift: float32 [1024], P('col')
- grad_joint_weight: float32 [1024, 3072], P('row', 'col')
- grad_joint_bias: float32 [2048], P('col')
- grad_output_weight: float32 [1024, 1024], P('col', 'row')
- grad_output_bias: float32 [1024], P('col')
- grad_second_gain: float32 [1024], P('col')
- grad_second_shift: float32 [1024], P('col')
- grad_up_weight: float32 [1024, 4096], P('row', 'col')
- grad_up_bias: float32 [4096], P('col')
- grad_down_weight: float32 [4096, 1024], P('col', 'row')
- grad_down_bias: float32 [1024], P('col')
The draws below stay inside these ranges and needn't reach their ends.
All inputs are finite; a program needn't handle non-finite values.
Results may differ from the reference program's by a relative error of at most 0.015.
Values may be sent and summed in bfloat16 or wider, within the bound.
No kernel may reach another device: no remote copies, remote signals or barrier semaphores. Data moves between devices by JAX's collectives and lax.ppermute only.
A program may use at most 128 MiB of HBM per device.

```python
import math
import jax
import jax.numpy as jnp
from jax import lax

D = 1024
HEADS = 8
HDIM = 128
FF = 4096
LEN = 1024
SEQS = 16
TOKENS = 16384


def set_ends(result, stream_key, least, largest):
    spot = [jax.random.randint(jax.random.fold_in(stream_key, axis), (), 0, length) for axis, length in enumerate(result.shape)]
    main_axis = result.shape.index(max(result.shape))
    neighbour = spot[:main_axis] + [(spot[main_axis] + 1) % result.shape[main_axis]] + spot[main_axis + 1:]
    return result.at[tuple(spot)].set(least).at[tuple(neighbour)].set(largest)


def block_scale(key, extent, pieces, low, largest):
    gain = 1.0
    for dim, blocks in pieces:
        heights = jax.random.uniform(jax.random.fold_in(jax.random.fold_in(key, 6), dim), (blocks,), jnp.float32, low / len(pieces), largest / len(pieces))
        gain = gain * jnp.repeat(jnp.exp(heights), extent[dim] // blocks).reshape((-1,) + (1,) * (len(extent) - 1 - dim))
    return gain


def centred(stream_key, dims, scale, most, shards=(), kind=jnp.bfloat16):
    factor_of = block_scale(stream_key, dims, shards, -0.22, 0.18) if shards else 1.0
    drawn = jax.random.normal(stream_key, dims, jnp.float32) * scale * factor_of
    return jnp.minimum(jnp.maximum(drawn, -most), most).astype(kind)


def setup_inputs(seed: int = 0) -> dict:
    keys = jax.random.split(jax.random.key(seed), 16)
    return {
        "tokens_in": centred(keys[0], (TOKENS, D), 1.0, 6.0, ((0, 16), (1, 2))),
        "cotangent": centred(keys[1], (TOKENS, D), 1.0, 6.0, ((0, 16), (1, 2))),
        "prefix_length": set_ends(jax.random.randint(keys[2], (SEQS,), LEN // 10, LEN // 2 + 1), jax.random.fold_in(keys[2], 1), LEN // 10, (LEN // 2 + 1) - 1).astype(jnp.int32),
        "first_gain": jnp.clip(1.0 + 0.18 * jax.random.normal(keys[3], (D,), jnp.float32), 0.1, 1.9),
        "first_shift": centred(keys[4], (D,), 0.3, 4.0, ((0, 2),), jnp.float32),
        "joint_weight": centred(keys[5], (D, 3 * D), D ** -0.5, 0.1875, ((0, 4), (1, 2))),
        "joint_bias": centred(keys[6], (2 * D,), 0.5, 6.0, ((0, 2),), jnp.float32),
        "output_weight": centred(keys[7], (D, D), (max(1, D * 4 // LEN)) ** -0.5, 3.0, ((0, 2), (1, 4))),
        "output_bias": centred(keys[8], (D,), 0.3, 4.0, ((0, 2),), jnp.float32),
        "second_gain": jnp.clip(1.0 + 0.18 * jax.random.normal(keys[9], (D,), jnp.float32), 0.1, 1.9),
        "second_shift": centred(keys[10], (D,), 0.3, 4.0, ((0, 2),), jnp.float32),
        "up_weight": centred(keys[11], (D, FF), D ** -0.5, 0.1875, ((0, 4), (1, 2))),
        "up_bias": centred(keys[12], (FF,), 0.5, 6.0, ((0, 2),), jnp.float32),
        "down_weight": centred(keys[13], (FF, D), FF ** -0.5, 0.09375, ((0, 2), (1, 4))),
        "down_bias": centred(keys[14], (D,), 0.3, 4.0, ((0, 2),), jnp.float32),
    }


EPSILON = 1e-05

@jax.custom_vjp
def low(v):
    return lax.optimization_barrier(v.astype(jnp.bfloat16)).astype(jnp.float32)

@jax.custom_vjp
def low_back(v):
    return v

def low_keep(v):
    return (low(v), None)

def low_pass(kept, grad):
    return (grad,)

def back_keep(v):
    return (v, None)

def back_low(kept, grad):
    return (low(grad),)
low.defvjp(low_keep, low_pass)
low_back.defvjp(back_keep, back_low)

def matmul(left, right):
    return jnp.dot(left, right, precision=lax.Precision.HIGHEST)

def gelu_exact(values):
    return values * 0.5 * (1.0 + jax.scipy.special.erf(values * 2.0 ** (-0.5)))

def layer_norm(values, gain_vec, offset):
    average = lax.optimization_barrier(jnp.mean(values, axis=-1, keepdims=True))
    spread = lax.optimization_barrier(jnp.mean(values * values, axis=-1, keepdims=True)) - average * average
    return (values - average) * lax.rsqrt(spread + EPSILON) * gain_vec + offset

def attend(queries, key_rows, value_rows, prefix_end):
    scores = low_back(jnp.einsum('qhd,khd->hqk', queries, key_rows, precision=lax.Precision.HIGHEST) * HDIM ** (-0.5))
    places = jnp.arange(LEN).astype(jnp.int32)
    prefix_end = prefix_end.astype(jnp.int32)
    visible = ((places[None, :] <= places[:, None]) | (places[None, :] < prefix_end))[None]
    maximum = lax.optimization_barrier(jnp.max(jnp.where(visible, scores, -jnp.inf), axis=-1, keepdims=True))
    shifted = jnp.where(visible, scores - maximum, jnp.zeros_like(scores))
    terms = jnp.where(visible, jnp.exp(shifted), jnp.zeros_like(scores))
    weights = low(terms / lax.optimization_barrier(jnp.sum(terms, axis=-1, keepdims=True)))
    return jnp.einsum('hqk,khd->qhd', weights, value_rows, precision=lax.Precision.HIGHEST)

def decoder_layer(params, inputs, prefix_ends):
    first_gain, first_shift, joint_weight, joint_bias, output_weight, output_bias, second_gain, second_shift, up_weight, up_bias, down_weight, down_bias = params
    normed = low(layer_norm(inputs, first_gain, first_shift))
    projected = matmul(normed, joint_weight).reshape(-1, HEADS, 3, HDIM)
    bias_rows = joint_bias.reshape(HEADS, 2, HDIM)
    projected = projected + jnp.stack([bias_rows[:, 0], jnp.zeros_like(bias_rows[:, 0]), bias_rows[:, 1]], axis=1)
    projected = low(low_back(projected)).reshape(-1, LEN, HEADS, 3, HDIM)

    def per_sequence(packed):
        seq_rows, prefix_end = packed
        return jax.checkpoint(attend)(seq_rows[:, :, 0], seq_rows[:, :, 1], seq_rows[:, :, 2], prefix_end)
    attended = lax.map(per_sequence, (projected, prefix_ends)).reshape(-1, D)
    attended = low(low_back(attended))
    residual = inputs + low_back(matmul(attended, output_weight) + output_bias)
    normed_two = low(layer_norm(residual, second_gain, second_shift))
    hidden = low_back(matmul(normed_two, up_weight) + up_bias)
    active = low(gelu_exact(hidden))
    return residual + low_back(matmul(active, down_weight) + down_bias)

def reference(tokens_in, cotangent, prefix_length, first_gain, first_shift, joint_weight, joint_bias, output_weight, output_bias, second_gain, second_shift, up_weight, up_bias, down_weight, down_bias):
    params = tuple((member.astype(jnp.float32) for member in (first_gain, first_shift, joint_weight, joint_bias, output_weight, output_bias, second_gain, second_shift, up_weight, up_bias, down_weight, down_bias)))
    group_size = math.gcd(int(SEQS), max(1, 4096 // int(LEN)))
    step_count = SEQS // group_size
    inputs = tokens_in.astype(jnp.float32).reshape(step_count, group_size * LEN, D)
    cotangents = cotangent.astype(jnp.float32).reshape(step_count, group_size * LEN, D)
    prefixes = prefix_length.astype(jnp.int32).reshape(step_count, group_size)

    def accumulate(totals, packed):
        block_in, block_cot, block_prefix = packed

        def forward(weights, values):
            return decoder_layer(weights, values, block_prefix)
        outputs, pullback = jax.vjp(forward, params, block_in)
        weight_grads, input_grads = pullback(block_cot)
        totals = jax.tree.map(jnp.add, totals, weight_grads)
        return (totals, (outputs.astype(jnp.bfloat16), input_grads.astype(jnp.bfloat16)))
    zeroes = jax.tree.map(lambda member: jnp.zeros(member.shape, jnp.float32), params)
    totals, (outputs, input_grads) = lax.scan(accumulate, zeroes, (inputs, cotangents, prefixes))
    return (outputs.reshape(TOKENS, D), input_grads.reshape(TOKENS, D), totals[0], totals[1], totals[2], totals[3], totals[4], totals[5], totals[6], totals[7], totals[8], totals[9], totals[10], totals[11])
```

```python
import math

import jax
import jax.numpy as jnp
from jax import lax
from jax.experimental import pallas as pl
from jax.experimental.pallas import tpu as pltpu
from jax.sharding import PartitionSpec as P

D = 1024
HALF = 512
HDIM = 128
LEN = 1024
MAX_PREFIX = 512
EPSILON = 1e-05
NEGATIVE = -1e30
LOG2E = math.log2(math.e)
SCALE = HDIM**-0.5
TILE = 256

BF = jnp.bfloat16
F32 = jnp.float32
NT = (((1,), (1,)), ((), ()))
TN = (((0,), (0,)), ((), ()))


def vmem():
    return pl.BlockSpec(memory_space=pltpu.VMEM)


def smem():
    return pl.BlockSpec(memory_space=pltpu.SMEM)


def anywhere():
    return pl.BlockSpec(memory_space=pl.ANY)


def params(mib=60):
    return pltpu.CompilerParams(vmem_limit_bytes=mib << 20)


def shape(dims, kind=BF):
    return jax.ShapeDtypeStruct(tuple(dims), kind)


def dot(left, right, dims=(((1,), (0,)), ((), ()))):
    return lax.dot_general(left, right, dims, preferred_element_type=F32)


class Layout:
    def __init__(self, mesh):
        self.R = mesh.shape["row"]
        self.Q = mesh.shape["dp"]
        self.block = D // self.R
        s = self.Q
        while self.block // s < 16:
            s //= 2
        self.s = s
        self.piece = self.block // s
        bits = self.Q.bit_length() - 1
        low = [1 << b for b in range(bits // 2)]
        high = [1 << b for b in range(bits // 2, bits)]
        mixed = []
        while low or high:
            if low:
                mixed.append(low.pop(0))
            if high:
                mixed.append(high.pop(0))
        k = s.bit_length() - 1
        self.split_bits = mixed[:k]
        self.rest_bits = mixed[k:]
        self.order_a = list(range(k))
        self.order_b = [1, 0] + list(range(2, k)) if k >= 2 else list(range(k))
        self.row_bits = [1 << b for b in range(self.R.bit_length() - 1)]


def swap(value, axis, size, bit):
    return lax.ppermute(value, axis, [(i, i ^ bit) for i in range(size)])


def swap_cores(value):
    return lax.ppermute(value, "col", [(0, 1), (1, 0)])


def device_ids(lay):
    z = lax.axis_index("row")
    d = lax.axis_index("dp")
    c = lax.axis_index("col")
    q = sum(((d // bit) % 2) << i for i, bit in enumerate(lay.split_bits))
    return jnp.stack([z ^ (c * (lay.R // 2)), q, c]).astype(jnp.int32)


def gather_row(lay, quarter):
    held = quarter[None]
    offsets = [0]
    for bit in reversed(lay.row_bits):
        got = swap(held, "row", lay.R, bit)
        held = jnp.concatenate([held, got], axis=0)
        offsets = offsets + [o ^ bit for o in offsets]
    return held[1:], offsets[1:]


def gather_dp(lay, part, order):
    held = part[None]
    offsets = [0]
    got, got_offsets = None, []
    for i in order:
        if got is not None:
            held = jnp.concatenate([held, got], axis=0)
            offsets = offsets + got_offsets
        got = swap(held, "dp", lay.Q, lay.split_bits[i])
        got_offsets = [o ^ (1 << i) for o in offsets]
    return (held, got), (offsets, got_offsets)


def gather_weight(lay, quarter, axis):
    others, z_offsets = gather_row(lay, quarter)
    middle = others.shape[axis] // 2
    left = lax.slice_in_dim(others, 0, middle, axis=axis)
    right = lax.slice_in_dim(others, middle, 2 * middle, axis=axis)
    (a0, a1), (qa0, qa1) = gather_dp(lay, left, lay.order_a)
    (b0, b1), (qb0, qb1) = gather_dp(lay, right, lay.order_b)
    return (a0, a1, b0, b1), (qa0, qa1, qb0, qb1), z_offsets


def piece_copies(lay, ids, refs, offsets, z_offsets, place):
    pairs = []
    for which, (ref, q_offsets) in enumerate(zip(refs, offsets)):
        for i, qo in enumerate(q_offsets):
            for k, zo in enumerate(z_offsets):
                q = ids[1] ^ qo
                z = ids[0] ^ zo
                pairs.extend(place(ref.at[i, k], which // 2, q, z))
    return pairs


def start_copies(pairs, sems):
    copies = [pltpu.make_async_copy(a, b, sems.at[i]) for i, (a, b) in enumerate(pairs)]
    for copy in copies:
        copy.start()
    return copies


def wait_copies(copies):
    for copy in copies:
        copy.wait()


def aligned(value, multiple):
    return pl.multiple_of(value * multiple, multiple)


def split_store(lay, ids, block, z, refs, first_a, first_b):
    keep_a, send_a, keep_b, send_b = refs
    half = block.shape[1] // 2
    for q in range(lay.s):
        rows = block[q * lay.piece : (q + 1) * lay.piece].astype(BF)
        for keep, send, bit, part in (
            (keep_a, send_a, first_a, rows[:, :half]),
            (keep_b, send_b, first_b, rows[:, half:]),
        ):
            mine = ((ids[1] >> bit) & 1) == ((q >> bit) & 1)
            spot = z * (lay.s // 2) + ((q >> (bit + 1)) << bit) + (q & ((1 << bit) - 1))

            def to_keep(keep=keep, spot=spot, part=part):
                keep[spot] = part

            def to_send(send=send, spot=spot, part=part):
                send[spot] = part

            pl.when(mine)(to_keep)
            pl.when(jnp.logical_not(mine))(to_send)


def grad_shapes(lay, columns):
    return [shape((lay.R * lay.s // 2, lay.piece, columns // 2))] * 4


def add_split(ids_bits, groups):
    flat = [a for group in groups for pair in group for a in pair]
    outs = []
    for group in groups:
        g, _, m, _ = group[0][0].shape
        columns = sum(pair[0].shape[3] for pair in group)
        outs += [shape((g, m, columns))] * 2

    def kernel(bits, *refs):
        ins, results = refs[: len(flat)], refs[len(flat) :]
        at = 0
        for n, group in enumerate(groups):
            mine = bits[n]
            keep, send = results[2 * n], results[2 * n + 1]
            column = 0
            for _ in group:
                a, b = ins[at], ins[at + 1]
                at += 2
                width = a.shape[3]
                for g in range(a.shape[0]):
                    for target, bit in ((send, 1 - mine), (keep, mine)):
                        total = a[g, bit].astype(F32) + b[g, bit].astype(F32)
                        target[g, :, column : column + width] = total.astype(BF)
                column += width

    return pl.pallas_call(
        kernel,
        in_specs=[smem()] + [vmem()] * len(flat),
        out_specs=[vmem()] * len(outs),
        out_shape=outs,
        compiler_params=params(32),
        name="add_split",
    )(ids_bits, *flat)


def reduce_group(lay, ids, parts):
    keep_a, send_a, keep_b, send_b = parts
    k = len(lay.split_bits)
    left_a = sorted(set(range(k)) - {lay.order_a[0]}, reverse=True)
    left_b = sorted(set(range(k)) - {lay.order_b[0]}, reverse=True)
    half = keep_a.shape[2]
    for step in range(1, k + 1):
        got_a = swap(send_a, "dp", lay.Q, lay.split_bits[lay.order_a[step - 1]])
        got_b = swap(send_b, "dp", lay.Q, lay.split_bits[lay.order_b[step - 1]])
        if step == k:
            break

        def view(value, left, bit):
            before = lay.R * 2 ** left.index(bit)
            after = 2 ** (len(left) - 1 - left.index(bit))
            return value.reshape(before, 2, after * lay.piece, half)

        bit_a, bit_b = lay.order_a[step], lay.order_b[step]
        keep_a, send_a, keep_b, send_b = add_split(
            jnp.stack([(ids[1] >> bit_a) & 1, (ids[1] >> bit_b) & 1]),
            [
                [(view(keep_a, left_a, bit_a), view(got_a, left_a, bit_a))],
                [(view(keep_b, left_b, bit_b), view(got_b, left_b, bit_b))],
            ],
        )
        left_a = [b for b in left_a if b != bit_a]
        left_b = [b for b in left_b if b != bit_b]
    pairs = [(keep_a, got_a), (keep_b, got_b)]
    rows = lay.R
    for i, bit in enumerate(lay.row_bits):
        keep, send = add_split(
            ((ids[0] >> i) & 1)[None],
            [[tuple(v.reshape(rows // 2, 2, lay.piece, v.shape[-1]) for v in pair) for pair in pairs]],
        )
        pairs = [(keep, swap(send, "row", lay.R, bit))]
        rows //= 2
    total = pairs[0][0].astype(F32) + pairs[0][1].astype(F32)
    total = total.reshape(lay.piece, -1)
    for bit in lay.rest_bits:
        total = total + swap(total.astype(BF), "dp", lay.Q, bit).astype(F32)
    return total.astype(BF)


def spread_group(lay, total):
    held, offsets = total[None], [0]
    for i in lay.order_a:
        got = swap(held, "dp", lay.Q, lay.split_bits[i])
        held = jnp.concatenate([held, got], axis=0)
        offsets = offsets + [o ^ (1 << i) for o in offsets]
    return held, offsets


def finish_group(lay, ids, held, offsets, plan):
    outs = [shape((n, lay.block) if t else (lay.block, n), F32) for _, n, t in plan]
    columns = held.shape[2]

    def kernel(ids, held_ref, *refs):
        results, scratch = refs[:-1], refs[-1]
        for i, offset in enumerate(offsets):
            at = aligned(ids[1] ^ offset, lay.piece)
            scratch[pl.ds(at, lay.piece), :] = held_ref[i].astype(F32)
        for result, (first, n, transposed) in zip(results, plan):
            value = scratch[:, first : first + n]
            result[...] = value.T if transposed else value

    return pl.pallas_call(
        kernel,
        in_specs=[smem(), vmem()],
        out_specs=[vmem()] * len(outs),
        out_shape=outs,
        scratch_shapes=[pltpu.VMEM((lay.block, columns), F32)],
        compiler_params=params(32),
        name="finish_group",
    )(ids, held)


def both(own, other):
    return jnp.concatenate([own, other], axis=1)


def row_stats(values):
    average = jnp.mean(values, axis=1, keepdims=True)
    square = jnp.mean(values * values, axis=1, keepdims=True)
    return average, lax.rsqrt(square - average * average + EPSILON)


def norm_grad(gradient, centered, factor, gain):
    scaled = gradient * gain
    first = jnp.mean(scaled, axis=1, keepdims=True)
    second = jnp.mean(scaled * centered, axis=1, keepdims=True)
    return factor * (scaled - first - centered * second)


def tiles():
    return [slice(i, i + TILE) for i in range(0, LEN, TILE)]


V_GAIN1, V_SHIFT1, V_GAIN2, V_SHIFT2, V_OBIAS = range(5)


def pair_row(own_ref, other_ref, i):
    return both(own_ref[i : i + 1, :], other_ref[i : i + 1, :])


def first_norm_project(lay, ids, x_own, x_other, vec_own, vec_other, bias, joint_block, output_block, gathered):
    refs_j, q_offsets, z_offsets = gathered
    width = joint_block.shape[1]
    o_rows = output_block.shape[0]
    block, piece = lay.block, lay.piece
    half = refs_j[0].shape[3]

    def place(source, which, q, z):
        row = aligned(z * lay.s + q, piece)
        if which == 0:
            return [(source, ("j", row, 0, half))]
        out = [(source.at[:, : width - half], ("j", row, half, width - half))]
        per = o_rows // lay.s
        for b in range(per // piece):
            first = width - half + b * block
            out.append((source.at[:, first : first + block], ("o", q * per + b * piece, z * block, block)))
        return out

    def kernel(ids, xo, xt, vo, vt, bias, jb, ob, a0, a1, b0, b1, full, qkv, j_full, o_full, sems):
        def target(t):
            kind, row, col, n = t
            if kind == "j":
                return j_full.at[pl.ds(row, piece), col : col + n]
            return o_full.at[pl.ds(pl.multiple_of(row, piece), piece), pl.ds(pl.multiple_of(col, block), n)]

        pairs = [(a, target(t)) for a, t in piece_copies(lay, ids, (a0, a1, b0, b1), q_offsets, z_offsets, place)]
        pairs.append((jb, j_full.at[pl.ds(aligned(ids[0], block), block), :]))
        pairs.append((ob, o_full.at[:, pl.ds(aligned(ids[0], block), block)]))
        copies = start_copies(pairs, sems)
        gain = pair_row(vo, vt, V_GAIN1)
        shift = pair_row(vo, vt, V_SHIFT1)
        for t in tiles():
            x = both(xo[t, :], xt[t, :]).astype(F32)
            average, factor = row_stats(x)
            full[t, :] = ((x - average) * factor * gain + shift).astype(BF)
        wait_copies(copies)
        for t in tiles():
            qkv[t, :] = (dot(full[t, :], j_full[...]) + bias[...]).astype(BF)

    pieces_n = lay.s * (lay.R - 1)
    n_copies = 2 * pieces_n + pieces_n * (o_rows // lay.s // piece) + 2
    return pl.pallas_call(
        kernel,
        in_specs=[smem()] + [vmem()] * 5 + [anywhere()] * 6,
        out_specs=[vmem()] * 4,
        out_shape=[shape((LEN, D)), shape((LEN, width)), shape((D, width)), shape((o_rows, D))],
        scratch_shapes=[pltpu.SemaphoreType.DMA((n_copies,))],
        compiler_params=params(),
        name="first_norm_project",
    )(ids, x_own, x_other, vec_own, vec_other, bias, joint_block, output_block, *refs_j)


def visible_mask(lo, rows, queries, prefix):
    key_id = lax.broadcasted_iota(jnp.int32, (rows, queries), 0) + lo
    query_id = lax.broadcasted_iota(jnp.int32, (rows, queries), 1) + lo
    return (key_id <= query_id) | (key_id < prefix)


def attention_forward(prefix, qkv, heads):
    bq, per = 512, 2

    def kernel(prefix_ref, qkv_ref, out_ref, log_ref):
        prefix_end = prefix_ref[0]
        for h in range(per):
            base = h * 3 * HDIM
            keys = qkv_ref[:, base + HDIM : base + 2 * HDIM]
            values_t = qkv_ref[:, base + 2 * HDIM : base + 3 * HDIM].T
            for lo in range(0, LEN, bq):
                n = max(MAX_PREFIX, lo + bq)
                query = qkv_ref[lo : lo + bq, base : base + HDIM]
                scores = dot(keys[:n], query, NT)
                tail = jnp.where(visible_mask(lo, n - lo, bq, prefix_end), scores[lo:], NEGATIVE)
                scores = tail if lo == 0 else jnp.concatenate([scores[:lo], tail], axis=0)
                top = jnp.max(scores, axis=0, keepdims=True) * (SCALE * LOG2E)
                weights = jnp.exp2(scores * (SCALE * LOG2E) - top)
                total = jnp.sum(weights, axis=0, keepdims=True)
                mixed = dot(values_t[:, :n], weights.astype(BF)) * (1.0 / total)
                out_ref[lo : lo + bq, h * HDIM : (h + 1) * HDIM] = mixed.T.astype(BF)
                log_ref[h, :, lo : lo + bq] = top + jnp.log2(total)

    return pl.pallas_call(
        kernel,
        grid=(heads // per,),
        in_specs=[smem(), pl.BlockSpec((LEN, 3 * HDIM * per), lambda h: (0, h))],
        out_specs=[
            pl.BlockSpec((LEN, HDIM * per), lambda h: (0, h)),
            pl.BlockSpec((per, 1, LEN), lambda h: (h, 0, 0)),
        ],
        out_shape=[shape((LEN, HDIM * heads)), shape((heads, 1, LEN), F32)],
        compiler_params=params(),
        name="attention_forward",
    )(prefix, qkv)


def output_project(attended, o_full):
    def kernel(a_ref, o_ref, out_ref):
        for t in tiles():
            out_ref[t, :] = dot(a_ref[t, :], o_ref[...]).astype(BF)

    return pl.pallas_call(
        kernel,
        in_specs=[vmem()] * 2,
        out_specs=vmem(),
        out_shape=shape((LEN, D)),
        compiler_params=params(),
        name="output_project",
    )(attended, o_full)


def second_norm_up(lay, ids, x_own, x_other, part_own, part_other, vec_own, vec_other, bias, up_block, gathered):
    refs_u, q_offsets, z_offsets = gathered
    width = up_block.shape[1]
    piece, block = lay.piece, lay.block
    half = refs_u[0].shape[3]

    def place(source, which, q, z):
        return [(source, (aligned(z * lay.s + q, piece), which * half))]

    def kernel(ids, xo, xt, po, pt, vo, vt, bias, ub, a0, a1, b0, b1, residual, centered, factor_ref, full, active, slope, u_full, sems):
        pairs = [
            (a, u_full.at[pl.ds(row, piece), col : col + half])
            for a, (row, col) in piece_copies(lay, ids, (a0, a1, b0, b1), q_offsets, z_offsets, place)
        ]
        pairs.append((ub, u_full.at[pl.ds(aligned(ids[0], block), block), :]))
        copies = start_copies(pairs, sems)
        gain = pair_row(vo, vt, V_GAIN2)
        shift = pair_row(vo, vt, V_SHIFT2)
        out_bias = pair_row(vo, vt, V_OBIAS)
        for t in tiles():
            x = both(xo[t, :], xt[t, :]).astype(F32)
            branch = po[t, :].astype(F32) + both(pt[t, HALF:], pt[t, :HALF]).astype(F32)
            res = x + (branch + out_bias)
            residual[t, :] = res[:, :HALF]
            average, factor = row_stats(res)
            cent = (res - average) * factor
            centered[t, :] = cent.astype(BF)
            factor_ref[t, :] = factor
            full[t, :] = (cent * gain + shift).astype(BF)
        wait_copies(copies)
        for t in tiles():
            hidden = dot(full[t, :], u_full[...]) + bias[...]
            bell = jnp.exp(-0.5 * hidden * hidden) * (1.0 / math.sqrt(2.0 * math.pi))
            phi = 0.5 * (1.0 + lax.erf(hidden * 2.0**-0.5))
            active[t, :] = (hidden * phi).astype(BF)
            slope[t, :] = (phi + hidden * bell).astype(BF)

    n_copies = 2 * lay.s * (lay.R - 1) + 1
    return pl.pallas_call(
        kernel,
        in_specs=[smem()] + [vmem()] * 7 + [anywhere()] * 5,
        out_specs=[vmem()] * 7,
        out_shape=[
            shape((LEN, HALF), F32),
            shape((LEN, D)),
            shape((LEN, 1), F32),
            shape((LEN, D)),
            shape((LEN, width)),
            shape((LEN, width)),
            shape((D, width)),
        ],
        scratch_shapes=[pltpu.SemaphoreType.DMA((n_copies,))],
        compiler_params=params(),
        name="second_norm_up",
    )(ids, x_own, x_other, part_own, part_other, vec_own, vec_other, bias, up_block, *refs_u)


def weight_grad(lay, ids, sides, name):
    columns = sum(right.shape[1] for _, right in sides)
    flat = [ids]
    for left, right in sides:
        flat += list(left) + [right]
    lefts = [len(left) for left, _ in sides]
    first_a, first_b = lay.order_a[0], lay.order_b[0]

    def kernel(ids, *refs):
        ins, outs = refs[: len(flat) - 1], refs[len(flat) - 1 :]
        for z in range(lay.R):
            parts, at = [], 0
            for n in lefts:
                feature = z * lay.block
                ref = ins[at + (feature * n) // D]
                column = feature % (D // n)
                parts.append(dot(ref[:, column : column + lay.block], ins[at + n][...], TN))
                at += n + 1
            block = parts[0] if len(parts) == 1 else jnp.concatenate(parts, axis=1)
            split_store(lay, ids, block, z, outs, first_a, first_b)

    return pl.pallas_call(
        kernel,
        in_specs=[smem()] + [vmem()] * (len(flat) - 1),
        out_specs=[vmem()] * 4,
        out_shape=grad_shapes(lay, columns),
        compiler_params=params(),
        name=name,
    )(*flat)


def hidden_backward(lay, ids, cot_own, cot_other, slope, u_full, down_block, gathered):
    refs_d, q_offsets, z_offsets = gathered
    width = down_block.shape[0]
    block = lay.block
    rows = width // lay.s
    half = rows // 2

    def place(source, which, q, z):
        return [(source, (q * rows + which * half, z * block))]

    def kernel(ids, co, ct, slope_ref, u_full, db, a0, a1, b0, b1, hidden_grad, partial, bias_grad, d_full, sems):
        pairs = [
            (a, d_full.at[pl.ds(pl.multiple_of(row, half), half), pl.ds(pl.multiple_of(col, block), block)])
            for a, (row, col) in piece_copies(lay, ids, (a0, a1, b0, b1), q_offsets, z_offsets, place)
        ]
        pairs.append((db, d_full.at[:, pl.ds(aligned(ids[0], block), block)]))
        wait_copies(start_copies(pairs, sems))
        sums = jnp.zeros((1, width), F32)
        for t in tiles():
            grad = dot(both(co[t, :], ct[t, :]), d_full[...], NT) * slope_ref[t, :].astype(F32)
            low = grad.astype(BF)
            hidden_grad[t, :] = low
            sums = sums + jnp.sum(low.astype(F32), axis=0, keepdims=True)
            partial[t, :] = dot(low, u_full[...], NT).astype(BF)
        bias_grad[...] = sums

    n_copies = 2 * lay.s * (lay.R - 1) + 1
    return pl.pallas_call(
        kernel,
        in_specs=[smem()] + [vmem()] * 4 + [anywhere()] * 5,
        out_specs=[vmem()] * 4,
        out_shape=[shape((LEN, width)), shape((LEN, D)), shape((1, width), F32), shape((width, D))],
        scratch_shapes=[pltpu.SemaphoreType.DMA((n_copies,))],
        compiler_params=params(),
        name="hidden_backward",
    )(ids, cot_own, cot_other, slope, u_full, down_block, *refs_d)


def second_norm_backward(cot_own, cot_other, part_own, part_other, centered, factor, vec_own, vec_other, o_full):
    heads_width = o_full.shape[0]

    def kernel(co, ct, po, pt, cent_ref, factor_ref, vo, vt, o_ref, branch, res_grad, att_grad, sums_ref):
        gain = pair_row(vo, vt, V_GAIN2)
        sums = [jnp.zeros((1, HALF), F32)] * 4
        for t in tiles():
            grad = po[t, :].astype(F32) + both(pt[t, HALF:], pt[t, :HALF]).astype(F32)
            cent = cent_ref[t, :].astype(F32)
            cot = both(co[t, :], ct[t, :]).astype(F32)
            total = cot + norm_grad(grad, cent, factor_ref[t, :], gain)
            low = total.astype(BF)
            branch[t, :] = low
            res_grad[t, :] = total[:, :HALF]
            att_grad[t, :] = dot(low, o_ref[...], NT).astype(BF)
            news = (grad[:, :HALF] * cent[:, :HALF], grad[:, :HALF], low[:, :HALF].astype(F32), cot[:, :HALF])
            sums = [s + jnp.sum(v, axis=0, keepdims=True) for s, v in zip(sums, news)]
        for i in range(4):
            sums_ref[i : i + 1, :] = sums[i]

    return pl.pallas_call(
        kernel,
        in_specs=[vmem()] * 9,
        out_specs=[vmem()] * 4,
        out_shape=[shape((LEN, D)), shape((LEN, HALF), F32), shape((LEN, heads_width)), shape((4, HALF), F32)],
        compiler_params=params(),
        name="second_norm_backward",
    )(cot_own, cot_other, part_own, part_other, centered, factor, vec_own, vec_other, o_full)


def attention_backward(prefix, qkv, grads, logs, attended, heads):
    bq, per = 256, 1

    def kernel(prefix_ref, qkv_ref, grad_ref, log_ref, att_ref, out_ref, sums_ref, key_sum, value_sum):
        prefix_end = prefix_ref[0]
        keys = qkv_ref[:, HDIM : 2 * HDIM]
        values = qkv_ref[:, 2 * HDIM : 3 * HDIM]
        keys_t = keys.T
        query_total = jnp.zeros((1, HDIM), F32)
        for lo in reversed(range(0, LEN, bq)):
            n = max(MAX_PREFIX, lo + bq)
            query = qkv_ref[lo : lo + bq, 0:HDIM]
            grad = grad_ref[lo : lo + bq, :]
            scores = dot(keys[:n], query, NT) * (SCALE * LOG2E)
            weights = jnp.exp2(scores - log_ref[0, :, lo : lo + bq])
            tail = jnp.where(visible_mask(lo, n - lo, bq, prefix_end), weights[lo:], 0.0)
            weights = tail if lo == 0 else jnp.concatenate([weights[:lo], tail], axis=0)
            weight_grad_t = dot(values[:n], grad, NT)
            mixed = grad.astype(F32) * att_ref[lo : lo + bq, :].astype(F32)
            delta = jnp.sum(mixed.T, axis=0, keepdims=True)
            score_grad = (weights * (weight_grad_t - delta)).astype(BF)
            value_part = dot(weights.astype(BF), grad)
            key_part = dot(score_grad, query)
            if lo + bq == LEN:
                value_sum[...] = value_part
                key_sum[...] = key_part
            else:
                value_sum[:n, :] += value_part
                key_sum[:n, :] += key_part
            query_part = (dot(keys_t[:, :n], score_grad).T * SCALE).astype(BF)
            out_ref[lo : lo + bq, 0:HDIM] = query_part
            query_total = query_total + jnp.sum(query_part.astype(F32), axis=0, keepdims=True)
        out_ref[:, HDIM : 2 * HDIM] = (key_sum[...] * SCALE).astype(BF)
        value_low = value_sum[...].astype(BF)
        out_ref[:, 2 * HDIM : 3 * HDIM] = value_low
        sums_ref[0] = both(query_total, jnp.sum(value_low.astype(F32), axis=0, keepdims=True))

    return pl.pallas_call(
        kernel,
        grid=(heads,),
        in_specs=[
            smem(),
            pl.BlockSpec((LEN, 3 * HDIM), lambda h: (0, h)),
            pl.BlockSpec((LEN, HDIM), lambda h: (0, h)),
            pl.BlockSpec((1, 1, LEN), lambda h: (h, 0, 0)),
            pl.BlockSpec((LEN, HDIM), lambda h: (0, h)),
        ],
        out_specs=[
            pl.BlockSpec((LEN, 3 * HDIM), lambda h: (0, h)),
            pl.BlockSpec((1, 1, 2 * HDIM), lambda h: (h, 0, 0)),
        ],
        out_shape=[shape((LEN, 3 * HDIM * heads)), shape((heads, 1, 2 * HDIM), F32)],
        scratch_shapes=[pltpu.VMEM((LEN, HDIM), F32), pltpu.VMEM((LEN, HDIM), F32)],
        compiler_params=params(),
        name="attention_backward",
    )(prefix, qkv, grads, logs, attended)


def project_backward(grads, weight):
    def kernel(g_ref, w_ref, out_ref):
        for t in tiles():
            out_ref[t, :] = dot(g_ref[t, :], w_ref[...], NT).astype(BF)

    return pl.pallas_call(
        kernel,
        in_specs=[vmem()] * 2,
        out_specs=vmem(),
        out_shape=shape((LEN, D)),
        compiler_params=params(),
        name="project_backward",
    )(grads, weight)


def down_project(active, d_full):
    def kernel(a_ref, d_ref, own, other):
        for t in tiles():
            value = dot(a_ref[t, :], d_ref[...]).astype(BF)
            own[t, :] = value[:, :HALF]
            other[t, :] = value[:, HALF:]

    return pl.pallas_call(
        kernel,
        in_specs=[vmem()] * 2,
        out_specs=[vmem()] * 2,
        out_shape=[shape((LEN, HALF))] * 2,
        compiler_params=params(),
        name="down_project",
    )(active, d_full)


def first_norm_backward(x_own, x_other, part_own, part_other, vec_own, vec_other, res_grad):
    def kernel(xo, xt, po, pt, vo, vt, res_ref, out, sums_ref):
        gain = pair_row(vo, vt, V_GAIN1)
        sums = [jnp.zeros((1, HALF), F32)] * 2
        for t in tiles():
            x = both(xo[t, :], xt[t, :]).astype(F32)
            average, factor = row_stats(x)
            cent = (x - average) * factor
            grad = po[t, :].astype(F32) + both(pt[t, HALF:], pt[t, :HALF]).astype(F32)
            back = norm_grad(grad, cent, factor, gain)
            out[t, :] = (res_ref[t, :] + back[:, :HALF]).astype(BF)
            news = (grad[:, :HALF] * cent[:, :HALF], grad[:, :HALF])
            sums = [s + jnp.sum(v, axis=0, keepdims=True) for s, v in zip(sums, news)]
        for i in range(2):
            sums_ref[i : i + 1, :] = sums[i]

    return pl.pallas_call(
        kernel,
        in_specs=[vmem()] * 7,
        out_specs=[vmem()] * 2,
        out_shape=[shape((LEN, HALF)), shape((2, HALF), F32)],
        compiler_params=params(),
        name="first_norm_backward",
    )(x_own, x_other, part_own, part_other, vec_own, vec_other, res_grad)


def own_piece(lay, ids, block, pieces):
    rows = block.shape[0] // pieces
    return lax.dynamic_slice_in_dim(block, ids[1] * rows, rows, axis=0)


def layer(lay, tokens_in, cotangent, prefix_length, first_gain, first_shift, joint_weight, joint_bias,
          output_weight, output_bias, second_gain, second_shift, up_weight, up_bias, down_weight, down_bias):
    heads = joint_bias.shape[0] // (2 * HDIM)
    ids = device_ids(lay)

    x_own, x_other = tokens_in, swap_cores(tokens_in)
    zero_row = jnp.zeros_like(first_gain)
    vec_own = jnp.stack(
        [first_gain, first_shift, second_gain, second_shift, output_bias, zero_row, zero_row, zero_row]
    )
    vec_other = swap_cores(vec_own)

    output_piece = own_piece(lay, ids, output_weight, lay.s)
    output_piece = jnp.concatenate(
        [output_piece[i : i + lay.piece] for i in range(0, output_piece.shape[0], lay.piece)], axis=1
    )
    joint_out = gather_weight(
        lay, jnp.concatenate([own_piece(lay, ids, joint_weight, lay.s), output_piece], axis=1), 2
    )
    up_parts = gather_weight(lay, own_piece(lay, ids, up_weight, lay.s), 2)
    down_parts = gather_weight(lay, own_piece(lay, ids, down_weight, lay.s), 1)

    bias_rows = joint_bias.reshape(heads, 2, HDIM)
    joint_row = jnp.stack([bias_rows[:, 0], jnp.zeros_like(bias_rows[:, 0]), bias_rows[:, 1]], axis=1)
    full_one, qkv, j_full, o_full = first_norm_project(
        lay, ids, x_own, x_other, vec_own, vec_other, joint_row.reshape(1, -1), joint_weight, output_weight, joint_out
    )
    attended, logs = attention_forward(prefix_length, qkv, heads)
    branch_own = output_project(attended, o_full)
    branch_other = swap_cores(branch_own)
    residual, centered, factor, full_two, active, slope, u_full = second_norm_up(
        lay, ids, x_own, x_other, branch_own, branch_other, vec_own, vec_other,
        up_bias.reshape(1, -1), up_weight, up_parts,
    )
    cot_own, cot_other = cotangent, swap_cores(cotangent)
    down_grads = weight_grad(lay, ids, [((cot_own, cot_other), active)], "down_grad")
    down_total = reduce_group(lay, ids, down_grads)
    hidden_grad, norm_part, up_bias_grad, d_full = hidden_backward(
        lay, ids, cot_own, cot_other, slope, u_full, down_weight, down_parts
    )
    norm_other = swap_cores(norm_part)
    up_grads = weight_grad(lay, ids, [((full_two,), hidden_grad)], "up_grad")
    up_total = reduce_group(lay, ids, up_grads)
    branch_grad, res_grad, att_grad, sums_two = second_norm_backward(
        cot_own, cot_other, norm_part, norm_other, centered, factor, vec_own, vec_other, o_full
    )
    qkv_grad, joint_sums = attention_backward(prefix_length, qkv, att_grad, logs, attended, heads)
    joint_grads = weight_grad(
        lay, ids, [((full_one,), qkv_grad), ((branch_grad,), attended)], "joint_grad"
    )
    joint_total = reduce_group(lay, ids, joint_grads)
    first_part = project_backward(qkv_grad, j_full)
    first_other = swap_cores(first_part)
    tokens_grad, sums_one = first_norm_backward(
        x_own, x_other, first_part, first_other, vec_own, vec_other, res_grad
    )
    down_own, down_send = down_project(active, d_full)
    down_got = swap_cores(down_send)
    layer_out = (
        residual + (down_own.astype(F32) + down_got.astype(F32) + down_bias[None, :])
    ).astype(BF)

    small = jnp.concatenate(
        [sums_one.reshape(-1), sums_two.reshape(-1), joint_sums.reshape(-1), up_bias_grad.reshape(-1)]
    ).reshape(-1, HDIM)
    for bit in lay.split_bits + lay.rest_bits:
        small = small + swap(small, "dp", lay.Q, bit)
    for bit in lay.row_bits:
        small = small + swap(small, "row", lay.R, bit)
    small = small.reshape(-1)

    def take(start, n):
        return lax.slice_in_dim(small, start, start + n, axis=0)

    joint_n = joint_bias.shape[0]
    (grad_down,) = finish_group(lay, ids, *spread_group(lay, down_total), [(0, down_weight.shape[0], True)])
    (grad_up,) = finish_group(lay, ids, *spread_group(lay, up_total), [(0, up_weight.shape[1], False)])
    j_width = joint_weight.shape[1]
    grad_joint, grad_output = finish_group(
        lay, ids, *spread_group(lay, joint_total), [(0, j_width, False), (j_width, output_weight.shape[0], True)]
    )
    return (
        layer_out,
        tokens_grad,
        take(0, HALF),
        take(HALF, HALF),
        grad_joint,
        take(6 * HALF, joint_n),
        grad_output,
        take(4 * HALF, HALF),
        take(2 * HALF, HALF),
        take(3 * HALF, HALF),
        grad_up,
        take(6 * HALF + joint_n, up_bias.shape[0]),
        grad_down,
        take(5 * HALF, HALF),
    )


def solution(mesh):
    lay = Layout(mesh)
    vec, rows, cols, flat = P("col"), P("row", "col"), P("col", "row"), P(("dp", "row"), "col")

    def shards(*args):
        return layer(lay, *args)

    return jax.shard_map(
        shards,
        mesh=mesh,
        in_specs=(flat, flat, P(("dp", "row")), vec, vec, rows, vec, cols, vec, vec, vec, rows, vec, cols, vec),
        out_specs=(flat, flat, vec, vec, rows, vec, cols, vec, vec, vec, rows, vec, cols, vec),
        check_vma=False,
    )
```

```python
import math

import jax
import jax.numpy as jnp
from jax import lax
from jax.experimental import pallas as pl
from jax.experimental.pallas import tpu as pltpu
from jax.sharding import PartitionSpec as P

D = 1024
HALF = 512
HDIM = 128
LEN = 1024
MAX_PREFIX = 512
EPSILON = 1e-05
NEGATIVE = -1e30
LOG2E = math.log2(math.e)
SCALE = HDIM**-0.5
TILE = 256

BF = jnp.bfloat16
F32 = jnp.float32
NT = (((1,), (1,)), ((), ()))
TN = (((0,), (0,)), ((), ()))


def vmem():
    return pl.BlockSpec(memory_space=pltpu.VMEM)


def smem():
    return pl.BlockSpec(memory_space=pltpu.SMEM)


def anywhere():
    return pl.BlockSpec(memory_space=pltpu.HBM)


def params(mib=60):
    return pltpu.CompilerParams(vmem_limit_bytes=mib << 20)


def shape(dims, kind=BF):
    return jax.ShapeDtypeStruct(tuple(dims), kind)


def hbm(dims, kind=BF):
    return pltpu.HBM(tuple(dims), kind)


def dot(left, right, dims=(((1,), (0,)), ((), ()))):
    return lax.dot_general(left, right, dims, preferred_element_type=F32)


class Layout:
    def __init__(self, mesh):
        self.R = mesh.shape["row"]
        self.Q = mesh.shape["dp"]
        self.block = D // self.R
        s = self.Q
        while self.block // s < 16:
            s //= 2
        self.s = s
        self.piece = self.block // s
        bits = self.Q.bit_length() - 1
        low = [1 << b for b in range(bits // 2)]
        high = [1 << b for b in range(bits // 2, bits)]
        mixed = []
        while low or high:
            if low:
                mixed.append(low.pop(0))
            if high:
                mixed.append(high.pop(0))
        k = s.bit_length() - 1
        self.split_bits = mixed[:k]
        self.rest_bits = mixed[k:]
        self.order_a = list(range(k))
        self.order_b = [1, 0] + list(range(2, k)) if k >= 2 else list(range(k))
        self.row_bits = [1 << b for b in range(self.R.bit_length() - 1)]


def swap(value, axis, size, bit):
    return lax.ppermute(value, axis, [(i, i ^ bit) for i in range(size)])


def swap_cores(value):
    return lax.ppermute(value, "col", [(0, 1), (1, 0)])


def device_ids(lay):
    z = lax.axis_index("row")
    d = lax.axis_index("dp")
    c = lax.axis_index("col")
    q = sum(((d // bit) % 2) << i for i, bit in enumerate(lay.split_bits))
    return jnp.stack([z ^ (c * (lay.R // 2)), q, c]).astype(jnp.int32)


COST = {
    "first_norm_project": 9,
    "attention_first": 5,
    "attention_second": 7,
    "second_norm_up": 15,
    "down_grad": 9,
    "hidden_backward": 17,
    "up_grad": 9,
    "second_norm_backward": 9,
    "attention_backward": 6,
    "joint_grad_a": 8,
    "joint_grad_b": 6,
    "project_backward": 8,
    "first_norm_backward": 6,
    "down_project": 9,
    "joint_sum_a": 32,
    "joint_sum_b": 40,
    "up_rows": 40,
}
COST_SCALE = 0.25 * 3.69e6


def call(kernel, name, ins, outs, grid=(), scratch=(), after=(), passing=(), mib=None):
    n_in, n_after, n_out, n_pass = len(ins), len(after), len(outs), len(passing)

    def body(*refs):
        refs = list(refs)
        first_out = n_in + n_after + n_pass
        token = first_out + n_out + n_pass
        kernel(*refs[:n_in], *refs[first_out : first_out + n_out], *refs[token + 1 :])

    results = pl.pallas_call(
        body,
        grid=grid,
        in_specs=[spec for _, spec in ins] + [anywhere()] * (n_after + n_pass),
        out_specs=[spec for _, spec in outs] + [anywhere()] * (n_pass + 1),
        out_shape=[kind for kind, _ in outs]
        + [shape(a.shape, a.dtype) for a in passing]
        + [shape((8, HDIM), F32)],
        scratch_shapes=list(scratch),
        compiler_params=params(mib or (8 if "sum" in name or "rows" in name else 18 if name in COST else 8)),
        input_output_aliases={n_in + n_after + i: n_out + i for i in range(n_pass)},
        cost_estimate=pl.CostEstimate(
            flops=1, bytes_accessed=int(COST_SCALE * COST.get(name, 2)), transcendentals=0
        ),
        name=name,
    )(*[array for array, _ in ins], *after, *passing)
    return results[:-1], results[-1]


def hold(arrays, after, name):
    return call(lambda: None, name, [], [], after=after, passing=arrays, mib=8)


def row_tile(width):
    return pl.BlockSpec((TILE, width), lambda i: (i, 0))


def whole(*dims):
    return pl.BlockSpec(dims, lambda i: (0,) * len(dims))


ROW_GRID = (LEN // TILE,)


def own_pieces(ids, parts, rows):
    return jnp.concatenate(
        [lax.dynamic_slice_in_dim(block, ids[1] * step + first, rows, axis=0) for block, step, first in parts], axis=1
    )


def extract(lay, ids, block, rows, after):
    def kernel(ids, source, out, sem):
        copy = pltpu.make_async_copy(source.at[pl.ds(pl.multiple_of(ids[1] * rows, 16), rows), :], out, sem)
        copy.start()
        copy.wait()

    (out,), token = call(
        kernel,
        "extract",
        [(ids, smem()), (block, anywhere())],
        [(shape((rows, block.shape[1])), vmem())],
        scratch=[pltpu.SemaphoreType.DMA],
        after=after,
    )
    return out, token


def cut(lay, arrays, axis, after, name):
    n, rows, columns = arrays[0].shape
    rows, columns = (rows // 2, columns) if axis == 1 else (rows, columns // 2)
    kind = shape((n, rows, columns))

    def spec(i):
        return pl.BlockSpec((1, rows, columns), lambda k: (k, i, 0) if axis == 1 else (k, 0, i))

    def kernel(a, b, left, right):
        left[...] = a[...]
        right[...] = b[...]

    out = pl.BlockSpec((1, rows, columns), lambda k: (k, 0, 0))
    return call(
        kernel, name, [(arrays[0], spec(0)), (arrays[1], spec(1))], [(kind, out)] * 2, grid=(n,), after=after
    )


def join(arrays, after, name):
    rows = sum(a.shape[0] for a in arrays)

    def kernel(*refs):
        at = 0
        for ref in refs[:-1]:
            refs[-1][at : at + ref.shape[0]] = ref[...]
            at += ref.shape[0]

    (out,), token = call(
        kernel, name, [(a, vmem()) for a in arrays], [(shape((rows, *arrays[0].shape[1:])), vmem())], after=after
    )
    return out, token


class Gathered:
    def __init__(self, lay, piece, axis, name, at_once):
        self.lay, self.axis, self.name = lay, axis, name
        piece = piece[None]
        if at_once:
            self.z_offsets = list(range(1, lay.R))
            self.got = [swap(piece, "row", lay.R, k) for k in self.z_offsets]
            self.bits = []
        else:
            self.bits = list(reversed(lay.row_bits))
            self.held, self.held_offsets = [piece], [0]
            self.got, self.z_offsets = [], []
            self.step()

    def step(self):
        bit = self.bits.pop(0)
        sent = self.held[0]
        self.got.append(swap(sent, "row", self.lay.R, bit))
        self.z_offsets += [o ^ bit for o in self.held_offsets]
        self.held_offsets = self.held_offsets + [o ^ bit for o in self.held_offsets]

    def double(self, after):
        token = after[0]
        while self.bits:
            self.held[0], token = join([self.held[0], self.got[-1]], (token, *after[1:]), self.name + "_double")
            self.step()
        return token

    def spread(self, after):
        lay = self.lay
        self.others, token = join(self.got, after, self.name + "_join")
        self.size = self.others.shape[self.axis]
        self.pieces = [(self.others, 0, 0, self.size)]
        for i in range(min(2, len(lay.split_bits))):
            self.pieces.append((swap(self.others, "dp", lay.Q, lay.split_bits[i]), 1 << i, 0, self.size))
        return token

    def forward(self, after):
        lay, half = self.lay, self.size // 2
        if len(lay.split_bits) < 2:
            return after[0]
        (left, right), token = cut(
            lay, [self.pieces[1][0], self.pieces[2][0]], self.axis, after, self.name
        )
        self.pieces.append((swap(left, "dp", lay.Q, lay.split_bits[1]), 3, 0, half))
        self.pieces.append((swap(right, "dp", lay.Q, lay.split_bits[0]), 3, half, half))
        for i, bit in list(enumerate(lay.split_bits))[2:]:
            self.pieces += [(swap(a, "dp", lay.Q, bit), q | 1 << i, f, n) for a, q, f, n in self.pieces]
        return token

    def sources(self, ids, refs, first=0):
        at = 0
        for _, qo, begin, size in self.pieces:
            if begin + size <= first:
                continue
            for k, zo in enumerate(self.z_offsets):
                yield refs[at].at[k], begin, size, ids[1] ^ qo, ids[0] ^ zo
            at += 1

    def arrays(self, first=0):
        return [a for a, _, begin, size in self.pieces if begin + size > first]


class Weight:
    def __init__(self, gathered, block, dims, pairs, first=0):
        self.block, self.dims, self.pairs = block, dims, pairs
        arrays = gathered.arrays(first)
        self.operands = [(a, anywhere()) for a in arrays] + [(block, anywhere())]
        self.n = len(self.operands)

        class Fake:
            def __getitem__(self, i):
                return self

            @property
            def at(self):
                return self

        fake = Fake()
        copies_n = len(list(pairs([1, 0], [fake] * self.n, fake)))
        self.scratch = [pltpu.VMEM(dims, BF), pltpu.SemaphoreType.DMA((copies_n,))]

    def copies(self, ids, refs, target, sems):
        return [
            pltpu.make_async_copy(a, b, sems.at[i])
            for i, (a, b) in enumerate(self.pairs(ids, refs, target))
        ]


def start_all(copies):
    for copy in copies:
        copy.start()


def wait_all(copies):
    for copy in copies:
        copy.wait()


def aligned(value, multiple):
    return value * multiple if isinstance(value, int) else pl.multiple_of(value * multiple, multiple)


def joint_weight_of(gathered, block):
    lay = gathered.lay
    width = block.shape[1]

    def pairs(ids, refs, target):
        for source, first, size, q, z in gathered.sources(ids, refs):
            n = min(first + size, width) - first
            rows = pl.ds(aligned(z * lay.s + q, lay.piece), lay.piece)
            yield source.at[:, :n], target.at[rows, first : first + n]
        yield refs[-1], target.at[pl.ds(aligned(ids[0], lay.block), lay.block), :]

    return Weight(gathered, block, (D, width), pairs)


def output_weight_of(gathered, block, column):
    lay = gathered.lay
    rows = block.shape[0]
    per = rows // lay.s

    def pairs(ids, refs, target):
        for source, first, _, q, z in gathered.sources(ids, refs, column):
            for b in range(per // lay.piece):
                at = column + b * lay.block - first
                yield (
                    source.at[:, at : at + lay.block],
                    target.at[
                        pl.ds(aligned(q * (per // lay.piece) + b, lay.piece), lay.piece),
                        pl.ds(aligned(z, lay.block), lay.block),
                    ],
                )
        yield refs[-1], target.at[:, pl.ds(aligned(ids[0], lay.block), lay.block)]

    return Weight(gathered, block, (rows, D), pairs, column)


def up_weight_of(gathered, block):
    lay = gathered.lay

    def pairs(ids, refs, target):
        for source, first, size, q, z in gathered.sources(ids, refs):
            rows = pl.ds(aligned(z * lay.s + q, lay.piece), lay.piece)
            yield source, target.at[rows, first : first + size]
        yield refs[-1], target.at[pl.ds(aligned(ids[0], lay.block), lay.block), :]

    return Weight(gathered, block, (D, block.shape[1]), pairs)


def down_weight_of(gathered, block):
    lay = gathered.lay
    rows = block.shape[0]
    per = rows // lay.s

    def pairs(ids, refs, target):
        for source, first, size, q, z in gathered.sources(ids, refs):
            row = aligned(q * (per // size) + first // size, size)
            yield source, target.at[pl.ds(row, size), pl.ds(aligned(z, lay.block), lay.block)]
        yield refs[-1], target.at[:, pl.ds(aligned(ids[0], lay.block), lay.block)]

    return Weight(gathered, block, (rows, D), pairs)


def weight_grad(lay, ids, sides, orders, name, after=()):
    columns = sum(r.shape[1] for _, rights in sides for r in rights)
    width = columns // len(orders)
    ins = [(ids, smem())]
    for left, rights in sides:
        ins.append((left, pl.BlockSpec((LEN, lay.block), lambda z: (0, z))))
        ins.extend((r, whole(*r.shape)) for r in rights)
    counts = [len(rights) for _, rights in sides]
    n_out = 2 * len(orders)
    out = pl.BlockSpec((lay.s // 2, lay.piece, width), lambda z: (z, 0, 0))

    def kernel(ids, *refs):
        ins, outs = refs[:-n_out], refs[-n_out:]
        parts, at = [], 0
        for n in counts:
            left = ins[at][...]
            parts.extend(dot(left, ins[at + 1 + i][...], TN).astype(BF) for i in range(n))
            at += n + 1
        block = parts[0] if len(parts) == 1 else jnp.concatenate(parts, axis=1)
        for q in range(lay.s):
            rows = block[q * lay.piece : (q + 1) * lay.piece]
            for i, order in enumerate(orders):
                keep, send, bit = outs[2 * i], outs[2 * i + 1], order[0]
                part = rows[:, i * width : (i + 1) * width]
                mine = ((ids[1] >> bit) & 1) == ((q >> bit) & 1)
                spot = ((q >> (bit + 1)) << bit) + (q & ((1 << bit) - 1))

                def to_keep(keep=keep, spot=spot, part=part):
                    keep[spot] = part

                def to_send(send=send, spot=spot, part=part):
                    send[spot] = part

                pl.when(mine)(to_keep)
                pl.when(jnp.logical_not(mine))(to_send)

    kind = shape((lay.R * lay.s // 2, lay.piece, width))
    return call(kernel, name, ins, [(kind, out)] * n_out, grid=(lay.R,), after=after)


class Small:
    def __init__(self, lay, arrays):
        self.lay = lay
        self.bits = [("dp", lay.Q, bit) for bit in lay.split_bits + lay.rest_bits]
        self.bits += [("row", lay.R, bit) for bit in lay.row_bits]
        self.value = jnp.concatenate([a.reshape(-1) for a in arrays]).reshape(-1, HDIM)
        self.send()

    def send(self):
        self.got = swap(self.value, *self.bits.pop(0))

    def add(self, after):
        def kernel(a, b, out):
            out[...] = a[...] + b[...]

        ins = [(self.value, vmem()), (self.got, vmem())]
        (self.value,), token = call(kernel, "small_sum", ins, [(shape(self.value.shape, F32), vmem())], after=after)
        return token

    def step(self, after):
        token = self.add(after)
        self.send()
        return token

    def finish(self, after):
        while self.bits:
            after = (self.step(after),)
        return self.add(after)


class Reduction:
    def __init__(self, lay, ids, orders, parts):
        self.lay, self.ids, self.orders, self.step = lay, ids, orders, 0
        k = len(lay.split_bits)
        self.left = [sorted(set(range(k)) - {order[0]}, reverse=True) for order in orders]
        self.send(parts)

    def send(self, parts):
        self.keep, self.got = list(parts[0::2]), []
        for order, part in zip(self.orders, parts[1::2]):
            self.got.append(swap(part, "dp", self.lay.Q, self.lay.split_bits[order[self.step]]))
        self.step += 1

    def advance(self, after, name, passing=()):
        lay, n = self.lay, len(self.orders)
        bits = [order[self.step] for order in self.orders]
        ins, outs = [(self.ids, smem())], []
        for i, bit in enumerate(bits):
            groups = lay.R * 2 ** self.left[i].index(bit)
            rows = 2 ** (len(self.left[i]) - 1 - self.left[i].index(bit)) * lay.piece
            width = self.keep[i].shape[-1]
            for value in (self.keep[i], self.got[i]):
                ins.append(
                    (value.reshape(groups, 2, rows, width), pl.BlockSpec((1, 2, rows, width), lambda g: (g, 0, 0, 0)))
                )
            outs += [(shape((groups, rows, width)), pl.BlockSpec((1, rows, width), lambda g: (g, 0, 0)))] * 2

        def kernel(ids, *refs):
            ins, outs = refs[: 2 * n], refs[2 * n :]
            for i, bit in enumerate(bits):
                mine = (ids[1] >> bit) & 1
                a, b = ins[2 * i], ins[2 * i + 1]
                for target, which in ((outs[2 * i], mine), (outs[2 * i + 1], 1 - mine)):
                    target[0] = (a[0, which].astype(F32) + b[0, which].astype(F32)).astype(BF)

        parts, token = call(kernel, name, ins, outs, grid=(groups,), after=after, passing=passing)
        self.left = [[b for b in left if b != bit] for left, bit in zip(self.left, bits)]
        self.send(parts[: 2 * n])
        return parts[2 * n :], token


def first_rows(reduction, after, name):
    lay, ids, n = reduction.lay, reduction.ids, len(reduction.orders)
    ins = [(ids, smem())]
    width = reduction.keep[0].shape[-1]
    for i in range(n):
        for value in (reduction.keep[i], reduction.got[i]):
            value = value.reshape(lay.R // 2, 2, lay.piece, width)
            ins.append((value, pl.BlockSpec((1, 2, lay.piece, width), lambda g: (g, 0, 0, 0))))
    out = pl.BlockSpec((1, lay.piece, n * width), lambda g: (g, 0, 0))

    def kernel(ids, *refs):
        ins, (keep, send) = refs[:-2], refs[-2:]
        mine = ids[0] & 1
        for target, bit in ((keep, mine), (send, 1 - mine)):
            for i in range(n):
                a, b = ins[2 * i], ins[2 * i + 1]
                target[0, :, i * width : (i + 1) * width] = (a[0, bit].astype(F32) + b[0, bit].astype(F32)).astype(BF)

    kind = shape((lay.R // 2, lay.piece, n * width))
    (keep, send), token = call(kernel, name, ins, [(kind, out)] * 2, grid=(lay.R // 2,), after=after)
    return (keep, swap(send, "row", lay.R, 1)), token


def next_rows(lay, ids, pair, after, name):
    token = after[0]
    for i, bit in list(enumerate(lay.row_bits))[1:]:
        keep, got = pair
        groups = keep.shape[0] // 2
        columns = keep.shape[-1]
        ins = [(ids, smem())]
        for value in pair:
            value = value.reshape(groups, 2, lay.piece, columns)
            ins.append((value, pl.BlockSpec((1, 2, lay.piece, columns), lambda g: (g, 0, 0, 0))))
        out = pl.BlockSpec((1, lay.piece, columns), lambda g: (g, 0, 0))

        def kernel(ids, a, b, keep, send, i=i):
            mine = (ids[0] >> i) & 1
            for target, which in ((keep, mine), (send, 1 - mine)):
                target[0] = (a[0, which].astype(F32) + b[0, which].astype(F32)).astype(BF)

        kind = shape((groups, lay.piece, columns))
        (keep, send), token = call(kernel, name, ins, [(kind, out)] * 2, grid=(groups,), after=(token, *after[1:]))
        pair = (keep, swap(send, "row", lay.R, bit))
    return pair, token


def row_total(lay, pair, after, name, ready=(), passing=()):
    width = pair[0].shape[-1]
    columns = width + sum(r.shape[1] for r in ready)

    def kernel(*refs):
        (*others, a, b), out = refs[:-1], refs[-1]
        column = 0
        for ref in others:
            out[:, column : column + ref.shape[1]] = ref[...]
            column += ref.shape[1]
        out[:, column:] = (a[...].astype(F32) + b[...].astype(F32)).astype(BF)

    (total, *passed), token = call(
        kernel,
        name,
        [(v, vmem()) for v in ready] + [(v.reshape(lay.piece, width), vmem()) for v in pair],
        [(shape((lay.piece, columns)), vmem())],
        after=after,
        passing=passing,
    )
    return (total, *passed), token


def rest_sum(lay, total):
    for bit in lay.rest_bits:
        total = (total.astype(F32) + swap(total, "dp", lay.Q, bit).astype(F32)).astype(BF)
    return total


def spread(lay, total):
    got = [total]
    for offset in range(1, lay.s):
        mask = sum(bit for i, bit in enumerate(lay.split_bits) if (offset >> i) & 1)
        got.append(swap(total, "dp", lay.Q, mask))
    return got


def finish(lay, ids, pieces, plan, name, after=()):
    outs = []
    for spans, transposed in plan:
        n = sum(c for _, c in spans)
        outs.append((shape((n, lay.block) if transposed else (lay.block, n), F32), vmem()))
    widest = max([HDIM] + [sum(c for _, c in spans) for spans, t in plan if t])

    def kernel(ids, *refs):
        ins, results, scratch = refs[: lay.s], refs[lay.s : -1], refs[-1]
        for (spans, transposed), result in zip(plan, results):
            column = 0
            for first, n in spans:
                for offset in range(lay.s):
                    rows = pl.ds(aligned(ids[1] ^ offset, lay.piece), lay.piece)
                    value = ins[offset][:, first : first + n].astype(F32)
                    if transposed:
                        scratch[rows, column : column + n] = value
                    else:
                        result[rows, column : column + n] = value
                column += n
            if transposed:
                result[...] = scratch[:, :column].T

    return call(
        kernel,
        name,
        [(ids, smem())] + [(p, vmem()) for p in pieces],
        outs,
        scratch=[pltpu.VMEM((lay.block, widest), F32)],
        after=after,
        mib=18,
    )


def both(own, other):
    return jnp.concatenate([own, other], axis=1)


def row_stats(values):
    average = jnp.mean(values, axis=1, keepdims=True)
    square = jnp.mean(values * values, axis=1, keepdims=True)
    return average, lax.rsqrt(square - average * average + EPSILON)


def norm_grad(gradient, centered, factor, gain):
    scaled = gradient * gain
    first = jnp.mean(scaled, axis=1, keepdims=True)
    second = jnp.mean(scaled * centered, axis=1, keepdims=True)
    return factor * (scaled - first - centered * second)


V_GAIN1, V_SHIFT1, V_GAIN2, V_SHIFT2, V_OBIAS = range(5)


def pair_row(own_ref, other_ref, i):
    return both(own_ref[i : i + 1, :], other_ref[i : i + 1, :])


def branch_sum(own, other):
    return own[...].astype(F32) + both(other[:, HALF:], other[:, :HALF]).astype(F32)


def pair_up(pairs, after):
    def kernel(*refs):
        n = len(pairs)
        for i in range(n):
            refs[2 * n + i][:, :HALF] = refs[2 * i][...]
            refs[2 * n + i][:, HALF:] = refs[2 * i + 1][...]

    return call(
        kernel,
        "pair_up",
        [(v, row_tile(HALF)) for pair in pairs for v in pair],
        [(shape((LEN, D)), row_tile(D))] * len(pairs),
        grid=ROW_GRID,
        after=after,
    )


def first_norm_project(ids, x, vecs, bias, joint, after):
    width = bias.shape[1]

    def kernel(ids, x_ref, vo, vt, bias, *refs):
        pieces, full, qkv, weight, sems = refs[: joint.n], *refs[joint.n :]
        copies = joint.copies(ids, pieces, weight, sems)
        first = pl.program_id(0) == 0
        pl.when(first)(lambda: start_all(copies))
        values = x_ref[...].astype(F32)
        average, factor = row_stats(values)
        normed = (values - average) * factor * pair_row(vo, vt, V_GAIN1) + pair_row(vo, vt, V_SHIFT1)
        low = normed.astype(BF)
        full[...] = low
        pl.when(first)(lambda: wait_all(copies))
        qkv[...] = (dot(low, weight[...]) + bias[...]).astype(BF)

    return call(
        kernel,
        "first_norm_project",
        [(ids, smem()), (x, row_tile(D)), *[(v, whole(8, HALF)) for v in vecs], (bias, whole(1, width))]
        + joint.operands,
        [(hbm((LEN, D)), row_tile(D)), (shape((LEN, width)), row_tile(width))],
        grid=ROW_GRID,
        scratch=joint.scratch,
        after=after,
    )


def visible_mask(lo, rows, queries, prefix):
    key_id = lax.broadcasted_iota(jnp.int32, (rows, queries), 0) + lo
    query_id = lax.broadcasted_iota(jnp.int32, (rows, queries), 1) + lo
    return (key_id <= query_id) | (key_id < prefix)


def attend(prefix_ref, qkv_ref, out_ref, log_ref):
    bq = 512
    prefix_end = prefix_ref[0]
    for h in range(log_ref.shape[0]):
        base = h * 3 * HDIM
        keys = qkv_ref[:, base + HDIM : base + 2 * HDIM]
        values_t = qkv_ref[:, base + 2 * HDIM : base + 3 * HDIM].T
        for lo in range(0, LEN, bq):
            n = max(MAX_PREFIX, lo + bq)
            query = qkv_ref[lo : lo + bq, base : base + HDIM]
            scores = dot(keys[:n], query, NT)
            tail = jnp.where(visible_mask(lo, n - lo, bq, prefix_end), scores[lo:], NEGATIVE)
            scores = tail if lo == 0 else jnp.concatenate([scores[:lo], tail], axis=0)
            top = jnp.max(scores, axis=0, keepdims=True) * (SCALE * LOG2E)
            weights = jnp.exp2(scores * (SCALE * LOG2E) - top)
            total = jnp.sum(weights, axis=0, keepdims=True)
            mixed = dot(values_t[:, :n], weights.astype(BF)) * (1.0 / total)
            out_ref[lo : lo + bq, h * HDIM : (h + 1) * HDIM] = mixed.T.astype(BF)
            log_ref[h, :, lo : lo + bq] = top + jnp.log2(total)


def attention_first(prefix, qkv, heads, after):
    return call(
        attend,
        "attention_first",
        [(prefix, smem()), (qkv, pl.BlockSpec((LEN, 3 * HDIM * heads), lambda i: (0, 0)))],
        [
            (shape((LEN, HDIM * heads)), whole(LEN, HDIM * heads)),
            (shape((heads, 1, LEN), F32), whole(heads, 1, LEN)),
        ],
        grid=(1,),
        after=after,
    )


def attention_second(ids, prefix, qkv, heads, attended_first, output, after):
    width = HDIM * heads

    def kernel(ids, prefix_ref, qkv_ref, first_ref, *refs):
        pieces, (out_ref, log_ref, branch, weight, sems) = refs[: output.n], refs[output.n :]
        copies = output.copies(ids, pieces, weight, sems)
        start_all(copies)
        attend(prefix_ref, qkv_ref, out_ref, log_ref)
        wait_all(copies)
        for lo in range(0, LEN, TILE):
            rows = slice(lo, lo + TILE)
            branch[rows, :] = dot(both(first_ref[rows, :], out_ref[rows, :]), weight[...]).astype(BF)

    return call(
        kernel,
        "attention_second",
        [(ids, smem()), (prefix, smem()), (qkv, pl.BlockSpec((LEN, 3 * HDIM * heads), lambda i: (0, 1))),
         (attended_first, whole(LEN, width))]
        + output.operands,
        [
            (shape((LEN, width)), whole(LEN, width)),
            (shape((heads, 1, LEN), F32), whole(heads, 1, LEN)),
            (shape((LEN, D)), whole(LEN, D)),
        ],
        grid=(1,),
        scratch=output.scratch,
        after=after,
    )


def second_norm_up(ids, x, parts, vecs, bias, up, after):
    width = bias.shape[1]

    def kernel(ids, x_ref, po, pt, vo, vt, bias, *refs):
        pieces = refs[: up.n]
        residual, centered, factor_ref, full, active, slope, weight, sems = refs[up.n :]
        copies = up.copies(ids, pieces, weight, sems)
        first = pl.program_id(0) == 0
        pl.when(first)(lambda: start_all(copies))
        res = x_ref[...].astype(F32) + (branch_sum(po, pt) + pair_row(vo, vt, V_OBIAS))
        residual[...] = res[:, :HALF]
        average, factor = row_stats(res)
        cent = (res - average) * factor
        centered[...] = cent.astype(BF)
        factor_ref[...] = factor
        low = (cent * pair_row(vo, vt, V_GAIN2) + pair_row(vo, vt, V_SHIFT2)).astype(BF)
        full[...] = low
        pl.when(first)(lambda: wait_all(copies))
        hidden = dot(low, weight[...]) + bias[...]
        bell = jnp.exp(-0.5 * hidden * hidden) * (1.0 / math.sqrt(2.0 * math.pi))
        phi = 0.5 * (1.0 + lax.erf(hidden * 2.0**-0.5))
        active[...] = (hidden * phi).astype(BF)
        slope[...] = (phi + hidden * bell).astype(BF)

    return call(
        kernel,
        "second_norm_up",
        [(ids, smem()), (x, row_tile(D)), *[(p, row_tile(D)) for p in parts], *[(v, whole(8, HALF)) for v in vecs],
         (bias, whole(1, width))]
        + up.operands,
        [
            (hbm((LEN, HALF), F32), row_tile(HALF)),
            (hbm((LEN, D)), row_tile(D)),
            (hbm((LEN, 1), F32), row_tile(1)),
            (hbm((LEN, D)), row_tile(D)),
            (shape((LEN, width)), row_tile(width)),
            (shape((LEN, width)), row_tile(width)),
        ],
        grid=ROW_GRID,
        scratch=up.scratch,
        after=after,
    )


def hidden_backward(ids, cot, slope, up, down, after):
    width = slope.shape[1]

    def kernel(ids, cot_ref, slope_ref, *refs):
        up_pieces, refs = refs[: up.n], refs[up.n :]
        down_pieces, refs = refs[: down.n], refs[down.n :]
        hidden_grad, partial, bias_grad, up_full, up_sems, down_full, down_sems = refs
        down_copies = down.copies(ids, down_pieces, down_full, down_sems)
        up_copies = up.copies(ids, up_pieces, up_full, up_sems)
        first = pl.program_id(0) == 0

        def begin():
            start_all(down_copies)
            start_all(up_copies)
            bias_grad[...] = jnp.zeros_like(bias_grad)
            wait_all(down_copies)

        pl.when(first)(begin)
        grad = dot(cot_ref[...], down_full[...], NT) * slope_ref[...].astype(F32)
        low = grad.astype(BF)
        hidden_grad[...] = low
        bias_grad[...] += jnp.sum(low.astype(F32), axis=0, keepdims=True)
        pl.when(first)(lambda: wait_all(up_copies))
        partial[...] = dot(low, up_full[...], NT).astype(BF)

    return call(
        kernel,
        "hidden_backward",
        [(ids, smem()), (cot, row_tile(D)), (slope, row_tile(width))] + up.operands + down.operands,
        [(hbm((LEN, width)), row_tile(width)), (shape((LEN, D)), row_tile(D)), (shape((1, width), F32), whole(1, width))],
        grid=ROW_GRID,
        scratch=up.scratch + down.scratch,
        after=after,
    )


def second_norm_backward(ids, cot, parts, centered, factor, vecs, output, after):
    width = output.dims[0]

    def kernel(ids, cot_ref, po, pt, cent_ref, factor_ref, vo, vt, *refs):
        pieces, (branch, res_grad, att_grad, sums_ref, weight, sems) = refs[: output.n], refs[output.n :]
        copies = output.copies(ids, pieces, weight, sems)
        first = pl.program_id(0) == 0

        def begin():
            start_all(copies)
            sums_ref[...] = jnp.zeros_like(sums_ref)

        pl.when(first)(begin)
        grad = branch_sum(po, pt)
        cent = cent_ref[...].astype(F32)
        cot = cot_ref[...].astype(F32)
        total = cot + norm_grad(grad, cent, factor_ref[...], pair_row(vo, vt, V_GAIN2))
        low = total.astype(BF)
        branch[...] = low
        res_grad[...] = total[:, :HALF]
        news = (grad[:, :HALF] * cent[:, :HALF], grad[:, :HALF], low[:, :HALF].astype(F32), cot[:, :HALF])
        for i, value in enumerate(news):
            sums_ref[i : i + 1, :] += jnp.sum(value, axis=0, keepdims=True)
        pl.when(first)(lambda: wait_all(copies))
        att_grad[...] = dot(low, weight[...], NT).astype(BF)

    return call(
        kernel,
        "second_norm_backward",
        [(ids, smem()), (cot, row_tile(D)), *[(p, row_tile(D)) for p in parts], (centered, row_tile(D)),
         (factor, row_tile(1)), *[(v, whole(8, HALF)) for v in vecs]]
        + output.operands,
        [
            (shape((LEN, D)), row_tile(D)),
            (shape((LEN, HALF), F32), row_tile(HALF)),
            (shape((LEN, width)), row_tile(width)),
            (shape((4, HALF), F32), whole(4, HALF)),
        ],
        grid=ROW_GRID,
        scratch=output.scratch,
        after=after,
    )


def attention_backward(prefix, qkv, grads, logs, attended, first_head, heads, after):
    bq = 256

    def kernel(prefix_ref, qkv_ref, grad_ref, log_ref, att_ref, out_ref, sums_ref, key_sum, value_sum):
        prefix_end = prefix_ref[0]
        keys = qkv_ref[:, HDIM : 2 * HDIM]
        values = qkv_ref[:, 2 * HDIM : 3 * HDIM]
        keys_t = keys.T
        query_total = jnp.zeros((1, HDIM), F32)
        for lo in reversed(range(0, LEN, bq)):
            n = max(MAX_PREFIX, lo + bq)
            query = qkv_ref[lo : lo + bq, 0:HDIM]
            grad = grad_ref[lo : lo + bq, :]
            scores = dot(keys[:n], query, NT) * (SCALE * LOG2E)
            weights = jnp.exp2(scores - log_ref[0, :, lo : lo + bq])
            tail = jnp.where(visible_mask(lo, n - lo, bq, prefix_end), weights[lo:], 0.0)
            weights = tail if lo == 0 else jnp.concatenate([weights[:lo], tail], axis=0)
            weight_grad_t = dot(values[:n], grad, NT)
            mixed = grad.astype(F32) * att_ref[lo : lo + bq, :].astype(F32)
            delta = jnp.sum(mixed.T, axis=0, keepdims=True)
            score_grad = (weights * (weight_grad_t - delta)).astype(BF)
            value_part = dot(weights.astype(BF), grad)
            key_part = dot(score_grad, query)
            if lo + bq == LEN:
                value_sum[...] = value_part
                key_sum[...] = key_part
            else:
                value_sum[:n, :] += value_part
                key_sum[:n, :] += key_part
            query_part = (dot(keys_t[:, :n], score_grad).T * SCALE).astype(BF)
            out_ref[lo : lo + bq, 0:HDIM] = query_part
            query_total = query_total + jnp.sum(query_part.astype(F32), axis=0, keepdims=True)
        out_ref[:, HDIM : 2 * HDIM] = (key_sum[...] * SCALE).astype(BF)
        value_low = value_sum[...].astype(BF)
        out_ref[:, 2 * HDIM : 3 * HDIM] = value_low
        sums_ref[0] = both(query_total, jnp.sum(value_low.astype(F32), axis=0, keepdims=True))

    return call(
        kernel,
        "attention_backward",
        [
            (prefix, smem()),
            (qkv, pl.BlockSpec((LEN, 3 * HDIM), lambda h: (0, h + first_head))),
            (grads, pl.BlockSpec((LEN, HDIM), lambda h: (0, h + first_head))),
            (logs, pl.BlockSpec((1, 1, LEN), lambda h: (h, 0, 0))),
            (attended, pl.BlockSpec((LEN, HDIM), lambda h: (0, h))),
        ],
        [
            (shape((LEN, 3 * HDIM * heads)), pl.BlockSpec((LEN, 3 * HDIM), lambda h: (0, h))),
            (shape((heads, 1, 2 * HDIM), F32), pl.BlockSpec((1, 1, 2 * HDIM), lambda h: (h, 0, 0))),
        ],
        grid=(heads,),
        scratch=[pltpu.VMEM((LEN, HDIM), F32), pltpu.VMEM((LEN, HDIM), F32)],
        after=after,
    )


def project_backward(ids, grads, x, vecs, joint, after):
    widths = [g.shape[1] for g in grads]

    def kernel(ids, x_ref, vo, vt, *refs):
        grad_refs, refs = refs[: len(grads)], refs[len(grads) :]
        pieces, (own, other, sums, weight, sems) = refs[: joint.n], refs[joint.n :]
        copies = joint.copies(ids, pieces, weight, sems)
        first = pl.program_id(0) == 0
        pl.when(first)(lambda: start_all(copies))
        values = x_ref[...].astype(F32)
        average, factor = row_stats(values)
        pl.when(first)(lambda: wait_all(copies))
        total, column = 0.0, 0
        for ref, width in zip(grad_refs, widths):
            total = total + dot(ref[...], weight[:, column : column + width], NT)
            column += width
        own[...] = total[:, :HALF].astype(BF)
        other[:, :HALF] = total[:, HALF:].astype(BF)
        scaled = total * pair_row(vo, vt, V_GAIN1)
        lane = lax.broadcasted_iota(jnp.int32, (TILE, HDIM), 1)
        packed = jnp.zeros((TILE, HDIM), F32)
        parts = jnp.zeros((TILE, HDIM), F32)
        for i, value in enumerate((scaled, scaled * ((values - average) * factor))):
            row_sum = jnp.sum(value, axis=1, keepdims=True)
            high = row_sum.astype(BF).astype(F32)
            packed = jnp.where(lane == 2 * i, high, jnp.where(lane == 2 * i + 1, row_sum - high, packed))
            parts = jnp.where(lane == i, row_sum, parts)
        other[:, HALF:] = packed.astype(BF)
        sums[...] = parts

    return call(
        kernel,
        "project_backward",
        [(ids, smem()), (x, row_tile(D)), *[(v, whole(8, HALF)) for v in vecs]]
        + [(g, row_tile(g.shape[1])) for g in grads]
        + joint.operands,
        [
            (shape((LEN, HALF)), row_tile(HALF)),
            (shape((LEN, HALF + HDIM)), row_tile(HALF + HDIM)),
            (shape((LEN, HDIM), F32), row_tile(HDIM)),
        ],
        grid=ROW_GRID,
        scratch=joint.scratch,
        after=after,
    )


def down_project(ids, active, down, after):
    def kernel(ids, a_ref, *refs):
        pieces, (own, other, weight, sems) = refs[: down.n], refs[down.n :]
        copies = down.copies(ids, pieces, weight, sems)

        def begin():
            start_all(copies)
            wait_all(copies)

        pl.when(pl.program_id(0) == 0)(begin)
        value = dot(a_ref[...], weight[...]).astype(BF)
        own[...] = value[:, :HALF]
        other[...] = value[:, HALF:]

    return call(
        kernel,
        "down_project",
        [(ids, smem()), (active, row_tile(active.shape[1]))] + down.operands,
        [(shape((LEN, HALF)), row_tile(HALF))] * 2,
        grid=ROW_GRID,
        scratch=down.scratch,
        after=after,
    )


def first_norm_backward(x, own, other, sums, vecs, res_grad, after):
    def kernel(x_ref, po, pt, so, vo, res_ref, out, sums_ref):
        pl.when(pl.program_id(0) == 0)(lambda: sums_ref.__setitem__(..., jnp.zeros_like(sums_ref)))
        values = x_ref[...].astype(F32)
        average, factor = row_stats(values)
        cent = (values[:, :HALF] - average) * factor
        grad = po[...].astype(F32) + pt[:, :HALF].astype(F32)
        got = pt[:, HALF:].astype(F32)
        first = (so[:, 0:1] + (got[:, 0:1] + got[:, 1:2])) * (1.0 / D)
        second = (so[:, 1:2] + (got[:, 2:3] + got[:, 3:4])) * (1.0 / D)
        back = factor * (grad * vo[V_GAIN1 : V_GAIN1 + 1, :] - first - cent * second)
        out[...] = (res_ref[...] + back).astype(BF)
        for i, value in enumerate((grad * cent, grad)):
            sums_ref[i : i + 1, :] += jnp.sum(value, axis=0, keepdims=True)

    return call(
        kernel,
        "first_norm_backward",
        [(x, row_tile(D)), (own, row_tile(HALF)), (other, row_tile(HALF + HDIM)), (sums, row_tile(HDIM)),
         (vecs[0], whole(8, HALF)), (res_grad, row_tile(HALF))],
        [(shape((LEN, HALF)), row_tile(HALF)), (shape((2, HALF), F32), whole(2, HALF))],
        grid=ROW_GRID,
        after=after,
    )


def layer(lay, tokens_in, cotangent, prefix_length, first_gain, first_shift, joint_weight, joint_bias,
          output_weight, output_bias, second_gain, second_shift, up_weight, up_bias, down_weight, down_bias):
    heads = joint_bias.shape[0] // (2 * HDIM)
    ids = device_ids(lay)

    j_width, o_rows, ff = joint_weight.shape[1], output_weight.shape[0], down_weight.shape[0]
    per = o_rows // lay.s
    jo_piece = own_pieces(
        ids, [(joint_weight, lay.piece, 0), *[(output_weight, per, b * lay.piece) for b in range(per // lay.piece)]], lay.piece
    )
    jo = Gathered(lay, jo_piece, 2, "joint_pieces", True)

    zero_row = jnp.zeros_like(first_gain)
    vec_own = jnp.stack(
        [first_gain, first_shift, second_gain, second_shift, output_bias, zero_row, zero_row, zero_row]
    )
    vecs = (vec_own, swap_cores(vec_own))
    bias_rows = joint_bias.reshape(heads, 2, HDIM)
    joint_row = jnp.stack([bias_rows[:, 0], jnp.zeros_like(bias_rows[:, 0]), bias_rows[:, 1]], axis=1).reshape(1, -1)
    (x, cot), token = pair_up(
        [(tokens_in, swap_cores(tokens_in)), (cotangent, swap_cores(cotangent))], (*vecs, joint_row)
    )

    token = jo.spread((token,))
    up_piece, up_token = extract(lay, ids, up_weight, lay.piece, (token,))
    up = Gathered(lay, up_piece, 2, "up_pieces", False)
    token = up.double((up_token,))
    token = jo.forward((token,))
    down_piece, down_token = extract(lay, ids, down_weight, ff // lay.s, (token, *up.got))
    down = Gathered(lay, down_piece, 1, "down_pieces", False)
    token = up.spread((token, *jo.arrays()))
    joint_w = joint_weight_of(jo, joint_weight)
    output_w = output_weight_of(jo, output_weight, j_width)

    (full_one, qkv), token = first_norm_project(
        ids, x, vecs, joint_row, joint_w, (up.others, down_token)
    )
    pair = heads // 2
    token = down.double((token,))
    (attended_a, logs_a), token = attention_first(prefix_length, qkv, pair, (token,))
    token = up.forward((token,))
    up_w = up_weight_of(up, up_weight)
    (attended_b, logs_b, branch), token = attention_second(
        ids, prefix_length, qkv, pair, attended_a, output_w, (token,)
    )
    token = down.spread((token,))
    (branch,), token = hold([branch], (token, *up.arrays()), "hold_branch")
    (residual, centered, factor, full_two, active, slope), token = second_norm_up(
        ids, x, (branch, swap_cores(branch)), vecs, up_bias.reshape(1, -1), up_w, (token,)
    )
    token = down.forward((token,))
    down_w = down_weight_of(down, down_weight)
    both_orders = [lay.order_a, lay.order_b]
    later_steps = range(len(lay.split_bits) - 1)
    down_parts, token = weight_grad(lay, ids, [(cot, [active])], both_orders, "down_grad", (token,))
    down_parts, token = hold(down_parts, (token, *down.arrays()), "hold_down")
    down_red = Reduction(lay, ids, both_orders, down_parts)

    (hidden_grad, norm_part, up_bias_grad), token = hidden_backward(ids, cot, slope, up_w, down_w, (token,))
    passed, token = weight_grad(lay, ids, [(full_two, [hidden_grad])], both_orders, "up_grad", (token,))
    passed = [norm_part, *passed]
    for _ in later_steps:
        passed, token = down_red.advance((token,), "down_sum", passed)
    norm_part, *up_parts = passed
    up_red = Reduction(lay, ids, both_orders, up_parts)
    norm_parts = (norm_part, swap_cores(norm_part))
    (branch_grad, res_grad, att_grad, sums_two), token = second_norm_backward(
        ids, cot, norm_parts, centered, factor, vecs, output_w, (token,)
    )
    (qkv_grad_a, joint_sums_a), token = attention_backward(
        prefix_length, qkv, att_grad, logs_a, attended_a, 0, pair, (token,)
    )
    (qkv_grad_b, joint_sums_b), token = attention_backward(
        prefix_length, qkv, att_grad, logs_b, attended_b, pair, pair, (token,)
    )
    down_rows, token = first_rows(down_red, (token,), "down_rows")
    parts_a, token = weight_grad(
        lay, ids, [(full_one, [qkv_grad_a]), (branch_grad, [attended_a, attended_b])], [lay.order_a],
        "joint_grad_a", (token,),
    )
    red_a = Reduction(lay, ids, [lay.order_a], parts_a)
    parts_b, token = weight_grad(lay, ids, [(full_one, [qkv_grad_b])], [lay.order_b], "joint_grad_b", (token,))
    red_b = Reduction(lay, ids, [lay.order_b], parts_b)
    for _ in later_steps:
        _, token = up_red.advance((token,), "up_sum")
    down_rows, token = next_rows(lay, ids, down_rows, (token,), "down_rows_2")
    (first_own, first_send, row_sums), token = project_backward(
        ids, [qkv_grad_a, qkv_grad_b], x, vecs, joint_w, (token,)
    )
    (down_total, first_send), token = row_total(lay, down_rows, (token,), "down_total", (), [first_send])
    first_got = swap_cores(first_send)
    (down_own, down_send), token = down_project(ids, active, down_w, (token,))
    up_rows, token = first_rows(up_red, (token,), "up_rows")
    for _ in later_steps:
        _, token = red_b.advance((token,), "joint_sum_b")
    for _ in later_steps:
        _, token = red_a.advance((token,), "joint_sum_a")
    (tokens_grad, sums_one), token = first_norm_backward(
        x, first_own, first_got, row_sums, vecs, res_grad, (token,)
    )
    small = Small(lay, (sums_one, sums_two, joint_sums_a, joint_sums_b, up_bias_grad))
    up_rows, token = next_rows(lay, ids, up_rows, (token,), "up_rows_2")
    rows_b, token = first_rows(red_b, (token,), "joint_rows_b")
    (ffn_total,), token = row_total(lay, up_rows, (token,), "up_total", [down_total])
    ffn_pieces = spread(lay, rest_sum(lay, ffn_total))
    token = small.step((token,))
    rows_a, token = first_rows(red_a, (token,), "joint_rows_a")
    token = small.step((token,))
    rows_b, token = next_rows(lay, ids, rows_b, (token,), "joint_rows_b_2")
    rows_a, token = next_rows(lay, ids, rows_a, (token,), "joint_rows_a_2")

    layer_out = (
        residual + (down_own.astype(F32) + swap_cores(down_send).astype(F32) + down_bias[None, :])
    ).astype(BF)
    token = small.step((token,))
    (total_b,), token = row_total(lay, rows_b, (token,), "joint_total_b")
    (joint_total,), token = row_total(lay, rows_a, (token,), "joint_total_a", [total_b])
    joint_pieces = spread(lay, rest_sum(lay, joint_total))
    token = small.finish((token,))
    small = small.value.reshape(-1)
    (grad_down, grad_up), token = finish(
        lay, ids, ffn_pieces, [([(0, ff)], True), ([(ff, ff)], False)], "finish_ffn", (token,)
    )
    mid = j_width // 2
    (grad_joint, grad_output), token = finish(
        lay,
        ids,
        joint_pieces,
        [([(mid, mid), (0, mid)], False), ([(2 * mid, o_rows)], True)],
        "finish_attention",
        (token,),
    )

    def take(start, n):
        return lax.slice_in_dim(small, start, start + n, axis=0)

    joint_n = joint_bias.shape[0]
    return (
        layer_out,
        tokens_grad,
        take(0, HALF),
        take(HALF, HALF),
        grad_joint,
        take(6 * HALF, joint_n),
        grad_output,
        take(4 * HALF, HALF),
        take(2 * HALF, HALF),
        take(3 * HALF, HALF),
        grad_up,
        take(6 * HALF + joint_n, up_bias.shape[0]),
        grad_down,
        take(5 * HALF, HALF),
    )


def solution(mesh):
    lay = Layout(mesh)
    vec, rows, cols, flat = P("col"), P("row", "col"), P("col", "row"), P(("dp", "row"), "col")

    def shards(*args):
        return layer(lay, *args)

    return jax.shard_map(
        shards,
        mesh=mesh,
        in_specs=(flat, flat, P(("dp", "row")), vec, vec, rows, vec, cols, vec, vec, vec, rows, vec, cols, vec),
        out_specs=(flat, flat, vec, vec, rows, vec, cols, vec, vec, vec, rows, vec, cols, vec),
        check_vma=False,
    )
```

```python
import math

import jax
import jax.numpy as jnp
from jax import lax
from jax.experimental import pallas as pl
from jax.experimental.pallas import tpu as pltpu
from jax.sharding import PartitionSpec as P

D = 1024
HALF = 512
HDIM = 128
LEN = 1024
MAX_PREFIX = 512
EPSILON = 1e-05
NEGATIVE = -1e30
LOG2E = math.log2(math.e)
SCALE = HDIM**-0.5
TILE = 256

BF = jnp.bfloat16
F32 = jnp.float32
NT = (((1,), (1,)), ((), ()))
TN = (((0,), (0,)), ((), ()))


def vmem():
    return pl.BlockSpec(memory_space=pltpu.VMEM)


def smem():
    return pl.BlockSpec(memory_space=pltpu.SMEM)


def anywhere():
    return pl.BlockSpec(memory_space=pltpu.HBM)


def params(mib=60):
    return pltpu.CompilerParams(vmem_limit_bytes=mib << 20)


def shape(dims, kind=BF):
    return jax.ShapeDtypeStruct(tuple(dims), kind)


def hbm(dims, kind=BF):
    return pltpu.HBM(tuple(dims), kind)


def dot(left, right, dims=(((1,), (0,)), ((), ()))):
    return lax.dot_general(left, right, dims, preferred_element_type=F32)


class Layout:
    def __init__(self, mesh):
        self.R = mesh.shape["row"]
        self.Q = mesh.shape["dp"]
        self.block = D // self.R
        s = self.Q
        while self.block // s < 16:
            s //= 2
        self.s = s
        self.piece = self.block // s
        bits = self.Q.bit_length() - 1
        low = [1 << b for b in range(bits // 2)]
        high = [1 << b for b in range(bits // 2, bits)]
        mixed = []
        while low or high:
            if low:
                mixed.append(low.pop(0))
            if high:
                mixed.append(high.pop(0))
        k = s.bit_length() - 1
        self.split_bits = mixed[:k]
        self.rest_bits = mixed[k:]
        self.order_a = list(range(k))
        self.order_b = [1, 0] + list(range(2, k)) if k >= 2 else list(range(k))
        self.row_bits = [1 << b for b in range(self.R.bit_length() - 1)]


def swap(value, axis, size, bit):
    return lax.ppermute(value, axis, [(i, i ^ bit) for i in range(size)])


def swap_cores(value):
    return lax.ppermute(value, "col", [(0, 1), (1, 0)])


def device_ids(lay):
    z = lax.axis_index("row")
    d = lax.axis_index("dp")
    c = lax.axis_index("col")
    q = sum(((d // bit) % 2) << i for i, bit in enumerate(lay.split_bits))
    return jnp.stack([z ^ (c * (lay.R // 2)), q, c]).astype(jnp.int32)


COST = {
    "first_norm_project": 9,
    "attention_first": 5,
    "attention_second": 7,
    "second_norm_up": 15,
    "down_grad": 9,
    "hidden_backward": 17,
    "up_grad": 9,
    "second_norm_backward": 9,
    "attention_backward": 6,
    "joint_grad": 10,
    "project_backward": 8,
    "first_norm_backward": 6,
    "down_project": 9,
    "joint_sum": 32,
}
COST_SCALE = 0.25 * 3.69e6


def call(kernel, name, ins, outs, grid=(), scratch=(), after=(), passing=(), mib=None):
    n_in, n_after, n_out, n_pass = len(ins), len(after), len(outs), len(passing)

    def body(*refs):
        refs = list(refs)
        first_out = n_in + n_after + n_pass
        token = first_out + n_out + n_pass
        kernel(*refs[:n_in], *refs[first_out : first_out + n_out], *refs[token + 1 :])

    results = pl.pallas_call(
        body,
        grid=grid,
        in_specs=[spec for _, spec in ins] + [anywhere()] * (n_after + n_pass),
        out_specs=[spec for _, spec in outs] + [anywhere()] * (n_pass + 1),
        out_shape=[kind for kind, _ in outs]
        + [shape(a.shape, a.dtype) for a in passing]
        + [shape((8, HDIM), F32)],
        scratch_shapes=list(scratch),
        compiler_params=params(mib or (8 if "sum" in name or "rows" in name else 18 if name in COST else 8)),
        input_output_aliases={n_in + n_after + i: n_out + i for i in range(n_pass)},
        cost_estimate=pl.CostEstimate(
            flops=1, bytes_accessed=int(COST_SCALE * COST.get(name, 2)), transcendentals=0
        ),
        name=name,
    )(*[array for array, _ in ins], *after, *passing)
    return results[:-1], results[-1]


def hold(arrays, after, name):
    return call(lambda: None, name, [], [], after=after, passing=arrays, mib=8)


def row_tile(width):
    return pl.BlockSpec((TILE, width), lambda i: (i, 0))


def whole(*dims):
    return pl.BlockSpec(dims, lambda i: (0,) * len(dims))


ROW_GRID = (LEN // TILE,)


def own_pieces(ids, parts, rows):
    return jnp.concatenate(
        [lax.dynamic_slice_in_dim(block, ids[1] * step + first, rows, axis=0) for block, step, first in parts], axis=1
    )


def extract(lay, ids, block, rows, after):
    def kernel(ids, source, out, sem):
        copy = pltpu.make_async_copy(source.at[pl.ds(pl.multiple_of(ids[1] * rows, 16), rows), :], out, sem)
        copy.start()
        copy.wait()

    (out,), token = call(
        kernel,
        "extract",
        [(ids, smem()), (block, anywhere())],
        [(shape((rows, block.shape[1])), vmem())],
        scratch=[pltpu.SemaphoreType.DMA],
        after=after,
    )
    return out, token


def cut(lay, arrays, axis, after, name):
    n, rows, columns = arrays[0].shape
    rows, columns = (rows // 2, columns) if axis == 1 else (rows, columns // 2)
    kind = shape((n, rows, columns))

    def spec(i):
        return pl.BlockSpec((1, rows, columns), lambda k: (k, i, 0) if axis == 1 else (k, 0, i))

    def kernel(a, b, left, right):
        left[...] = a[...]
        right[...] = b[...]

    out = pl.BlockSpec((1, rows, columns), lambda k: (k, 0, 0))
    return call(
        kernel, name, [(arrays[0], spec(0)), (arrays[1], spec(1))], [(kind, out)] * 2, grid=(n,), after=after
    )


def join(arrays, after, name):
    rows = sum(a.shape[0] for a in arrays)

    def kernel(*refs):
        at = 0
        for ref in refs[:-1]:
            refs[-1][at : at + ref.shape[0]] = ref[...]
            at += ref.shape[0]

    (out,), token = call(
        kernel, name, [(a, vmem()) for a in arrays], [(shape((rows, *arrays[0].shape[1:])), vmem())], after=after
    )
    return out, token


class Gathered:
    def __init__(self, lay, piece, axis, name, at_once):
        self.lay, self.axis, self.name = lay, axis, name
        piece = piece[None]
        if at_once:
            self.z_offsets = list(range(1, lay.R))
            self.got = [swap(piece, "row", lay.R, k) for k in self.z_offsets]
            self.bits = []
        else:
            self.bits = list(reversed(lay.row_bits))
            self.held, self.held_offsets = [piece], [0]
            self.got, self.z_offsets = [], []
            self.step()

    def step(self):
        bit = self.bits.pop(0)
        sent = self.held[0]
        self.got.append(swap(sent, "row", self.lay.R, bit))
        self.z_offsets += [o ^ bit for o in self.held_offsets]
        self.held_offsets = self.held_offsets + [o ^ bit for o in self.held_offsets]

    def double(self, after):
        token = after[0]
        while self.bits:
            self.held[0], token = join([self.held[0], self.got[-1]], (token, *after[1:]), self.name + "_double")
            self.step()
        return token

    def spread(self, after):
        lay = self.lay
        self.others, token = join(self.got, after, self.name + "_join")
        self.size = self.others.shape[self.axis]
        self.pieces = [(self.others, 0, 0, self.size)]
        for i in range(min(2, len(lay.split_bits))):
            self.pieces.append((swap(self.others, "dp", lay.Q, lay.split_bits[i]), 1 << i, 0, self.size))
        return token

    def forward(self, after):
        lay, half = self.lay, self.size // 2
        if len(lay.split_bits) < 2:
            return after[0]
        (left, right), token = cut(
            lay, [self.pieces[1][0], self.pieces[2][0]], self.axis, after, self.name
        )
        self.pieces.append((swap(left, "dp", lay.Q, lay.split_bits[1]), 3, 0, half))
        self.pieces.append((swap(right, "dp", lay.Q, lay.split_bits[0]), 3, half, half))
        for i, bit in list(enumerate(lay.split_bits))[2:]:
            self.pieces += [(swap(a, "dp", lay.Q, bit), q | 1 << i, f, n) for a, q, f, n in self.pieces]
        return token

    def sources(self, ids, refs, first=0):
        at = 0
        for _, qo, begin, size in self.pieces:
            if begin + size <= first:
                continue
            for k, zo in enumerate(self.z_offsets):
                yield refs[at].at[k], begin, size, ids[1] ^ qo, ids[0] ^ zo
            at += 1

    def arrays(self, first=0):
        return [a for a, _, begin, size in self.pieces if begin + size > first]


class Weight:
    def __init__(self, gathered, block, dims, pairs, first=0):
        self.block, self.dims, self.pairs = block, dims, pairs
        arrays = gathered.arrays(first)
        self.operands = [(a, anywhere()) for a in arrays] + [(block, anywhere())]
        self.n = len(self.operands)

        class Fake:
            def __getitem__(self, i):
                return self

            @property
            def at(self):
                return self

        fake = Fake()
        copies_n = len(list(pairs([1, 0], [fake] * self.n, fake)))
        self.scratch = [pltpu.VMEM(dims, BF), pltpu.SemaphoreType.DMA((copies_n,))]

    def copies(self, ids, refs, target, sems):
        return [
            pltpu.make_async_copy(a, b, sems.at[i])
            for i, (a, b) in enumerate(self.pairs(ids, refs, target))
        ]


def start_all(copies):
    for copy in copies:
        copy.start()


def wait_all(copies):
    for copy in copies:
        copy.wait()


def aligned(value, multiple):
    return value * multiple if isinstance(value, int) else pl.multiple_of(value * multiple, multiple)


def joint_weight_of(gathered, block):
    lay = gathered.lay
    width = block.shape[1]

    def pairs(ids, refs, target):
        for source, first, size, q, z in gathered.sources(ids, refs):
            n = min(first + size, width) - first
            rows = pl.ds(aligned(z * lay.s + q, lay.piece), lay.piece)
            yield source.at[:, :n], target.at[rows, first : first + n]
        yield refs[-1], target.at[pl.ds(aligned(ids[0], lay.block), lay.block), :]

    return Weight(gathered, block, (D, width), pairs)


def output_weight_of(gathered, block, column):
    lay = gathered.lay
    rows = block.shape[0]
    per = rows // lay.s

    def pairs(ids, refs, target):
        for source, first, _, q, z in gathered.sources(ids, refs, column):
            for b in range(per // lay.piece):
                at = column + b * lay.block - first
                yield (
                    source.at[:, at : at + lay.block],
                    target.at[
                        pl.ds(aligned(q * (per // lay.piece) + b, lay.piece), lay.piece),
                        pl.ds(aligned(z, lay.block), lay.block),
                    ],
                )
        yield refs[-1], target.at[:, pl.ds(aligned(ids[0], lay.block), lay.block)]

    return Weight(gathered, block, (rows, D), pairs, column)


def up_weight_of(gathered, block):
    lay = gathered.lay

    def pairs(ids, refs, target):
        for source, first, size, q, z in gathered.sources(ids, refs):
            rows = pl.ds(aligned(z * lay.s + q, lay.piece), lay.piece)
            yield source, target.at[rows, first : first + size]
        yield refs[-1], target.at[pl.ds(aligned(ids[0], lay.block), lay.block), :]

    return Weight(gathered, block, (D, block.shape[1]), pairs)


def down_weight_of(gathered, block):
    lay = gathered.lay
    rows = block.shape[0]
    per = rows // lay.s

    def pairs(ids, refs, target):
        for source, first, size, q, z in gathered.sources(ids, refs):
            row = aligned(q * (per // size) + first // size, size)
            yield source, target.at[pl.ds(row, size), pl.ds(aligned(z, lay.block), lay.block)]
        yield refs[-1], target.at[:, pl.ds(aligned(ids[0], lay.block), lay.block)]

    return Weight(gathered, block, (rows, D), pairs)


def store_piece(ids, keep, send, bit, q, value):
    spot = ((q >> (bit + 1)) << bit) + (q & ((1 << bit) - 1))
    mine = ((ids[1] >> bit) & 1) == ((q >> bit) & 1)
    pl.when(mine)(lambda: keep.__setitem__(spot, value))
    pl.when(jnp.logical_not(mine))(lambda: send.__setitem__(spot, value))


def small_chunks(refs):
    two, joint_a, joint_b, up, first = refs
    for row in range(4):
        yield from (two[row : row + 1, i : i + HDIM] for i in range(0, HALF, HDIM))
    for ref in (joint_a, joint_b):
        for head in range(ref.shape[0]):
            yield from (ref[head, :, i : i + HDIM] for i in range(0, ref.shape[2], HDIM))
    yield from (up[:, i : i + HDIM] for i in range(0, up.shape[1], HDIM))
    for begin in (0, HALF):
        for row in range(2):
            yield from (first[row : row + 1, i : i + HDIM] for i in range(begin, begin + HALF, HDIM))


def weight_grad(lay, ids, parts, orders, name, smalls, after=()):
    ins, widths = [(ids, smem())], []
    for sides in parts:
        for left, right in sides:
            ins.append((left, pl.BlockSpec((LEN, lay.block), lambda z: (0, z))))
            ins.append((right, whole(*right.shape)))
        widths.append(sum(right.shape[1] for _, right in sides))
    widths[0] += HDIM
    ins.extend((v, whole(*v.shape)) for v in smalls)
    n_out = 2 * len(orders)

    def kernel(ids, *refs):
        ins, outs, rows_ref = list(refs[: -n_out - 1]), refs[-n_out - 1 : -1], refs[-1]
        small_refs = ins[-len(smalls) :]

        def fill():
            rows_ref[...] = jnp.zeros_like(rows_ref)
            for i, chunk in enumerate(small_chunks(small_refs)):
                rows_ref[i : i + 1, :] = chunk

        pl.when(pl.program_id(0) == 0)(fill)
        for i, order in enumerate(orders):
            values = []
            for _ in parts[i]:
                left, right = ins.pop(0), ins.pop(0)
                values.append(dot(left[...], right[...], TN).astype(BF))
            if i == 0:
                values.append(rows_ref[...].astype(BF))
            block = jnp.concatenate(values, axis=1)
            for q in range(lay.s):
                part = block[q * lay.piece : (q + 1) * lay.piece]
                store_piece(ids, outs[2 * i], outs[2 * i + 1], order[0], q, part)

    outs = []
    for width in widths:
        out = pl.BlockSpec((lay.s // 2, lay.piece, width), lambda z: (z, 0, 0))
        outs += [(shape((lay.R * lay.s // 2, lay.piece, width)), out)] * 2
    return call(
        kernel, name, ins, outs, grid=(lay.R,), scratch=[pltpu.VMEM((lay.block, HDIM), F32)], after=after
    )


def output_grad(lay, ids, left, rights, orders, name, after):
    width = rights[0].shape[1]
    n_out = 2 * len(orders)
    if len(rights) != len(orders):
        return halves_grad(lay, ids, left, jnp.concatenate(rights, axis=1), orders, name, after)

    def kernel(ids, left_ref, *refs):
        for i, order in enumerate(orders):
            block = dot(left_ref[...], refs[i][...], TN).astype(BF)
            keep, send = refs[len(rights) + 2 * i : len(rights) + 2 * i + 2]
            for q in range(lay.s):
                store_piece(ids, keep, send, order[0], q, block[q * lay.piece : (q + 1) * lay.piece])

    out = pl.BlockSpec((lay.s // 2, lay.piece, width), lambda z: (z, 0, 0))
    return call(
        kernel,
        name,
        [(ids, smem()), (left, pl.BlockSpec((LEN, lay.block), lambda z: (0, z)))]
        + [(r, whole(*r.shape)) for r in rights],
        [(shape((lay.R * lay.s // 2, lay.piece, width)), out)] * n_out,
        grid=(lay.R,),
        after=after,
        mib=18,
    )


def halves_grad(lay, ids, left, right, orders, name, after):
    width = right.shape[1] // len(orders)
    n_out = 2 * len(orders)

    def kernel(ids, left_ref, right_ref, *outs):
        block = dot(left_ref[...], right_ref[...], TN).astype(BF)
        for i, order in enumerate(orders):
            for q in range(lay.s):
                keep, send, bit = outs[2 * i], outs[2 * i + 1], order[0]
                part = block[q * lay.piece : (q + 1) * lay.piece, i * width : (i + 1) * width]
                store_piece(ids, keep, send, bit, q, part)

    out = pl.BlockSpec((lay.s // 2, lay.piece, width), lambda z: (z, 0, 0))
    return call(
        kernel,
        name,
        [(ids, smem()), (left, pl.BlockSpec((LEN, lay.block), lambda z: (0, z))), (right, whole(*right.shape))],
        [(shape((lay.R * lay.s // 2, lay.piece, width)), out)] * n_out,
        grid=(lay.R,),
        after=after,
    )


class Reduction:
    def __init__(self, lay, ids, orders, parts):
        self.lay, self.ids, self.orders, self.step = lay, ids, orders, 0
        k = len(lay.split_bits)
        self.left = [sorted(set(range(k)) - {order[0]}, reverse=True) for order in orders]
        self.send(parts)

    def send(self, parts):
        self.keep, self.got = list(parts[0::2]), []
        for order, part in zip(self.orders, parts[1::2]):
            self.got.append(swap(part, "dp", self.lay.Q, self.lay.split_bits[order[self.step]]))
        self.step += 1

    def advance(self, after, name, passing=(), joined=()):
        lay, n = self.lay, len(self.orders)
        bits = [order[self.step] for order in self.orders]
        ins, outs = [(self.ids, smem())], []
        reds = [self, *joined]
        for i, bit in enumerate(bits):
            groups = lay.R * 2 ** self.left[i].index(bit)
            rows = 2 ** (len(self.left[i]) - 1 - self.left[i].index(bit)) * lay.piece
            width = sum(r.keep[i].shape[-1] for r in reds)
            for value in [v for r in reds for v in (r.keep[i], r.got[i])]:
                columns = value.shape[-1]
                ins.append(
                    (value.reshape(groups, 2, rows, columns), pl.BlockSpec((1, 2, rows, columns), lambda g: (g, 0, 0, 0)))
                )
            outs += [(shape((groups, rows, width)), pl.BlockSpec((1, rows, width), lambda g: (g, 0, 0)))] * 2

        def kernel(ids, *refs):
            ins, outs = list(refs[: 2 * n * len(reds)]), refs[2 * n * len(reds) :]
            for i, bit in enumerate(bits):
                mine = (ids[1] >> bit) & 1
                first = 0
                for _ in reds:
                    a, b = ins.pop(0), ins.pop(0)
                    last = first + a.shape[3]
                    for target, which in ((outs[2 * i], mine), (outs[2 * i + 1], 1 - mine)):
                        target[0, :, first:last] = (a[0, which].astype(F32) + b[0, which].astype(F32)).astype(BF)
                    first = last

        parts, token = call(kernel, name, ins, outs, grid=(groups,), after=after, passing=passing)
        self.left = [[b for b in left if b != bit] for left, bit in zip(self.left, bits)]
        self.send(parts[: 2 * n])
        return parts[2 * n :], token


def first_rows(reduction, after, name, passing=()):
    lay, ids, n = reduction.lay, reduction.ids, len(reduction.orders)
    ins = [(ids, smem())]
    widths = [keep.shape[-1] for keep in reduction.keep]
    starts = [sum(widths[:i]) for i in range(n)]
    columns = sum(widths)
    for i, width in enumerate(widths):
        for value in (reduction.keep[i], reduction.got[i]):
            value = value.reshape(lay.R // 2, 2, lay.piece, width)
            ins.append((value, pl.BlockSpec((1, 2, lay.piece, width), lambda g: (g, 0, 0, 0))))
    out = pl.BlockSpec((1, lay.piece, columns), lambda g: (g, 0, 0))

    def kernel(ids, *refs):
        ins, (keep, send) = refs[:-2], refs[-2:]
        mine = ids[0] & 1
        for target, bit in ((keep, mine), (send, 1 - mine)):
            for i in range(n):
                a, b = ins[2 * i], ins[2 * i + 1]
                total = (a[0, bit].astype(F32) + b[0, bit].astype(F32)).astype(BF)
                target[0, :, starts[i] : starts[i] + widths[i]] = total

    kind = shape((lay.R // 2, lay.piece, columns))
    (keep, send, *passed), token = call(
        kernel, name, ins, [(kind, out)] * 2, grid=(lay.R // 2,), after=after, passing=passing
    )
    return ((keep, swap(send, "row", lay.R, 1)), *passed), token


def next_rows(lay, ids, pair, after, name):
    token = after[0]
    for i, bit in list(enumerate(lay.row_bits))[1:]:
        keep, got = pair
        groups = keep.shape[0] // 2
        columns = keep.shape[-1]
        ins = [(ids, smem())]
        for value in pair:
            value = value.reshape(groups, 2, lay.piece, columns)
            ins.append((value, pl.BlockSpec((1, 2, lay.piece, columns), lambda g: (g, 0, 0, 0))))
        out = pl.BlockSpec((1, lay.piece, columns), lambda g: (g, 0, 0))

        def kernel(ids, a, b, keep, send, i=i):
            mine = (ids[0] >> i) & 1
            for target, which in ((keep, mine), (send, 1 - mine)):
                target[0] = (a[0, which].astype(F32) + b[0, which].astype(F32)).astype(BF)

        kind = shape((groups, lay.piece, columns))
        (keep, send), token = call(kernel, name, ins, [(kind, out)] * 2, grid=(groups,), after=(token, *after[1:]))
        pair = (keep, swap(send, "row", lay.R, bit))
    return pair, token


def row_total(lay, pair, after, name, ready=(), passing=()):
    width = pair[0].shape[-1]
    columns = width + sum(r.shape[1] for r in ready)

    def kernel(*refs):
        (*others, a, b), out = refs[:-1], refs[-1]
        column = 0
        for ref in others:
            out[:, column : column + ref.shape[1]] = ref[...]
            column += ref.shape[1]
        out[:, column:] = (a[...].astype(F32) + b[...].astype(F32)).astype(BF)

    (total, *passed), token = call(
        kernel,
        name,
        [(v, vmem()) for v in ready] + [(v.reshape(lay.piece, width), vmem()) for v in pair],
        [(shape((lay.piece, columns)), vmem())],
        after=after,
        passing=passing,
    )
    return (total, *passed), token


def rest_sum(lay, total):
    for bit in lay.rest_bits:
        total = (total.astype(F32) + swap(total, "dp", lay.Q, bit).astype(F32)).astype(BF)
    return total


def spread(lay, total):
    got = [total]
    for offset in range(1, lay.s):
        mask = sum(bit for i, bit in enumerate(lay.split_bits) if (offset >> i) & 1)
        got.append(swap(total, "dp", lay.Q, mask))
    return got


class Spread:
    def __init__(self, lay, total):
        self.lay = lay
        self.pieces = {0: total}
        for i in range(min(2, len(lay.split_bits))):
            self.pieces[1 << i] = swap(total, "dp", lay.Q, lay.split_bits[i])

    def forward(self, after, name):
        lay, token = self.lay, after[0]
        if len(lay.split_bits) >= 2:
            (left, right), token = cut(lay, [self.pieces[1][None], self.pieces[2][None]], 2, after, name)
            self.pieces[3] = (
                swap(left[0], "dp", lay.Q, lay.split_bits[1]),
                swap(right[0], "dp", lay.Q, lay.split_bits[0]),
            )
        for i, bit in list(enumerate(lay.split_bits))[2:]:
            for q, piece in list(self.pieces.items()):
                self.pieces[q | 1 << i] = jax.tree.map(lambda v: swap(v, "dp", lay.Q, bit), piece)
        return token

    def all(self):
        return [self.pieces[q] for q in range(self.lay.s)]


def finish(lay, ids, pieces, plan, name, after=()):
    outs = []
    for spans, transposed in plan:
        n = sum(c for _, c in spans)
        outs.append((shape((n, lay.block) if transposed else (lay.block, n), F32), vmem()))
    arrays = jax.tree.leaves(pieces)
    n_in = len(arrays)
    widest = max([HDIM] + [sum(c for _, c in spans) for spans, t in plan if t])

    def kernel(ids, *refs):
        ins, results, scratch = list(refs[:n_in]), refs[n_in:-1], refs[-1]
        values = []
        for piece in pieces:
            if isinstance(piece, tuple):
                values.append(jnp.concatenate([ins.pop(0)[...], ins.pop(0)[...]], axis=1))
            else:
                values.append(ins.pop(0))
        for (spans, transposed), result in zip(plan, results):
            column = 0
            for first, n in spans:
                for offset in range(lay.s):
                    rows = pl.ds(aligned(ids[1] ^ offset, lay.piece), lay.piece)
                    value = values[offset][:, first : first + n].astype(F32)
                    if transposed:
                        scratch[rows, column : column + n] = value
                    else:
                        result[rows, column : column + n] = value
                column += n
            if transposed:
                result[...] = scratch[:, :column].T

    return call(
        kernel,
        name,
        [(ids, smem())] + [(p, vmem()) for p in arrays],
        outs,
        scratch=[pltpu.VMEM((lay.block, widest), F32)],
        after=after,
        mib=18,
    )


def both(own, other):
    return jnp.concatenate([own, other], axis=1)


def row_stats(values):
    average = jnp.mean(values, axis=1, keepdims=True)
    square = jnp.mean(values * values, axis=1, keepdims=True)
    return average, lax.rsqrt(square - average * average + EPSILON)


def norm_grad(gradient, centered, factor, gain):
    scaled = gradient * gain
    first = jnp.mean(scaled, axis=1, keepdims=True)
    second = jnp.mean(scaled * centered, axis=1, keepdims=True)
    return factor * (scaled - first - centered * second)


V_GAIN1, V_SHIFT1, V_GAIN2, V_SHIFT2, V_OBIAS = range(5)


def pair_row(own_ref, other_ref, i):
    return both(own_ref[i : i + 1, :], other_ref[i : i + 1, :])


def branch_sum(own, other):
    return own[...].astype(F32) + both(other[:, HALF:], other[:, :HALF]).astype(F32)


def pair_up(pairs, after):
    def kernel(*refs):
        n = len(pairs)
        for i in range(n):
            refs[2 * n + i][:, :HALF] = refs[2 * i][...]
            refs[2 * n + i][:, HALF:] = refs[2 * i + 1][...]

    return call(
        kernel,
        "pair_up",
        [(v, row_tile(HALF)) for pair in pairs for v in pair],
        [(shape((LEN, D)), row_tile(D))] * len(pairs),
        grid=ROW_GRID,
        after=after,
    )


def first_norm_project(ids, x, vecs, bias, joint, after):
    width = bias.shape[1]

    def kernel(ids, x_ref, vo, vt, bias, *refs):
        pieces, full, qkv, weight, sems = refs[: joint.n], *refs[joint.n :]
        copies = joint.copies(ids, pieces, weight, sems)
        first = pl.program_id(0) == 0
        pl.when(first)(lambda: start_all(copies))
        values = x_ref[...].astype(F32)
        average, factor = row_stats(values)
        normed = (values - average) * factor * pair_row(vo, vt, V_GAIN1) + pair_row(vo, vt, V_SHIFT1)
        low = normed.astype(BF)
        full[...] = low
        pl.when(first)(lambda: wait_all(copies))
        qkv[...] = (dot(low, weight[...]) + bias[...]).astype(BF)

    return call(
        kernel,
        "first_norm_project",
        [(ids, smem()), (x, row_tile(D)), *[(v, whole(8, HALF)) for v in vecs], (bias, whole(1, width))]
        + joint.operands,
        [(hbm((LEN, D)), row_tile(D)), (shape((LEN, width)), row_tile(width))],
        grid=ROW_GRID,
        scratch=joint.scratch,
        after=after,
    )


def visible_mask(lo, rows, queries, prefix):
    key_id = lax.broadcasted_iota(jnp.int32, (rows, queries), 0) + lo
    query_id = lax.broadcasted_iota(jnp.int32, (rows, queries), 1) + lo
    return (key_id <= query_id) | (key_id < prefix)


def attend(prefix_ref, qkv_ref, out_ref, log_ref):
    bq = 512
    prefix_end = prefix_ref[0]
    for h in range(log_ref.shape[0]):
        base = h * 3 * HDIM
        keys = qkv_ref[:, base + HDIM : base + 2 * HDIM]
        values_t = qkv_ref[:, base + 2 * HDIM : base + 3 * HDIM].T
        for lo in range(0, LEN, bq):
            n = max(MAX_PREFIX, lo + bq)
            query = qkv_ref[lo : lo + bq, base : base + HDIM]
            scores = dot(keys[:n], query, NT)
            tail = jnp.where(visible_mask(lo, n - lo, bq, prefix_end), scores[lo:], NEGATIVE)
            scores = tail if lo == 0 else jnp.concatenate([scores[:lo], tail], axis=0)
            top = jnp.max(scores, axis=0, keepdims=True) * (SCALE * LOG2E)
            weights = jnp.exp2(scores * (SCALE * LOG2E) - top)
            total = jnp.sum(weights, axis=0, keepdims=True)
            mixed = dot(values_t[:, :n], weights.astype(BF)) * (1.0 / total)
            out_ref[lo : lo + bq, h * HDIM : (h + 1) * HDIM] = mixed.T.astype(BF)
            log_ref[h, :, lo : lo + bq] = top + jnp.log2(total)


def attention_first(prefix, qkv, heads, after):
    return call(
        attend,
        "attention_first",
        [(prefix, smem()), (qkv, pl.BlockSpec((LEN, 3 * HDIM * heads), lambda i: (0, 0)))],
        [
            (shape((LEN, HDIM * heads)), whole(LEN, HDIM * heads)),
            (shape((heads, 1, LEN), F32), whole(heads, 1, LEN)),
        ],
        grid=(1,),
        after=after,
    )


def attention_second(ids, prefix, qkv, heads, attended_first, output, after):
    width = HDIM * heads

    def kernel(ids, prefix_ref, qkv_ref, first_ref, *refs):
        pieces, (out_ref, log_ref, branch, weight, sems) = refs[: output.n], refs[output.n :]
        copies = output.copies(ids, pieces, weight, sems)
        start_all(copies)
        attend(prefix_ref, qkv_ref, out_ref, log_ref)
        wait_all(copies)
        for lo in range(0, LEN, TILE):
            rows = slice(lo, lo + TILE)
            branch[rows, :] = dot(both(first_ref[rows, :], out_ref[rows, :]), weight[...]).astype(BF)

    return call(
        kernel,
        "attention_second",
        [(ids, smem()), (prefix, smem()), (qkv, pl.BlockSpec((LEN, 3 * HDIM * heads), lambda i: (0, 1))),
         (attended_first, whole(LEN, width))]
        + output.operands,
        [
            (shape((LEN, width)), whole(LEN, width)),
            (shape((heads, 1, LEN), F32), whole(heads, 1, LEN)),
            (shape((LEN, D)), whole(LEN, D)),
        ],
        grid=(1,),
        scratch=output.scratch,
        after=after,
    )


def second_norm_up(ids, x, parts, vecs, bias, up, after):
    width = bias.shape[1]

    def kernel(ids, x_ref, po, pt, vo, vt, bias, *refs):
        pieces = refs[: up.n]
        residual, centered, factor_ref, full, active, slope, weight, sems = refs[up.n :]
        copies = up.copies(ids, pieces, weight, sems)
        first = pl.program_id(0) == 0
        pl.when(first)(lambda: start_all(copies))
        res = x_ref[...].astype(F32) + (branch_sum(po, pt) + pair_row(vo, vt, V_OBIAS))
        residual[...] = res[:, :HALF]
        average, factor = row_stats(res)
        cent = (res - average) * factor
        centered[...] = cent.astype(BF)
        factor_ref[...] = factor
        low = (cent * pair_row(vo, vt, V_GAIN2) + pair_row(vo, vt, V_SHIFT2)).astype(BF)
        full[...] = low
        pl.when(first)(lambda: wait_all(copies))
        hidden = dot(low, weight[...]) + bias[...]
        bell = jnp.exp(-0.5 * hidden * hidden) * (1.0 / math.sqrt(2.0 * math.pi))
        phi = 0.5 * (1.0 + lax.erf(hidden * 2.0**-0.5))
        active[...] = (hidden * phi).astype(BF)
        slope[...] = (phi + hidden * bell).astype(BF)

    return call(
        kernel,
        "second_norm_up",
        [(ids, smem()), (x, row_tile(D)), *[(p, row_tile(D)) for p in parts], *[(v, whole(8, HALF)) for v in vecs],
         (bias, whole(1, width))]
        + up.operands,
        [
            (hbm((LEN, HALF), F32), row_tile(HALF)),
            (hbm((LEN, D)), row_tile(D)),
            (hbm((LEN, 1), F32), row_tile(1)),
            (hbm((LEN, D)), row_tile(D)),
            (shape((LEN, width)), row_tile(width)),
            (shape((LEN, width)), row_tile(width)),
        ],
        grid=ROW_GRID,
        scratch=up.scratch,
        after=after,
    )


def hidden_backward(ids, cot, slope, up, down, after):
    width = slope.shape[1]

    def kernel(ids, cot_ref, slope_ref, *refs):
        up_pieces, refs = refs[: up.n], refs[up.n :]
        down_pieces, refs = refs[: down.n], refs[down.n :]
        hidden_grad, partial, bias_grad, up_full, up_sems, down_full, down_sems = refs
        down_copies = down.copies(ids, down_pieces, down_full, down_sems)
        up_copies = up.copies(ids, up_pieces, up_full, up_sems)
        first = pl.program_id(0) == 0

        def begin():
            start_all(down_copies)
            start_all(up_copies)
            bias_grad[...] = jnp.zeros_like(bias_grad)
            wait_all(down_copies)

        pl.when(first)(begin)
        grad = dot(cot_ref[...], down_full[...], NT) * slope_ref[...].astype(F32)
        low = grad.astype(BF)
        hidden_grad[...] = low
        bias_grad[...] += jnp.sum(low.astype(F32), axis=0, keepdims=True)
        pl.when(first)(lambda: wait_all(up_copies))
        partial[...] = dot(low, up_full[...], NT).astype(BF)

    return call(
        kernel,
        "hidden_backward",
        [(ids, smem()), (cot, row_tile(D)), (slope, row_tile(width))] + up.operands + down.operands,
        [(hbm((LEN, width)), row_tile(width)), (shape((LEN, D)), row_tile(D)), (shape((1, width), F32), whole(1, width))],
        grid=ROW_GRID,
        scratch=up.scratch + down.scratch,
        after=after,
    )


def second_norm_backward(ids, cot, parts, centered, factor, vecs, output, after):
    width = output.dims[0]

    def kernel(ids, cot_ref, po, pt, cent_ref, factor_ref, vo, vt, *refs):
        pieces, (branch, res_grad, att_grad, sums_ref, weight, sems) = refs[: output.n], refs[output.n :]
        copies = output.copies(ids, pieces, weight, sems)
        first = pl.program_id(0) == 0

        def begin():
            start_all(copies)
            sums_ref[...] = jnp.zeros_like(sums_ref)

        pl.when(first)(begin)
        grad = branch_sum(po, pt)
        cent = cent_ref[...].astype(F32)
        cot = cot_ref[...].astype(F32)
        total = cot + norm_grad(grad, cent, factor_ref[...], pair_row(vo, vt, V_GAIN2))
        low = total.astype(BF)
        branch[...] = low
        res_grad[...] = total[:, :HALF]
        news = (grad[:, :HALF] * cent[:, :HALF], grad[:, :HALF], low[:, :HALF].astype(F32), cot[:, :HALF])
        for i, value in enumerate(news):
            sums_ref[i : i + 1, :] += jnp.sum(value, axis=0, keepdims=True)
        pl.when(first)(lambda: wait_all(copies))
        att_grad[...] = dot(low, weight[...], NT).astype(BF)

    return call(
        kernel,
        "second_norm_backward",
        [(ids, smem()), (cot, row_tile(D)), *[(p, row_tile(D)) for p in parts], (centered, row_tile(D)),
         (factor, row_tile(1)), *[(v, whole(8, HALF)) for v in vecs]]
        + output.operands,
        [
            (shape((LEN, D)), row_tile(D)),
            (shape((LEN, HALF), F32), row_tile(HALF)),
            (shape((LEN, width)), row_tile(width)),
            (shape((4, HALF), F32), whole(4, HALF)),
        ],
        grid=ROW_GRID,
        scratch=output.scratch,
        after=after,
    )


def attention_backward(prefix, qkv, grads, logs, attended, first_head, heads, after):
    bq = 256

    def kernel(prefix_ref, qkv_ref, grad_ref, log_ref, att_ref, out_ref, sums_ref, key_sum, value_sum):
        prefix_end = prefix_ref[0]
        keys = qkv_ref[:, HDIM : 2 * HDIM]
        values = qkv_ref[:, 2 * HDIM : 3 * HDIM]
        keys_t = keys.T
        query_total = jnp.zeros((1, HDIM), F32)
        for lo in reversed(range(0, LEN, bq)):
            n = max(MAX_PREFIX, lo + bq)
            query = qkv_ref[lo : lo + bq, 0:HDIM]
            grad = grad_ref[lo : lo + bq, :]
            scores = dot(keys[:n], query, NT) * (SCALE * LOG2E)
            weights = jnp.exp2(scores - log_ref[0, :, lo : lo + bq])
            tail = jnp.where(visible_mask(lo, n - lo, bq, prefix_end), weights[lo:], 0.0)
            weights = tail if lo == 0 else jnp.concatenate([weights[:lo], tail], axis=0)
            weight_grad_t = dot(values[:n], grad, NT)
            mixed = grad.astype(F32) * att_ref[lo : lo + bq, :].astype(F32)
            delta = jnp.sum(mixed.T, axis=0, keepdims=True)
            score_grad = (weights * (weight_grad_t - delta)).astype(BF)
            value_part = dot(weights.astype(BF), grad)
            key_part = dot(score_grad, query)
            if lo + bq == LEN:
                value_sum[...] = value_part
                key_sum[...] = key_part
            else:
                value_sum[:n, :] += value_part
                key_sum[:n, :] += key_part
            query_part = (dot(keys_t[:, :n], score_grad).T * SCALE).astype(BF)
            out_ref[lo : lo + bq, 0:HDIM] = query_part
            query_total = query_total + jnp.sum(query_part.astype(F32), axis=0, keepdims=True)
        out_ref[:, HDIM : 2 * HDIM] = (key_sum[...] * SCALE).astype(BF)
        value_low = value_sum[...].astype(BF)
        out_ref[:, 2 * HDIM : 3 * HDIM] = value_low
        sums_ref[0] = both(query_total, jnp.sum(value_low.astype(F32), axis=0, keepdims=True))

    return call(
        kernel,
        "attention_backward",
        [
            (prefix, smem()),
            (qkv, pl.BlockSpec((LEN, 3 * HDIM), lambda h: (0, h + first_head))),
            (grads, pl.BlockSpec((LEN, HDIM), lambda h: (0, h + first_head))),
            (logs, pl.BlockSpec((1, 1, LEN), lambda h: (h, 0, 0))),
            (attended, pl.BlockSpec((LEN, HDIM), lambda h: (0, h))),
        ],
        [
            (shape((LEN, 3 * HDIM * heads)), pl.BlockSpec((LEN, 3 * HDIM), lambda h: (0, h))),
            (shape((heads, 1, 2 * HDIM), F32), pl.BlockSpec((1, 1, 2 * HDIM), lambda h: (h, 0, 0))),
        ],
        grid=(heads,),
        scratch=[pltpu.VMEM((LEN, HDIM), F32), pltpu.VMEM((LEN, HDIM), F32)],
        after=after,
    )


def project_backward(ids, grads, x, vecs, joint, after):
    widths = [g.shape[1] for g in grads]

    def kernel(ids, x_ref, vo, vt, *refs):
        grad_refs, refs = refs[: len(grads)], refs[len(grads) :]
        pieces, (own, other, sums, columns, weight, sems) = refs[: joint.n], refs[joint.n :]
        copies = joint.copies(ids, pieces, weight, sems)
        first = pl.program_id(0) == 0

        def begin():
            start_all(copies)
            columns[...] = jnp.zeros_like(columns)

        pl.when(first)(begin)
        values = x_ref[...].astype(F32)
        average, factor = row_stats(values)
        pl.when(first)(lambda: wait_all(copies))
        total, column = 0.0, 0
        for ref, width in zip(grad_refs, widths):
            total = total + dot(ref[...], weight[:, column : column + width], NT)
            column += width
        own[...] = total[:, :HALF].astype(BF)
        other[:, :HALF] = total[:, HALF:].astype(BF)
        gain = pair_row(vo, vt, V_GAIN1)
        product = total * ((values - average) * factor)
        columns[0:1, :] += jnp.sum(product, axis=0, keepdims=True)
        columns[1:2, :] += jnp.sum(total, axis=0, keepdims=True)
        lane = lax.broadcasted_iota(jnp.int32, (TILE, HDIM), 1)
        packed = jnp.zeros((TILE, HDIM), F32)
        parts = jnp.zeros((TILE, HDIM), F32)
        for i, value in enumerate((total * gain, product * gain)):
            row_sum = jnp.sum(value, axis=1, keepdims=True)
            high = row_sum.astype(BF).astype(F32)
            packed = jnp.where(lane == 2 * i, high, jnp.where(lane == 2 * i + 1, row_sum - high, packed))
            parts = jnp.where(lane == i, row_sum, parts)
        other[:, HALF:] = packed.astype(BF)
        sums[...] = parts

    return call(
        kernel,
        "project_backward",
        [(ids, smem()), (x, row_tile(D)), *[(v, whole(8, HALF)) for v in vecs]]
        + [(g, row_tile(g.shape[1])) for g in grads]
        + joint.operands,
        [
            (shape((LEN, HALF)), row_tile(HALF)),
            (shape((LEN, HALF + HDIM)), row_tile(HALF + HDIM)),
            (shape((LEN, HDIM), F32), row_tile(HDIM)),
            (shape((8, D), F32), whole(8, D)),
        ],
        grid=ROW_GRID,
        scratch=joint.scratch,
        after=after,
    )


MOST = LEN // 2


def most_tiles(width):
    return [
        pl.BlockSpec((TILE, width), lambda i: (jnp.minimum(i, MOST // TILE - 1), 0)),
        pl.BlockSpec((TILE, width), lambda i: (jnp.maximum(i - MOST // TILE, 0), 0)),
    ]


def in_most():
    return pl.program_id(0) < MOST // TILE


def down_project(ids, active, down, after):
    def kernel(ids, a_ref, *refs):
        pieces, (own, other, rest, weight, sems) = refs[: down.n], refs[down.n :]
        copies = down.copies(ids, pieces, weight, sems)

        def begin():
            start_all(copies)
            wait_all(copies)

        pl.when(pl.program_id(0) == 0)(begin)
        value = dot(a_ref[...], weight[...]).astype(BF)
        own[...] = value[:, :HALF]
        pl.when(in_most())(lambda: other.__setitem__(..., value[:, HALF:]))
        pl.when(jnp.logical_not(in_most()))(lambda: rest.__setitem__(..., value[:, HALF:]))

    return call(
        kernel,
        "down_project",
        [(ids, smem()), (active, row_tile(active.shape[1]))] + down.operands,
        [(shape((LEN, HALF)), row_tile(HALF))]
        + [(shape((n, HALF)), spec) for n, spec in zip((MOST, LEN - MOST), most_tiles(HALF))],
        grid=ROW_GRID,
        scratch=down.scratch,
        after=after,
    )


def add_output(residual, own, got, bias, after):
    def kernel(res, a, most, rest, bias, out):
        b = jnp.where(in_most(), most[...], rest[...])
        out[...] = (res[...] + (a[...].astype(F32) + b.astype(F32) + bias[...])).astype(BF)

    return call(
        kernel,
        "add_output",
        [(residual, row_tile(HALF)), (own, row_tile(HALF)), *zip(got, most_tiles(HALF)), (bias, whole(1, HALF))],
        [(shape((LEN, HALF)), row_tile(HALF))],
        grid=ROW_GRID,
        after=after,
    )


def first_norm_backward(x, own, other, sums, vecs, res_grad, after):
    def kernel(x_ref, po, pt, so, vo, res_ref, out):
        values = x_ref[...].astype(F32)
        average, factor = row_stats(values)
        cent = (values[:, :HALF] - average) * factor
        grad = po[...].astype(F32) + pt[:, :HALF].astype(F32)
        got = pt[:, HALF:].astype(F32)
        first = (so[:, 0:1] + (got[:, 0:1] + got[:, 1:2])) * (1.0 / D)
        second = (so[:, 1:2] + (got[:, 2:3] + got[:, 3:4])) * (1.0 / D)
        back = factor * (grad * vo[V_GAIN1 : V_GAIN1 + 1, :] - first - cent * second)
        out[...] = (res_ref[...] + back).astype(BF)

    return call(
        kernel,
        "first_norm_backward",
        [(x, row_tile(D)), (own, row_tile(HALF)), (other, row_tile(HALF + HDIM)), (sums, row_tile(HDIM)),
         (vecs[0], whole(8, HALF)), (res_grad, row_tile(HALF))],
        [(shape((LEN, HALF)), row_tile(HALF))],
        grid=ROW_GRID,
        after=after,
    )


def layer(lay, tokens_in, cotangent, prefix_length, first_gain, first_shift, joint_weight, joint_bias,
          output_weight, output_bias, second_gain, second_shift, up_weight, up_bias, down_weight, down_bias):
    heads = joint_bias.shape[0] // (2 * HDIM)
    ids = device_ids(lay)

    j_width, o_rows, ff = joint_weight.shape[1], output_weight.shape[0], down_weight.shape[0]
    per = o_rows // lay.s
    jo_piece = own_pieces(
        ids, [(joint_weight, lay.piece, 0), *[(output_weight, per, b * lay.piece) for b in range(per // lay.piece)]], lay.piece
    )
    jo = Gathered(lay, jo_piece, 2, "joint_pieces", True)

    zero_row = jnp.zeros_like(first_gain)
    vec_own = jnp.stack(
        [first_gain, first_shift, second_gain, second_shift, output_bias, zero_row, zero_row, zero_row]
    )
    vecs = (vec_own, swap_cores(vec_own))
    bias_rows = joint_bias.reshape(heads, 2, HDIM)
    joint_row = jnp.stack([bias_rows[:, 0], jnp.zeros_like(bias_rows[:, 0]), bias_rows[:, 1]], axis=1).reshape(1, -1)
    (x, cot), token = pair_up(
        [(tokens_in, swap_cores(tokens_in)), (cotangent, swap_cores(cotangent))], (*vecs, joint_row)
    )

    token = jo.spread((token,))
    up_piece, up_token = extract(lay, ids, up_weight, lay.piece, (token,))
    up = Gathered(lay, up_piece, 2, "up_pieces", False)
    token = up.double((up_token,))
    token = jo.forward((token,))
    down_piece, down_token = extract(lay, ids, down_weight, ff // lay.s, (token, *up.got))
    down = Gathered(lay, down_piece, 1, "down_pieces", False)
    token = up.spread((token, *jo.arrays()))
    joint_w = joint_weight_of(jo, joint_weight)
    output_w = output_weight_of(jo, output_weight, j_width)

    (full_one, qkv), token = first_norm_project(
        ids, x, vecs, joint_row, joint_w, (up.others, down_token)
    )
    pair = heads // 2
    token = down.double((token,))
    (attended_a, logs_a), token = attention_first(prefix_length, qkv, pair, (token,))
    token = up.forward((token,))
    up_w = up_weight_of(up, up_weight)
    (attended_b, logs_b, branch), token = attention_second(
        ids, prefix_length, qkv, pair, attended_a, output_w, (token,)
    )
    token = down.spread((token,))
    (branch,), token = hold([branch], (token, *up.arrays()), "hold_branch")
    (residual, centered, factor, full_two, active, slope), token = second_norm_up(
        ids, x, (branch, swap_cores(branch)), vecs, up_bias.reshape(1, -1), up_w, (token,)
    )
    token = down.forward((token,))
    down_w = down_weight_of(down, down_weight)
    both_orders = [lay.order_a, lay.order_b]
    later_steps = range(len(lay.split_bits) - 1)
    down_parts, token = halves_grad(lay, ids, cot, active, both_orders, "down_grad", (token,))
    down_parts, token = hold(down_parts, (token, *down.arrays()), "hold_down")
    down_red = Reduction(lay, ids, both_orders, down_parts)

    (hidden_grad, norm_part, up_bias_grad), token = hidden_backward(ids, cot, slope, up_w, down_w, (token,))
    passed, token = halves_grad(lay, ids, full_two, hidden_grad, both_orders, "up_grad", (token,))
    passed = [norm_part, *passed]
    for _ in later_steps:
        passed, token = down_red.advance((token,), "down_sum", passed)
    norm_part, *up_parts = passed
    up_red = Reduction(lay, ids, both_orders, up_parts)
    norm_parts = (norm_part, swap_cores(norm_part))
    (branch_grad, res_grad, att_grad, sums_two), token = second_norm_backward(
        ids, cot, norm_parts, centered, factor, vecs, output_w, (token,)
    )
    (qkv_grad_a, joint_sums_a), token = attention_backward(
        prefix_length, qkv, att_grad, logs_a, attended_a, 0, pair, (token,)
    )
    (qkv_grad_b, joint_sums_b), token = attention_backward(
        prefix_length, qkv, att_grad, logs_b, attended_b, pair, pair, (token,)
    )
    (down_rows,), token = first_rows(down_red, (token,), "down_rows")
    output_parts, token = output_grad(lay, ids, branch_grad, (attended_a, attended_b), both_orders, "output_grad", (token,))
    output_red = Reduction(lay, ids, both_orders, output_parts)
    (first_own, first_send, row_sums, first_sums), token = project_backward(
        ids, [qkv_grad_a, qkv_grad_b], x, vecs, joint_w, (token,)
    )
    down_rows, token = next_rows(lay, ids, down_rows, (token,), "down_rows_2")
    for i in later_steps:
        _, token = up_red.advance((token,), "up_sum", (), (output_red,) if i == 0 else ())
    joint_parts, token = weight_grad(
        lay,
        ids,
        [[(full_one, qkv_grad_a)], [(full_one, qkv_grad_b)]],
        both_orders,
        "joint_grad",
        (sums_two, joint_sums_a, joint_sums_b, up_bias_grad, first_sums),
        (token,),
    )
    joint_red = Reduction(lay, ids, both_orders, joint_parts)
    (down_own, *down_send), token = down_project(ids, active, down_w, (token,))
    (down_total,), token = row_total(lay, down_rows, (token,), "down_total")
    (up_rows, *down_send), token = first_rows(up_red, (token,), "up_rows", down_send)
    (layer_out,), token = add_output(
        residual, down_own, [swap_cores(p) for p in down_send], down_bias.reshape(1, -1), (token,)
    )
    up_rows, token = next_rows(lay, ids, up_rows, (token,), "up_rows_2")
    passed = [first_send]
    for _ in later_steps:
        passed, token = joint_red.advance((token,), "joint_sum", passed)
    (tokens_grad,), token = first_norm_backward(
        x, first_own, swap_cores(passed[0]), row_sums, vecs, res_grad, (token,)
    )
    (ffn_total,), token = row_total(lay, up_rows, (token,), "up_total", [down_total])
    ffn = Spread(lay, rest_sum(lay, ffn_total))
    (joint_rows,), token = first_rows(joint_red, (token,), "joint_rows")
    joint_rows, token = next_rows(lay, ids, joint_rows, (token,), "joint_rows_2")
    token = ffn.forward((token,), "ffn_pieces")
    (joint_total,), token = row_total(lay, joint_rows, (token,), "joint_total")
    joint_pieces = spread(lay, rest_sum(lay, joint_total))
    up_mid, o_mid = ff // 2, o_rows // 2
    up_half = up_mid + o_mid
    (grad_down, grad_up, grad_output), token = finish(
        lay,
        ids,
        ffn.all(),
        [
            ([(0, ff)], True),
            ([(ff, up_mid), (ff + up_half, up_mid)], False),
            ([(ff + up_mid, o_mid), (ff + up_half + up_mid, o_mid)], True),
        ],
        "finish_ffn",
        (token,),
    )
    mid = j_width // 2
    (grad_joint, small), token = finish(
        lay,
        ids,
        joint_pieces,
        [([(0, mid), (mid + HDIM, mid)], False), ([(mid, HDIM)], False)],
        "finish_attention",
        (token,),
    )
    small = small.reshape(-1)
    joint_n, up_n = joint_bias.shape[0], up_bias.shape[0]
    first_at = 4 * HALF + joint_n + up_n
    sums_one = small[first_at : first_at + 2 * HALF] + swap_cores(small[first_at + 2 * HALF : first_at + 4 * HALF])

    def take(start, n):
        return lax.slice_in_dim(small, start, start + n, axis=0)

    return (
        layer_out,
        tokens_grad,
        sums_one[:HALF],
        sums_one[HALF:],
        grad_joint,
        take(4 * HALF, joint_n),
        grad_output,
        take(2 * HALF, HALF),
        take(0, HALF),
        take(HALF, HALF),
        grad_up,
        take(4 * HALF + joint_n, up_n),
        grad_down,
        take(3 * HALF, HALF),
    )


def solution(mesh):
    lay = Layout(mesh)
    vec, rows, cols, flat = P("col"), P("row", "col"), P("col", "row"), P(("dp", "row"), "col")

    def shards(*args):
        return layer(lay, *args)

    return jax.shard_map(
        shards,
        mesh=mesh,
        in_specs=(flat, flat, P(("dp", "row")), vec, vec, rows, vec, cols, vec, vec, vec, rows, vec, cols, vec),
        out_specs=(flat, flat, vec, vec, rows, vec, cols, vec, vec, vec, rows, vec, cols, vec),
        check_vma=False,
    )
```

```python
import math

import jax
import jax.numpy as jnp
from jax import lax
from jax.experimental import pallas as pl
from jax.experimental.pallas import tpu as pltpu
from jax.sharding import PartitionSpec as P

D = 1024
HALF = 512
HDIM = 128
LEN = 1024
MAX_PREFIX = 512
EPSILON = 1e-05
NEGATIVE = -1e30
LOG2E = math.log2(math.e)
SCALE = HDIM**-0.5
TILE = 256

BF = jnp.bfloat16
F32 = jnp.float32
NT = (((1,), (1,)), ((), ()))
TN = (((0,), (0,)), ((), ()))


def vmem():
    return pl.BlockSpec(memory_space=pltpu.VMEM)


def smem():
    return pl.BlockSpec(memory_space=pltpu.SMEM)


def anywhere():
    return pl.BlockSpec(memory_space=pltpu.HBM)


def params(mib=60):
    return pltpu.CompilerParams(vmem_limit_bytes=mib << 20)


def shape(dims, kind=BF):
    return jax.ShapeDtypeStruct(tuple(dims), kind)


def hbm(dims, kind=BF):
    return pltpu.HBM(tuple(dims), kind)


def dot(left, right, dims=(((1,), (0,)), ((), ()))):
    return lax.dot_general(left, right, dims, preferred_element_type=F32)


class Layout:
    def __init__(self, mesh):
        self.R = mesh.shape["row"]
        self.Q = mesh.shape["dp"]
        self.block = D // self.R
        s = self.Q
        while self.block // s < 16:
            s //= 2
        self.s = s
        self.piece = self.block // s
        bits = self.Q.bit_length() - 1
        low = [1 << b for b in range(bits // 2)]
        high = [1 << b for b in range(bits // 2, bits)]
        mixed = []
        while low or high:
            if low:
                mixed.append(low.pop(0))
            if high:
                mixed.append(high.pop(0))
        k = s.bit_length() - 1
        self.split_bits = mixed[:k]
        self.rest_bits = mixed[k:]
        self.order_a = list(range(k))
        self.order_b = [1, 0] + list(range(2, k)) if k >= 2 else list(range(k))
        self.row_bits = [1 << b for b in range(self.R.bit_length() - 1)]


def swap(value, axis, size, bit):
    return lax.ppermute(value, axis, [(i, i ^ bit) for i in range(size)])


def swap_cores(value):
    return lax.ppermute(value, "col", [(0, 1), (1, 0)])


def device_ids(lay):
    z = lax.axis_index("row")
    d = lax.axis_index("dp")
    c = lax.axis_index("col")
    q = sum(((d // bit) % 2) << i for i, bit in enumerate(lay.split_bits))
    return jnp.stack([z ^ (c * (lay.R // 2)), q, c]).astype(jnp.int32)


COST = {
    "first_norm_project": 9,
    "attention_first": 5,
    "attention_second": 7,
    "second_norm_up": 15,
    "down_grad": 9,
    "hidden_backward": 17,
    "up_grad": 9,
    "second_norm_backward": 9,
    "attention_backward": 6,
    "joint_grad": 10,
    "project_backward": 8,
    "first_norm_backward": 6,
    "down_project": 9,
    "joint_sum": 32,
}
WIDE = {"second_norm_up": 18, "hidden_backward": 18, "attention_second": 18}
COST_SCALE = 0.25 * 3.69e6


def call(kernel, name, ins, outs, grid=(), scratch=(), after=(), passing=(), mib=None):
    n_in, n_after, n_out, n_pass = len(ins), len(after), len(outs), len(passing)

    def body(*refs):
        refs = list(refs)
        first_out = n_in + n_after + n_pass
        token = first_out + n_out + n_pass
        kernel(*refs[:n_in], *refs[first_out : first_out + n_out], *refs[token + 1 :])

    results = pl.pallas_call(
        body,
        grid=grid,
        in_specs=[spec for _, spec in ins] + [anywhere()] * (n_after + n_pass),
        out_specs=[spec for _, spec in outs] + [anywhere()] * (n_pass + 1),
        out_shape=[kind for kind, _ in outs]
        + [shape(a.shape, a.dtype) for a in passing]
        + [shape((8, HDIM), F32)],
        scratch_shapes=list(scratch),
        compiler_params=params(mib or (WIDE.get(name, 12) if name in COST else 8)),
        input_output_aliases={n_in + n_after + i: n_out + i for i in range(n_pass)},
        cost_estimate=pl.CostEstimate(
            flops=1, bytes_accessed=int(COST_SCALE * COST.get(name, 2)), transcendentals=0
        ),
        name=name,
    )(*[array for array, _ in ins], *after, *passing)
    return results[:-1], results[-1]


def hold(arrays, after, name):
    return call(lambda: None, name, [], [], after=after, passing=arrays, mib=8)


def row_tile(width):
    return pl.BlockSpec((TILE, width), lambda i: (i, 0))


def whole(*dims):
    return pl.BlockSpec(dims, lambda i: (0,) * len(dims))


ROW_GRID = (LEN // TILE,)


def own_pieces(ids, parts, rows):
    return jnp.concatenate(
        [lax.dynamic_slice_in_dim(block, ids[1] * step + first, rows, axis=0) for block, step, first in parts], axis=1
    )


def extract(lay, ids, block, rows, after):
    def kernel(ids, source, out, sem):
        copy = pltpu.make_async_copy(source.at[pl.ds(pl.multiple_of(ids[1] * rows, 16), rows), :], out, sem)
        copy.start()
        copy.wait()

    (out,), token = call(
        kernel,
        "extract",
        [(ids, smem()), (block, anywhere())],
        [(shape((rows, block.shape[1])), vmem())],
        scratch=[pltpu.SemaphoreType.DMA],
        after=after,
    )
    return out, token


def cut(lay, arrays, axis, after, name):
    n, rows, columns = arrays[0].shape
    rows, columns = (rows // 2, columns) if axis == 1 else (rows, columns // 2)
    kind = shape((n, rows, columns))

    def spec(i):
        return pl.BlockSpec((1, rows, columns), lambda k: (k, i, 0) if axis == 1 else (k, 0, i))

    def kernel(a, b, left, right):
        left[...] = a[...]
        right[...] = b[...]

    out = pl.BlockSpec((1, rows, columns), lambda k: (k, 0, 0))
    return call(
        kernel, name, [(arrays[0], spec(0)), (arrays[1], spec(1))], [(kind, out)] * 2, grid=(n,), after=after
    )


def join(arrays, after, name):
    rows = sum(a.shape[0] for a in arrays)

    def kernel(*refs):
        at = 0
        for ref in refs[:-1]:
            refs[-1][at : at + ref.shape[0]] = ref[...]
            at += ref.shape[0]

    (out,), token = call(
        kernel, name, [(a, vmem()) for a in arrays], [(shape((rows, *arrays[0].shape[1:])), vmem())], after=after
    )
    return out, token


class Gathered:
    def __init__(self, lay, piece, axis, name, at_once):
        self.lay, self.axis, self.name = lay, axis, name
        piece = piece[None]
        if at_once:
            self.z_offsets = list(range(1, lay.R))
            self.got = [swap(piece, "row", lay.R, k) for k in self.z_offsets]
            self.bits = []
        else:
            self.bits = list(reversed(lay.row_bits))
            self.held, self.held_offsets = [piece], [0]
            self.got, self.z_offsets = [], []
            self.step()

    def step(self):
        bit = self.bits.pop(0)
        sent = self.held[0]
        self.got.append(swap(sent, "row", self.lay.R, bit))
        self.z_offsets += [o ^ bit for o in self.held_offsets]
        self.held_offsets = self.held_offsets + [o ^ bit for o in self.held_offsets]

    def double(self, after):
        token = after[0]
        while self.bits:
            self.held[0], token = join([self.held[0], self.got[-1]], (token, *after[1:]), self.name + "_double")
            self.step()
        return token

    def spread(self, after):
        lay = self.lay
        self.others, token = join(self.got, after, self.name + "_join")
        self.size = self.others.shape[self.axis]
        self.pieces = [(self.others, 0, 0, self.size)]
        for i in range(min(2, len(lay.split_bits))):
            self.pieces.append((swap(self.others, "dp", lay.Q, lay.split_bits[i]), 1 << i, 0, self.size))
        return token

    def forward(self, after):
        lay, half = self.lay, self.size // 2
        if len(lay.split_bits) < 2:
            return after[0]
        (left, right), token = cut(
            lay, [self.pieces[1][0], self.pieces[2][0]], self.axis, after, self.name
        )
        self.pieces.append((swap(left, "dp", lay.Q, lay.split_bits[1]), 3, 0, half))
        self.pieces.append((swap(right, "dp", lay.Q, lay.split_bits[0]), 3, half, half))
        for i, bit in list(enumerate(lay.split_bits))[2:]:
            self.pieces += [(swap(a, "dp", lay.Q, bit), q | 1 << i, f, n) for a, q, f, n in self.pieces]
        return token

    def sources(self, ids, refs, first=0):
        at = 0
        for _, qo, begin, size in self.pieces:
            if begin + size <= first:
                continue
            for k, zo in enumerate(self.z_offsets):
                yield refs[at].at[k], begin, size, ids[1] ^ qo, ids[0] ^ zo
            at += 1

    def arrays(self, first=0):
        return [a for a, _, begin, size in self.pieces if begin + size > first]


class Weight:
    def __init__(self, gathered, block, dims, pairs, first=0):
        self.block, self.dims, self.pairs = block, dims, pairs
        arrays = gathered.arrays(first)
        self.operands = [(a, anywhere()) for a in arrays] + [(block, anywhere())]
        self.n = len(self.operands)

        class Fake:
            def __getitem__(self, i):
                return self

            @property
            def at(self):
                return self

        fake = Fake()
        copies_n = len(list(pairs([1, 0], [fake] * self.n, fake)))
        self.scratch = [pltpu.VMEM(dims, BF), pltpu.SemaphoreType.DMA((copies_n,))]

    def copies(self, ids, refs, target, sems):
        return [
            pltpu.make_async_copy(a, b, sems.at[i])
            for i, (a, b) in enumerate(self.pairs(ids, refs, target))
        ]


def start_all(copies):
    for copy in copies:
        copy.start()


def wait_all(copies):
    for copy in copies:
        copy.wait()


def aligned(value, multiple):
    return value * multiple if isinstance(value, int) else pl.multiple_of(value * multiple, multiple)


def joint_weight_of(gathered, block):
    lay = gathered.lay
    width = block.shape[1]

    def pairs(ids, refs, target):
        for source, first, size, q, z in gathered.sources(ids, refs):
            n = min(first + size, width) - first
            rows = pl.ds(aligned(z * lay.s + q, lay.piece), lay.piece)
            yield source.at[:, :n], target.at[rows, first : first + n]
        yield refs[-1], target.at[pl.ds(aligned(ids[0], lay.block), lay.block), :]

    return Weight(gathered, block, (D, width), pairs)


def output_weight_of(gathered, block, column):
    lay = gathered.lay
    rows = block.shape[0]
    per = rows // lay.s

    def pairs(ids, refs, target):
        for source, first, _, q, z in gathered.sources(ids, refs, column):
            for b in range(per // lay.piece):
                at = column + b * lay.block - first
                yield (
                    source.at[:, at : at + lay.block],
                    target.at[
                        pl.ds(aligned(q * (per // lay.piece) + b, lay.piece), lay.piece),
                        pl.ds(aligned(z, lay.block), lay.block),
                    ],
                )
        yield refs[-1], target.at[:, pl.ds(aligned(ids[0], lay.block), lay.block)]

    return Weight(gathered, block, (rows, D), pairs, column)


def up_weight_of(gathered, block):
    lay = gathered.lay

    def pairs(ids, refs, target):
        for source, first, size, q, z in gathered.sources(ids, refs):
            rows = pl.ds(aligned(z * lay.s + q, lay.piece), lay.piece)
            yield source, target.at[rows, first : first + size]
        yield refs[-1], target.at[pl.ds(aligned(ids[0], lay.block), lay.block), :]

    return Weight(gathered, block, (D, block.shape[1]), pairs)


def down_weight_of(gathered, block):
    lay = gathered.lay
    rows = block.shape[0]
    per = rows // lay.s

    def pairs(ids, refs, target):
        for source, first, size, q, z in gathered.sources(ids, refs):
            row = aligned(q * (per // size) + first // size, size)
            yield source, target.at[pl.ds(row, size), pl.ds(aligned(z, lay.block), lay.block)]
        yield refs[-1], target.at[:, pl.ds(aligned(ids[0], lay.block), lay.block)]

    return Weight(gathered, block, (rows, D), pairs)


def store_piece(ids, keep, send, bit, q, value):
    spot = ((q >> (bit + 1)) << bit) + (q & ((1 << bit) - 1))
    mine = ((ids[1] >> bit) & 1) == ((q >> bit) & 1)
    pl.when(mine)(lambda: keep.__setitem__(spot, value))
    pl.when(jnp.logical_not(mine))(lambda: send.__setitem__(spot, value))


def small_chunks(refs):
    two, joint_a, joint_b, up, first = refs
    for row in range(4):
        yield from (two[row : row + 1, i : i + HDIM] for i in range(0, HALF, HDIM))
    for ref in (joint_a, joint_b):
        for head in range(ref.shape[0]):
            yield from (ref[head, :, i : i + HDIM] for i in range(0, ref.shape[2], HDIM))
    yield from (up[:, i : i + HDIM] for i in range(0, up.shape[1], HDIM))
    for begin in (0, HALF):
        for row in range(2):
            yield from (first[row : row + 1, i : i + HDIM] for i in range(begin, begin + HALF, HDIM))


def weight_grad(lay, ids, parts, orders, name, smalls, after=()):
    ins, widths = [(ids, smem())], []
    for sides in parts:
        for left, right in sides:
            ins.append((left, pl.BlockSpec((LEN, lay.block), lambda z: (0, z))))
            ins.append((right, whole(*right.shape)))
        widths.append(sum(right.shape[1] for _, right in sides))
    widths[0] += HDIM
    ins.extend((v, whole(*v.shape)) for v in smalls)
    n_out = 2 * len(orders)

    def kernel(ids, *refs):
        ins, outs, rows_ref = list(refs[: -n_out - 1]), refs[-n_out - 1 : -1], refs[-1]
        small_refs = ins[-len(smalls) :]

        def fill():
            rows_ref[...] = jnp.zeros_like(rows_ref)
            for i, chunk in enumerate(small_chunks(small_refs)):
                rows_ref[i : i + 1, :] = chunk

        pl.when(pl.program_id(0) == 0)(fill)
        for i, order in enumerate(orders):
            values = []
            for _ in parts[i]:
                left, right = ins.pop(0), ins.pop(0)
                values.append(dot(left[...], right[...], TN).astype(BF))
            if i == 0:
                values.append(rows_ref[...].astype(BF))
            block = jnp.concatenate(values, axis=1)
            for q in range(lay.s):
                part = block[q * lay.piece : (q + 1) * lay.piece]
                store_piece(ids, outs[2 * i], outs[2 * i + 1], order[0], q, part)

    outs = []
    for width in widths:
        out = pl.BlockSpec((lay.s // 2, lay.piece, width), lambda z: (z, 0, 0))
        outs += [(shape((lay.R * lay.s // 2, lay.piece, width)), out)] * 2
    return call(
        kernel, name, ins, outs, grid=(lay.R,), scratch=[pltpu.VMEM((lay.block, HDIM), F32)], after=after
    )


def output_grad(lay, ids, left, rights, orders, name, after):
    width = rights[0].shape[1]
    n_out = 2 * len(orders)
    if len(rights) != len(orders):
        return halves_grad(lay, ids, left, jnp.concatenate(rights, axis=1), orders, name, after)

    def kernel(ids, left_ref, *refs):
        for i, order in enumerate(orders):
            block = dot(left_ref[...], refs[i][...], TN).astype(BF)
            keep, send = refs[len(rights) + 2 * i : len(rights) + 2 * i + 2]
            for q in range(lay.s):
                store_piece(ids, keep, send, order[0], q, block[q * lay.piece : (q + 1) * lay.piece])

    out = pl.BlockSpec((lay.s // 2, lay.piece, width), lambda z: (z, 0, 0))
    return call(
        kernel,
        name,
        [(ids, smem()), (left, pl.BlockSpec((LEN, lay.block), lambda z: (0, z)))]
        + [(r, whole(*r.shape)) for r in rights],
        [(shape((lay.R * lay.s // 2, lay.piece, width)), out)] * n_out,
        grid=(lay.R,),
        after=after,
        mib=12,
    )


def halves_grad(lay, ids, left, right, orders, name, after):
    width = right.shape[1] // len(orders)
    n_out = 2 * len(orders)

    def kernel(ids, left_ref, right_ref, *outs):
        block = dot(left_ref[...], right_ref[...], TN).astype(BF)
        for i, order in enumerate(orders):
            for q in range(lay.s):
                keep, send, bit = outs[2 * i], outs[2 * i + 1], order[0]
                part = block[q * lay.piece : (q + 1) * lay.piece, i * width : (i + 1) * width]
                store_piece(ids, keep, send, bit, q, part)

    out = pl.BlockSpec((lay.s // 2, lay.piece, width), lambda z: (z, 0, 0))
    return call(
        kernel,
        name,
        [(ids, smem()), (left, pl.BlockSpec((LEN, lay.block), lambda z: (0, z))), (right, whole(*right.shape))],
        [(shape((lay.R * lay.s // 2, lay.piece, width)), out)] * n_out,
        grid=(lay.R,),
        after=after,
    )


class Reduction:
    def __init__(self, lay, ids, orders, parts):
        self.lay, self.ids, self.orders, self.step = lay, ids, orders, 0
        k = len(lay.split_bits)
        self.left = [sorted(set(range(k)) - {order[0]}, reverse=True) for order in orders]
        self.send(parts)

    def send(self, parts):
        self.keep, self.got = list(parts[0::2]), []
        for order, part in zip(self.orders, parts[1::2]):
            self.got.append(swap(part, "dp", self.lay.Q, self.lay.split_bits[order[self.step]]))
        self.step += 1

    def advance(self, after, name, passing=(), joined=()):
        lay, n = self.lay, len(self.orders)
        bits = [order[self.step] for order in self.orders]
        ins, outs = [(self.ids, smem())], []
        reds = [self, *joined]
        for i, bit in enumerate(bits):
            groups = lay.R * 2 ** self.left[i].index(bit)
            rows = 2 ** (len(self.left[i]) - 1 - self.left[i].index(bit)) * lay.piece
            width = sum(r.keep[i].shape[-1] for r in reds)
            for value in [v for r in reds for v in (r.keep[i], r.got[i])]:
                columns = value.shape[-1]
                ins.append(
                    (value.reshape(groups, 2, rows, columns), pl.BlockSpec((1, 2, rows, columns), lambda g: (g, 0, 0, 0)))
                )
            outs += [(shape((groups, rows, width)), pl.BlockSpec((1, rows, width), lambda g: (g, 0, 0)))] * 2

        def kernel(ids, *refs):
            ins, outs = list(refs[: 2 * n * len(reds)]), refs[2 * n * len(reds) :]
            for i, bit in enumerate(bits):
                mine = (ids[1] >> bit) & 1
                first = 0
                for _ in reds:
                    a, b = ins.pop(0), ins.pop(0)
                    last = first + a.shape[3]
                    for target, which in ((outs[2 * i], mine), (outs[2 * i + 1], 1 - mine)):
                        target[0, :, first:last] = (a[0, which].astype(F32) + b[0, which].astype(F32)).astype(BF)
                    first = last

        parts, token = call(kernel, name, ins, outs, grid=(groups,), after=after, passing=passing)
        self.left = [[b for b in left if b != bit] for left, bit in zip(self.left, bits)]
        self.send(parts[: 2 * n])
        return parts[2 * n :], token


def first_rows(reduction, after, name, passing=()):
    lay, ids, n = reduction.lay, reduction.ids, len(reduction.orders)
    ins = [(ids, smem())]
    widths = [keep.shape[-1] for keep in reduction.keep]
    starts = [sum(widths[:i]) for i in range(n)]
    columns = sum(widths)
    for i, width in enumerate(widths):
        for value in (reduction.keep[i], reduction.got[i]):
            value = value.reshape(lay.R // 2, 2, lay.piece, width)
            ins.append((value, pl.BlockSpec((1, 2, lay.piece, width), lambda g: (g, 0, 0, 0))))
    out = pl.BlockSpec((1, lay.piece, columns), lambda g: (g, 0, 0))

    def kernel(ids, *refs):
        ins, (keep, send) = refs[:-2], refs[-2:]
        mine = ids[0] & 1
        for target, bit in ((keep, mine), (send, 1 - mine)):
            for i in range(n):
                a, b = ins[2 * i], ins[2 * i + 1]
                total = (a[0, bit].astype(F32) + b[0, bit].astype(F32)).astype(BF)
                target[0, :, starts[i] : starts[i] + widths[i]] = total

    kind = shape((lay.R // 2, lay.piece, columns))
    (keep, send, *passed), token = call(
        kernel, name, ins, [(kind, out)] * 2, grid=(lay.R // 2,), after=after, passing=passing
    )
    return ((keep, swap(send, "row", lay.R, 1)), *passed), token


def next_rows(lay, ids, pair, after, name):
    token = after[0]
    for i, bit in list(enumerate(lay.row_bits))[1:]:
        keep, got = pair
        groups = keep.shape[0] // 2
        columns = keep.shape[-1]
        ins = [(ids, smem())]
        for value in pair:
            value = value.reshape(groups, 2, lay.piece, columns)
            ins.append((value, pl.BlockSpec((1, 2, lay.piece, columns), lambda g: (g, 0, 0, 0))))
        out = pl.BlockSpec((1, lay.piece, columns), lambda g: (g, 0, 0))

        def kernel(ids, a, b, keep, send, i=i):
            mine = (ids[0] >> i) & 1
            for target, which in ((keep, mine), (send, 1 - mine)):
                target[0] = (a[0, which].astype(F32) + b[0, which].astype(F32)).astype(BF)

        kind = shape((groups, lay.piece, columns))
        (keep, send), token = call(kernel, name, ins, [(kind, out)] * 2, grid=(groups,), after=(token, *after[1:]))
        pair = (keep, swap(send, "row", lay.R, bit))
    return pair, token


def row_total(lay, pair, after, name, ready=(), passing=()):
    width = pair[0].shape[-1]
    columns = width + sum(r.shape[1] for r in ready)

    def kernel(*refs):
        (*others, a, b), out = refs[:-1], refs[-1]
        column = 0
        for ref in others:
            out[:, column : column + ref.shape[1]] = ref[...]
            column += ref.shape[1]
        out[:, column:] = (a[...].astype(F32) + b[...].astype(F32)).astype(BF)

    (total, *passed), token = call(
        kernel,
        name,
        [(v, vmem()) for v in ready] + [(v.reshape(lay.piece, width), vmem()) for v in pair],
        [(shape((lay.piece, columns)), vmem())],
        after=after,
        passing=passing,
    )
    return (total, *passed), token


def rest_sum(lay, total):
    for bit in lay.rest_bits:
        total = (total.astype(F32) + swap(total, "dp", lay.Q, bit).astype(F32)).astype(BF)
    return total


def spread(lay, total):
    got = [total]
    for offset in range(1, lay.s):
        mask = sum(bit for i, bit in enumerate(lay.split_bits) if (offset >> i) & 1)
        got.append(swap(total, "dp", lay.Q, mask))
    return got


class Spread:
    def __init__(self, lay, total):
        self.lay = lay
        self.pieces = {0: total}
        for i in range(min(2, len(lay.split_bits))):
            self.pieces[1 << i] = swap(total, "dp", lay.Q, lay.split_bits[i])

    def forward(self, after, name):
        lay, token = self.lay, after[0]
        if len(lay.split_bits) >= 2:
            (left, right), token = cut(lay, [self.pieces[1][None], self.pieces[2][None]], 2, after, name)
            self.pieces[3] = (
                swap(left[0], "dp", lay.Q, lay.split_bits[1]),
                swap(right[0], "dp", lay.Q, lay.split_bits[0]),
            )
        for i, bit in list(enumerate(lay.split_bits))[2:]:
            for q, piece in list(self.pieces.items()):
                self.pieces[q | 1 << i] = jax.tree.map(lambda v: swap(v, "dp", lay.Q, bit), piece)
        return token

    def all(self):
        return [self.pieces[q] for q in range(self.lay.s)]


def finish(lay, ids, pieces, plan, name, after=(), small=None):
    outs = []
    for spans, transposed in plan:
        n = sum(c for _, c in spans)
        outs.append((shape((n, lay.block) if transposed else (lay.block, n), F32), vmem()))
    if small:
        outs += [(shape((rows, HDIM), F32), vmem()) for rows in small[1]]
    arrays = jax.tree.leaves(pieces)
    n_in = len(arrays)
    widest = max([HDIM] + [sum(c for _, c in spans) for spans, t in plan if t])

    def kernel(ids, *refs):
        ins, results, scratch = list(refs[:n_in]), refs[n_in:-1], refs[-1]
        values = []
        for piece in pieces:
            if isinstance(piece, tuple):
                values.append(jnp.concatenate([ins.pop(0)[...], ins.pop(0)[...]], axis=1))
            else:
                values.append(ins.pop(0))
        for (spans, transposed), result in zip(plan, results):
            column = 0
            for first, n in spans:
                for offset in range(lay.s):
                    rows = pl.ds(aligned(ids[1] ^ offset, lay.piece), lay.piece)
                    value = values[offset][:, first : first + n].astype(F32)
                    if transposed:
                        scratch[rows, column : column + n] = value
                    else:
                        result[rows, column : column + n] = value
                column += n
            if transposed:
                result[...] = scratch[:, :column].T
        if small:
            for offset in range(lay.s):
                rows = pl.ds(aligned(ids[1] ^ offset, lay.piece), lay.piece)
                scratch[rows, :HDIM] = values[offset][:, small[0] : small[0] + HDIM].astype(F32)
            row = 0
            for count, result in zip(small[1], results[len(plan) :]):
                result[...] = scratch[row : row + count, :HDIM]
                row += count

    return call(
        kernel,
        name,
        [(ids, smem())] + [(p, vmem()) for p in arrays],
        outs,
        scratch=[pltpu.VMEM((lay.block, widest), F32)],
        after=after,
        mib=12,
    )


def both(own, other):
    return jnp.concatenate([own, other], axis=1)


def row_stats(values):
    average = jnp.mean(values, axis=1, keepdims=True)
    square = jnp.mean(values * values, axis=1, keepdims=True)
    return average, lax.rsqrt(square - average * average + EPSILON)


def norm_grad(gradient, centered, factor, gain):
    scaled = gradient * gain
    first = jnp.mean(scaled, axis=1, keepdims=True)
    second = jnp.mean(scaled * centered, axis=1, keepdims=True)
    return factor * (scaled - first - centered * second)


V_GAIN1, V_SHIFT1, V_GAIN2, V_SHIFT2, V_OBIAS = range(5)


def pair_row(own_ref, other_ref, i):
    return both(own_ref[i : i + 1, :], other_ref[i : i + 1, :])


def branch_sum(own, other):
    return own[...].astype(F32) + both(other[:, HALF:], other[:, :HALF]).astype(F32)


def pair_up(pairs, after):
    def kernel(*refs):
        n = len(pairs)
        for i in range(n):
            refs[2 * n + i][:, :HALF] = refs[2 * i][...]
            refs[2 * n + i][:, HALF:] = refs[2 * i + 1][...]

    return call(
        kernel,
        "pair_up",
        [(v, row_tile(HALF)) for pair in pairs for v in pair],
        [(shape((LEN, D)), row_tile(D))] * len(pairs),
        grid=ROW_GRID,
        after=after,
    )


def first_norm_project(ids, x, vecs, bias, joint, after):
    width = bias.shape[1]

    def kernel(ids, x_ref, vo, vt, bias, *refs):
        pieces, full, qkv, weight, sems = refs[: joint.n], *refs[joint.n :]
        copies = joint.copies(ids, pieces, weight, sems)
        first = pl.program_id(0) == 0
        pl.when(first)(lambda: start_all(copies))
        values = x_ref[...].astype(F32)
        average, factor = row_stats(values)
        normed = (values - average) * factor * pair_row(vo, vt, V_GAIN1) + pair_row(vo, vt, V_SHIFT1)
        low = normed.astype(BF)
        full[...] = low
        pl.when(first)(lambda: wait_all(copies))
        qkv[...] = (dot(low, weight[...]) + bias[...]).astype(BF)

    return call(
        kernel,
        "first_norm_project",
        [(ids, smem()), (x, row_tile(D)), *[(v, whole(8, HALF)) for v in vecs], (bias, whole(1, width))]
        + joint.operands,
        [(hbm((LEN, D)), row_tile(D)), (shape((LEN, width)), row_tile(width))],
        grid=ROW_GRID,
        scratch=joint.scratch,
        after=after,
    )


def visible_mask(lo, rows, queries, prefix):
    key_id = lax.broadcasted_iota(jnp.int32, (rows, queries), 0) + lo
    query_id = lax.broadcasted_iota(jnp.int32, (rows, queries), 1) + lo
    return (key_id <= query_id) | (key_id < prefix)


def attend(prefix_ref, qkv_ref, out_ref, log_ref):
    bq = 512
    prefix_end = prefix_ref[0]
    for h in range(log_ref.shape[0]):
        base = h * 3 * HDIM
        keys = qkv_ref[:, base + HDIM : base + 2 * HDIM]
        values_t = qkv_ref[:, base + 2 * HDIM : base + 3 * HDIM].T
        for lo in range(0, LEN, bq):
            n = max(MAX_PREFIX, lo + bq)
            query = qkv_ref[lo : lo + bq, base : base + HDIM]
            scores = dot(keys[:n], query, NT)
            tail = jnp.where(visible_mask(lo, n - lo, bq, prefix_end), scores[lo:], NEGATIVE)
            scores = tail if lo == 0 else jnp.concatenate([scores[:lo], tail], axis=0)
            top = jnp.max(scores, axis=0, keepdims=True) * (SCALE * LOG2E)
            weights = jnp.exp2(scores * (SCALE * LOG2E) - top)
            total = jnp.sum(weights, axis=0, keepdims=True)
            mixed = dot(values_t[:, :n], weights.astype(BF)) * (1.0 / total)
            out_ref[lo : lo + bq, h * HDIM : (h + 1) * HDIM] = mixed.T.astype(BF)
            log_ref[h, :, lo : lo + bq] = top + jnp.log2(total)


def attention_first(prefix, qkv, heads, after):
    return call(
        attend,
        "attention_first",
        [(prefix, smem()), (qkv, pl.BlockSpec((LEN, 3 * HDIM * heads), lambda i: (0, 0)))],
        [
            (shape((LEN, HDIM * heads)), whole(LEN, HDIM * heads)),
            (shape((heads, 1, LEN), F32), whole(heads, 1, LEN)),
        ],
        grid=(1,),
        after=after,
    )


def attention_second(ids, prefix, qkv, heads, attended_first, output, after):
    width = HDIM * heads

    def kernel(ids, prefix_ref, qkv_ref, first_ref, *refs):
        pieces, (out_ref, log_ref, branch, weight, sems) = refs[: output.n], refs[output.n :]
        copies = output.copies(ids, pieces, weight, sems)
        start_all(copies)
        attend(prefix_ref, qkv_ref, out_ref, log_ref)
        wait_all(copies)
        for lo in range(0, LEN, TILE):
            rows = slice(lo, lo + TILE)
            branch[rows, :] = dot(both(first_ref[rows, :], out_ref[rows, :]), weight[...]).astype(BF)

    return call(
        kernel,
        "attention_second",
        [(ids, smem()), (prefix, smem()), (qkv, pl.BlockSpec((LEN, 3 * HDIM * heads), lambda i: (0, 1))),
         (attended_first, whole(LEN, width))]
        + output.operands,
        [
            (shape((LEN, width)), whole(LEN, width)),
            (shape((heads, 1, LEN), F32), whole(heads, 1, LEN)),
            (shape((LEN, D)), whole(LEN, D)),
        ],
        grid=(1,),
        scratch=output.scratch,
        after=after,
    )


def second_norm_up(ids, x, parts, vecs, bias, up, after):
    width = bias.shape[1]

    def kernel(ids, x_ref, po, pt, vo, vt, bias, *refs):
        pieces = refs[: up.n]
        residual, centered, factor_ref, full, active, slope, weight, sems = refs[up.n :]
        copies = up.copies(ids, pieces, weight, sems)
        first = pl.program_id(0) == 0
        pl.when(first)(lambda: start_all(copies))
        res = x_ref[...].astype(F32) + (branch_sum(po, pt) + pair_row(vo, vt, V_OBIAS))
        residual[...] = res[:, :HALF]
        average, factor = row_stats(res)
        cent = (res - average) * factor
        centered[...] = cent.astype(BF)
        factor_ref[...] = factor
        low = (cent * pair_row(vo, vt, V_GAIN2) + pair_row(vo, vt, V_SHIFT2)).astype(BF)
        full[...] = low
        pl.when(first)(lambda: wait_all(copies))
        hidden = dot(low, weight[...]) + bias[...]
        bell = jnp.exp(-0.5 * hidden * hidden) * (1.0 / math.sqrt(2.0 * math.pi))
        phi = 0.5 * (1.0 + lax.erf(hidden * 2.0**-0.5))
        active[...] = (hidden * phi).astype(BF)
        slope[...] = (phi + hidden * bell).astype(BF)

    return call(
        kernel,
        "second_norm_up",
        [(ids, smem()), (x, row_tile(D)), *[(p, row_tile(D)) for p in parts], *[(v, whole(8, HALF)) for v in vecs],
         (bias, whole(1, width))]
        + up.operands,
        [
            (hbm((LEN, HALF), F32), row_tile(HALF)),
            (hbm((LEN, D)), row_tile(D)),
            (hbm((LEN, 1), F32), row_tile(1)),
            (hbm((LEN, D)), row_tile(D)),
            (shape((LEN, width)), row_tile(width)),
            (shape((LEN, width)), row_tile(width)),
        ],
        grid=ROW_GRID,
        scratch=up.scratch,
        after=after,
    )


def hidden_backward(ids, cot, slope, up, down, after):
    width = slope.shape[1]

    def kernel(ids, cot_ref, slope_ref, *refs):
        up_pieces, refs = refs[: up.n], refs[up.n :]
        down_pieces, refs = refs[: down.n], refs[down.n :]
        hidden_grad, partial, bias_grad, up_full, up_sems, down_full, down_sems = refs
        down_copies = down.copies(ids, down_pieces, down_full, down_sems)
        up_copies = up.copies(ids, up_pieces, up_full, up_sems)
        first = pl.program_id(0) == 0

        def begin():
            start_all(down_copies)
            start_all(up_copies)
            bias_grad[...] = jnp.zeros_like(bias_grad)
            wait_all(down_copies)

        pl.when(first)(begin)
        grad = dot(cot_ref[...], down_full[...], NT) * slope_ref[...].astype(F32)
        low = grad.astype(BF)
        hidden_grad[...] = low
        bias_grad[...] += jnp.sum(low.astype(F32), axis=0, keepdims=True)
        pl.when(first)(lambda: wait_all(up_copies))
        partial[...] = dot(low, up_full[...], NT).astype(BF)

    return call(
        kernel,
        "hidden_backward",
        [(ids, smem()), (cot, row_tile(D)), (slope, row_tile(width))] + up.operands + down.operands,
        [(hbm((LEN, width)), row_tile(width)), (shape((LEN, D)), row_tile(D)), (shape((1, width), F32), whole(1, width))],
        grid=ROW_GRID,
        scratch=up.scratch + down.scratch,
        after=after,
    )


def second_norm_backward(ids, cot, parts, centered, factor, vecs, output, after):
    width = output.dims[0]

    def kernel(ids, cot_ref, po, pt, cent_ref, factor_ref, vo, vt, *refs):
        pieces, (branch, res_grad, att_grad, sums_ref, weight, sems) = refs[: output.n], refs[output.n :]
        copies = output.copies(ids, pieces, weight, sems)
        first = pl.program_id(0) == 0

        def begin():
            start_all(copies)
            sums_ref[...] = jnp.zeros_like(sums_ref)

        pl.when(first)(begin)
        grad = branch_sum(po, pt)
        cent = cent_ref[...].astype(F32)
        cot = cot_ref[...].astype(F32)
        total = cot + norm_grad(grad, cent, factor_ref[...], pair_row(vo, vt, V_GAIN2))
        low = total.astype(BF)
        branch[...] = low
        res_grad[...] = total[:, :HALF]
        news = (grad[:, :HALF] * cent[:, :HALF], grad[:, :HALF], low[:, :HALF].astype(F32), cot[:, :HALF])
        for i, value in enumerate(news):
            sums_ref[i : i + 1, :] += jnp.sum(value, axis=0, keepdims=True)
        pl.when(first)(lambda: wait_all(copies))
        att_grad[...] = dot(low, weight[...], NT).astype(BF)

    return call(
        kernel,
        "second_norm_backward",
        [(ids, smem()), (cot, row_tile(D)), *[(p, row_tile(D)) for p in parts], (centered, row_tile(D)),
         (factor, row_tile(1)), *[(v, whole(8, HALF)) for v in vecs]]
        + output.operands,
        [
            (shape((LEN, D)), row_tile(D)),
            (shape((LEN, HALF), F32), row_tile(HALF)),
            (shape((LEN, width)), row_tile(width)),
            (shape((4, HALF), F32), whole(4, HALF)),
        ],
        grid=ROW_GRID,
        scratch=output.scratch,
        after=after,
    )


def attention_backward(prefix, qkv, grads, logs, attended, first_head, heads, after):
    bq = 256

    def kernel(prefix_ref, qkv_ref, grad_ref, log_ref, att_ref, out_ref, sums_ref, key_sum, value_sum):
        prefix_end = prefix_ref[0]
        keys = qkv_ref[:, HDIM : 2 * HDIM]
        values = qkv_ref[:, 2 * HDIM : 3 * HDIM]
        keys_t = keys.T
        query_total = jnp.zeros((1, HDIM), F32)
        for lo in reversed(range(0, LEN, bq)):
            n = max(MAX_PREFIX, lo + bq)
            query = qkv_ref[lo : lo + bq, 0:HDIM]
            grad = grad_ref[lo : lo + bq, :]
            scores = dot(keys[:n], query, NT) * (SCALE * LOG2E)
            weights = jnp.exp2(scores - log_ref[0, :, lo : lo + bq])
            tail = jnp.where(visible_mask(lo, n - lo, bq, prefix_end), weights[lo:], 0.0)
            weights = tail if lo == 0 else jnp.concatenate([weights[:lo], tail], axis=0)
            weight_grad_t = dot(values[:n], grad, NT)
            mixed = grad.astype(F32) * att_ref[lo : lo + bq, :].astype(F32)
            delta = jnp.sum(mixed.T, axis=0, keepdims=True)
            score_grad = (weights * (weight_grad_t - delta)).astype(BF)
            value_part = dot(weights.astype(BF), grad)
            key_part = dot(score_grad, query)
            if lo + bq == LEN:
                value_sum[...] = value_part
                key_sum[...] = key_part
            else:
                value_sum[:n, :] += value_part
                key_sum[:n, :] += key_part
            query_part = (dot(keys_t[:, :n], score_grad).T * SCALE).astype(BF)
            out_ref[lo : lo + bq, 0:HDIM] = query_part
            query_total = query_total + jnp.sum(query_part.astype(F32), axis=0, keepdims=True)
        out_ref[:, HDIM : 2 * HDIM] = (key_sum[...] * SCALE).astype(BF)
        value_low = value_sum[...].astype(BF)
        out_ref[:, 2 * HDIM : 3 * HDIM] = value_low
        sums_ref[0] = both(query_total, jnp.sum(value_low.astype(F32), axis=0, keepdims=True))

    return call(
        kernel,
        "attention_backward",
        [
            (prefix, smem()),
            (qkv, pl.BlockSpec((LEN, 3 * HDIM), lambda h: (0, h + first_head))),
            (grads, pl.BlockSpec((LEN, HDIM), lambda h: (0, h + first_head))),
            (logs, pl.BlockSpec((1, 1, LEN), lambda h: (h, 0, 0))),
            (attended, pl.BlockSpec((LEN, HDIM), lambda h: (0, h))),
        ],
        [
            (shape((LEN, 3 * HDIM * heads)), pl.BlockSpec((LEN, 3 * HDIM), lambda h: (0, h))),
            (shape((heads, 1, 2 * HDIM), F32), pl.BlockSpec((1, 1, 2 * HDIM), lambda h: (h, 0, 0))),
        ],
        grid=(heads,),
        scratch=[pltpu.VMEM((LEN, HDIM), F32), pltpu.VMEM((LEN, HDIM), F32)],
        after=after,
    )


def project_backward(ids, grads, x, vecs, joint, after):
    widths = [g.shape[1] for g in grads]

    def kernel(ids, x_ref, vo, vt, *refs):
        grad_refs, refs = refs[: len(grads)], refs[len(grads) :]
        pieces, (own, other, sums, columns, weight, sems) = refs[: joint.n], refs[joint.n :]
        copies = joint.copies(ids, pieces, weight, sems)
        first = pl.program_id(0) == 0

        def begin():
            start_all(copies)
            columns[...] = jnp.zeros_like(columns)

        pl.when(first)(begin)
        values = x_ref[...].astype(F32)
        average, factor = row_stats(values)
        pl.when(first)(lambda: wait_all(copies))
        total, column = 0.0, 0
        for ref, width in zip(grad_refs, widths):
            total = total + dot(ref[...], weight[:, column : column + width], NT)
            column += width
        own[...] = total[:, :HALF].astype(BF)
        other[:, :HALF] = total[:, HALF:].astype(BF)
        gain = pair_row(vo, vt, V_GAIN1)
        product = total * ((values - average) * factor)
        columns[0:1, :] += jnp.sum(product, axis=0, keepdims=True)
        columns[1:2, :] += jnp.sum(total, axis=0, keepdims=True)
        lane = lax.broadcasted_iota(jnp.int32, (TILE, HDIM), 1)
        packed = jnp.zeros((TILE, HDIM), F32)
        parts = jnp.zeros((TILE, HDIM), F32)
        for i, value in enumerate((total * gain, product * gain)):
            row_sum = jnp.sum(value, axis=1, keepdims=True)
            high = row_sum.astype(BF).astype(F32)
            packed = jnp.where(lane == 2 * i, high, jnp.where(lane == 2 * i + 1, row_sum - high, packed))
            parts = jnp.where(lane == i, row_sum, parts)
        other[:, HALF:] = packed.astype(BF)
        sums[...] = parts

    return call(
        kernel,
        "project_backward",
        [(ids, smem()), (x, row_tile(D)), *[(v, whole(8, HALF)) for v in vecs]]
        + [(g, row_tile(g.shape[1])) for g in grads]
        + joint.operands,
        [
            (shape((LEN, HALF)), row_tile(HALF)),
            (shape((LEN, HALF + HDIM)), row_tile(HALF + HDIM)),
            (shape((LEN, HDIM), F32), row_tile(HDIM)),
            (shape((8, D), F32), whole(8, D)),
        ],
        grid=ROW_GRID,
        scratch=joint.scratch,
        after=after,
    )


MOST = LEN // 2


def most_tiles(width):
    return [
        pl.BlockSpec((TILE, width), lambda i: (jnp.minimum(i, MOST // TILE - 1), 0)),
        pl.BlockSpec((TILE, width), lambda i: (jnp.maximum(i - MOST // TILE, 0), 0)),
    ]


def in_most():
    return pl.program_id(0) < MOST // TILE


def down_project(ids, active, down, after):
    def kernel(ids, a_ref, *refs):
        pieces, (own, other, rest, weight, sems) = refs[: down.n], refs[down.n :]
        copies = down.copies(ids, pieces, weight, sems)

        def begin():
            start_all(copies)
            wait_all(copies)

        pl.when(pl.program_id(0) == 0)(begin)
        value = dot(a_ref[...], weight[...]).astype(BF)
        own[...] = value[:, :HALF]
        pl.when(in_most())(lambda: other.__setitem__(..., value[:, HALF:]))
        pl.when(jnp.logical_not(in_most()))(lambda: rest.__setitem__(..., value[:, HALF:]))

    return call(
        kernel,
        "down_project",
        [(ids, smem()), (active, row_tile(active.shape[1]))] + down.operands,
        [(shape((LEN, HALF)), row_tile(HALF))]
        + [(shape((n, HALF)), spec) for n, spec in zip((MOST, LEN - MOST), most_tiles(HALF))],
        grid=ROW_GRID,
        scratch=down.scratch,
        after=after,
    )


def add_output(residual, own, got, bias, after):
    def kernel(res, a, most, rest, bias, out):
        b = jnp.where(in_most(), most[...], rest[...])
        out[...] = (res[...] + (a[...].astype(F32) + b.astype(F32) + bias[...])).astype(BF)

    return call(
        kernel,
        "add_output",
        [(residual, row_tile(HALF)), (own, row_tile(HALF)), *zip(got, most_tiles(HALF)), (bias, whole(1, HALF))],
        [(shape((LEN, HALF)), row_tile(HALF))],
        grid=ROW_GRID,
        after=after,
    )


def first_norm_backward(x, own, other, sums, vecs, res_grad, after):
    def kernel(x_ref, po, pt, so, vo, res_ref, out):
        values = x_ref[...].astype(F32)
        average, factor = row_stats(values)
        cent = (values[:, :HALF] - average) * factor
        grad = po[...].astype(F32) + pt[:, :HALF].astype(F32)
        got = pt[:, HALF:].astype(F32)
        first = (so[:, 0:1] + (got[:, 0:1] + got[:, 1:2])) * (1.0 / D)
        second = (so[:, 1:2] + (got[:, 2:3] + got[:, 3:4])) * (1.0 / D)
        back = factor * (grad * vo[V_GAIN1 : V_GAIN1 + 1, :] - first - cent * second)
        out[...] = (res_ref[...] + back).astype(BF)

    return call(
        kernel,
        "first_norm_backward",
        [(x, row_tile(D)), (own, row_tile(HALF)), (other, row_tile(HALF + HDIM)), (sums, row_tile(HDIM)),
         (vecs[0], whole(8, HALF)), (res_grad, row_tile(HALF))],
        [(shape((LEN, HALF)), row_tile(HALF))],
        grid=ROW_GRID,
        after=after,
    )


def layer(lay, tokens_in, cotangent, prefix_length, first_gain, first_shift, joint_weight, joint_bias,
          output_weight, output_bias, second_gain, second_shift, up_weight, up_bias, down_weight, down_bias):
    heads = joint_bias.shape[0] // (2 * HDIM)
    ids = device_ids(lay)

    j_width, o_rows, ff = joint_weight.shape[1], output_weight.shape[0], down_weight.shape[0]
    per = o_rows // lay.s
    jo_piece = own_pieces(
        ids, [(joint_weight, lay.piece, 0), *[(output_weight, per, b * lay.piece) for b in range(per // lay.piece)]], lay.piece
    )
    jo = Gathered(lay, jo_piece, 2, "joint_pieces", True)

    zero_row = jnp.zeros_like(first_gain)
    vec_own = jnp.stack(
        [first_gain, first_shift, second_gain, second_shift, output_bias, zero_row, zero_row, zero_row]
    )
    vecs = (vec_own, swap_cores(vec_own))
    bias_rows = joint_bias.reshape(heads, 2, HDIM)
    joint_row = jnp.stack([bias_rows[:, 0], jnp.zeros_like(bias_rows[:, 0]), bias_rows[:, 1]], axis=1).reshape(1, -1)
    (x, cot), token = pair_up(
        [(tokens_in, swap_cores(tokens_in)), (cotangent, swap_cores(cotangent))], (*vecs, joint_row)
    )

    token = jo.spread((token,))
    up_piece, up_token = extract(lay, ids, up_weight, lay.piece, (token,))
    up = Gathered(lay, up_piece, 2, "up_pieces", False)
    token = up.double((up_token,))
    token = jo.forward((token,))
    down_piece, down_token = extract(lay, ids, down_weight, ff // lay.s, (token, *up.got))
    down = Gathered(lay, down_piece, 1, "down_pieces", False)
    token = up.spread((token, *jo.arrays()))
    joint_w = joint_weight_of(jo, joint_weight)
    output_w = output_weight_of(jo, output_weight, j_width)

    (full_one, qkv), token = first_norm_project(
        ids, x, vecs, joint_row, joint_w, (up.others, down_token)
    )
    pair = heads // 2
    token = down.double((token,))
    (attended_a, logs_a), token = attention_first(prefix_length, qkv, pair, (token,))
    token = up.forward((token,))
    up_w = up_weight_of(up, up_weight)
    (attended_b, logs_b, branch), token = attention_second(
        ids, prefix_length, qkv, pair, attended_a, output_w, (token,)
    )
    token = down.spread((token,))
    (branch,), token = hold([branch], (token, *up.arrays()), "hold_branch")
    (residual, centered, factor, full_two, active, slope), token = second_norm_up(
        ids, x, (branch, swap_cores(branch)), vecs, up_bias.reshape(1, -1), up_w, (token,)
    )
    token = down.forward((token,))
    down_w = down_weight_of(down, down_weight)
    both_orders = [lay.order_a, lay.order_b]
    later_steps = range(len(lay.split_bits) - 1)
    down_parts, token = halves_grad(lay, ids, cot, active, both_orders, "down_grad", (token,))
    down_parts, token = hold(down_parts, (token, *down.arrays()), "hold_down")
    down_red = Reduction(lay, ids, both_orders, down_parts)

    (hidden_grad, norm_part, up_bias_grad), token = hidden_backward(ids, cot, slope, up_w, down_w, (token,))
    passed, token = halves_grad(lay, ids, full_two, hidden_grad, both_orders, "up_grad", (token,))
    passed = [norm_part, *passed]
    for _ in later_steps:
        passed, token = down_red.advance((token,), "down_sum", passed)
    norm_part, *up_parts = passed
    up_red = Reduction(lay, ids, both_orders, up_parts)
    norm_parts = (norm_part, swap_cores(norm_part))
    (branch_grad, res_grad, att_grad, sums_two), token = second_norm_backward(
        ids, cot, norm_parts, centered, factor, vecs, output_w, (token,)
    )
    (qkv_grad_a, joint_sums_a), token = attention_backward(
        prefix_length, qkv, att_grad, logs_a, attended_a, 0, pair, (token,)
    )
    (qkv_grad_b, joint_sums_b), token = attention_backward(
        prefix_length, qkv, att_grad, logs_b, attended_b, pair, pair, (token,)
    )
    (down_rows,), token = first_rows(down_red, (token,), "down_rows")
    output_parts, token = output_grad(lay, ids, branch_grad, (attended_a, attended_b), both_orders, "output_grad", (token,))
    output_red = Reduction(lay, ids, both_orders, output_parts)
    (first_own, first_send, row_sums, first_sums), token = project_backward(
        ids, [qkv_grad_a, qkv_grad_b], x, vecs, joint_w, (token,)
    )
    down_rows, token = next_rows(lay, ids, down_rows, (token,), "down_rows_2")
    for i in later_steps:
        _, token = up_red.advance((token,), "up_sum", (), (output_red,) if i == 0 else ())
    joint_parts, token = weight_grad(
        lay,
        ids,
        [[(full_one, qkv_grad_a)], [(full_one, qkv_grad_b)]],
        both_orders,
        "joint_grad",
        (sums_two, joint_sums_a, joint_sums_b, up_bias_grad, first_sums),
        (token,),
    )
    joint_red = Reduction(lay, ids, both_orders, joint_parts)
    (down_own, *down_send), token = down_project(ids, active, down_w, (token,))
    (down_total,), token = row_total(lay, down_rows, (token,), "down_total")
    (up_rows, *down_send), token = first_rows(up_red, (token,), "up_rows", down_send)
    (layer_out,), token = add_output(
        residual, down_own, [swap_cores(p) for p in down_send], down_bias.reshape(1, -1), (token,)
    )
    up_rows, token = next_rows(lay, ids, up_rows, (token,), "up_rows_2")
    passed = [first_send]
    for _ in later_steps:
        passed, token = joint_red.advance((token,), "joint_sum", passed)
    (tokens_grad,), token = first_norm_backward(
        x, first_own, swap_cores(passed[0]), row_sums, vecs, res_grad, (token,)
    )
    (ffn_total,), token = row_total(lay, up_rows, (token,), "up_total", [down_total])
    ffn = Spread(lay, rest_sum(lay, ffn_total))
    (joint_rows,), token = first_rows(joint_red, (token,), "joint_rows")
    joint_rows, token = next_rows(lay, ids, joint_rows, (token,), "joint_rows_2")
    token = ffn.forward((token,), "ffn_pieces")
    (joint_total,), token = row_total(lay, joint_rows, (token,), "joint_total")
    joint_pieces = spread(lay, rest_sum(lay, joint_total))
    up_mid, o_mid = ff // 2, o_rows // 2
    up_half = up_mid + o_mid
    (grad_down, grad_up, grad_output), token = finish(
        lay,
        ids,
        ffn.all(),
        [
            ([(0, ff)], True),
            ([(ff, up_mid), (ff + up_half, up_mid)], False),
            ([(ff + up_mid, o_mid), (ff + up_half + up_mid, o_mid)], True),
        ],
        "finish_ffn",
        (token,),
    )
    mid = j_width // 2
    counts = [HALF] * 4 + [joint_bias.shape[0], up_bias.shape[0], 2 * HALF, 2 * HALF]
    (grad_joint, *small), token = finish(
        lay,
        ids,
        joint_pieces,
        [([(0, mid), (mid + HDIM, mid)], False)],
        "finish_attention",
        (token,),
        (mid, [n // HDIM for n in counts]),
    )
    sums_one = (small[6] + swap_cores(small[7])).reshape(-1)
    second_gain_grad, second_shift_grad, output_bias_grad, down_bias_grad, joint_bias_grad, up_bias_grad = [
        v.reshape(-1) for v in small[:6]
    ]
    return (
        layer_out,
        tokens_grad,
        sums_one[:HALF],
        sums_one[HALF:],
        grad_joint,
        joint_bias_grad,
        grad_output,
        output_bias_grad,
        second_gain_grad,
        second_shift_grad,
        grad_up,
        up_bias_grad,
        grad_down,
        down_bias_grad,
    )


def solution(mesh):
    lay = Layout(mesh)
    vec, rows, cols, flat = P("col"), P("row", "col"), P("col", "row"), P(("dp", "row"), "col")

    def shards(*args):
        return layer(lay, *args)

    return jax.shard_map(
        shards,
        mesh=mesh,
        in_specs=(flat, flat, P(("dp", "row")), vec, vec, rows, vec, cols, vec, vec, vec, rows, vec, cols, vec),
        out_specs=(flat, flat, vec, vec, rows, vec, cols, vec, vec, vec, rows, vec, cols, vec),
        check_vma=False,
    )
```

```python
import math

import jax
import jax.numpy as jnp
from jax import lax
from jax.experimental import pallas as pl
from jax.experimental.pallas import tpu as pltpu
from jax.sharding import PartitionSpec as P

D = 1024
HALF = 512
HDIM = 128
LEN = 1024
MAX_PREFIX = 512
EPSILON = 1e-05
NEGATIVE = -1e30
LOG2E = math.log2(math.e)
SCALE = HDIM**-0.5
TILE = 256

BF = jnp.bfloat16
F32 = jnp.float32
NT = (((1,), (1,)), ((), ()))
TN = (((0,), (0,)), ((), ()))


def vmem():
    return pl.BlockSpec(memory_space=pltpu.VMEM)


def smem():
    return pl.BlockSpec(memory_space=pltpu.SMEM)


def anywhere():
    return pl.BlockSpec(memory_space=pltpu.HBM)


def params(mib=60):
    return pltpu.CompilerParams(vmem_limit_bytes=mib << 20)


def shape(dims, kind=BF):
    return jax.ShapeDtypeStruct(tuple(dims), kind)


def hbm(dims, kind=BF):
    return pltpu.HBM(tuple(dims), kind)


def dot(left, right, dims=(((1,), (0,)), ((), ()))):
    return lax.dot_general(left, right, dims, preferred_element_type=F32)


class Layout:
    def __init__(self, mesh):
        self.R = mesh.shape["row"]
        self.Q = mesh.shape["dp"]
        self.block = D // self.R
        s = self.Q
        while self.block // s < 16:
            s //= 2
        self.s = s
        self.piece = self.block // s
        bits = self.Q.bit_length() - 1
        low = [1 << b for b in range(bits // 2)]
        high = [1 << b for b in range(bits // 2, bits)]
        mixed = []
        while low or high:
            if low:
                mixed.append(low.pop(0))
            if high:
                mixed.append(high.pop(0))
        k = s.bit_length() - 1
        self.split_bits = mixed[:k]
        self.rest_bits = mixed[k:]
        self.order_a = list(range(k))
        self.order_b = [1, 0] + list(range(2, k)) if k >= 2 else list(range(k))
        self.row_bits = [1 << b for b in range(self.R.bit_length() - 1)]


def swap(value, axis, size, bit):
    return lax.ppermute(value, axis, [(i, i ^ bit) for i in range(size)])


def swap_cores(value):
    return lax.ppermute(value, "col", [(0, 1), (1, 0)])


def device_ids(lay):
    z = lax.axis_index("row")
    d = lax.axis_index("dp")
    c = lax.axis_index("col")
    q = sum(((d // bit) % 2) << i for i, bit in enumerate(lay.split_bits))
    return jnp.stack([z ^ (c * (lay.R // 2)), q, c]).astype(jnp.int32)


COST = {
    "first_norm_project": 9,
    "attention_first": 5,
    "attention_second": 7,
    "second_norm_up": 15,
    "down_grad": 9,
    "hidden_backward": 17,
    "up_grad": 9,
    "second_norm_backward": 9,
    "attention_backward": 6,
    "joint_grad": 10,
    "project_backward": 8,
    "first_norm_backward": 6,
    "down_project": 9,
    "joint_sum": 32,
}
WIDE = {"second_norm_up": 18, "hidden_backward": 18, "attention_second": 18}
COST_SCALE = 0.25 * 3.69e6


def call(kernel, name, ins, outs, grid=(), scratch=(), after=(), passing=(), mib=None):
    n_in, n_after, n_out, n_pass = len(ins), len(after), len(outs), len(passing)

    def body(*refs):
        refs = list(refs)
        first_out = n_in + n_after + n_pass
        token = first_out + n_out + n_pass
        kernel(*refs[:n_in], *refs[first_out : first_out + n_out], *refs[token + 1 :])

    results = pl.pallas_call(
        body,
        grid=grid,
        in_specs=[spec for _, spec in ins] + [anywhere()] * (n_after + n_pass),
        out_specs=[spec for _, spec in outs] + [anywhere()] * (n_pass + 1),
        out_shape=[kind for kind, _ in outs]
        + [shape(a.shape, a.dtype) for a in passing]
        + [shape((8, HDIM), F32)],
        scratch_shapes=list(scratch),
        compiler_params=params(mib or (WIDE.get(name, 12) if name in COST else 8)),
        input_output_aliases={n_in + n_after + i: n_out + i for i in range(n_pass)},
        cost_estimate=pl.CostEstimate(
            flops=1, bytes_accessed=int(COST_SCALE * COST.get(name, 2)), transcendentals=0
        ),
        name=name,
    )(*[array for array, _ in ins], *after, *passing)
    return results[:-1], results[-1]


def hold(arrays, after, name):
    return call(lambda: None, name, [], [], after=after, passing=arrays, mib=8)


def row_tile(width):
    return pl.BlockSpec((TILE, width), lambda i: (i, 0))


def whole(*dims):
    return pl.BlockSpec(dims, lambda i: (0,) * len(dims))


ROW_GRID = (LEN // TILE,)


def own_pieces(ids, parts, rows):
    return jnp.concatenate(
        [lax.dynamic_slice_in_dim(block, ids[1] * step + first, rows, axis=0) for block, step, first in parts], axis=1
    )


def extract(lay, ids, block, rows, after):
    def kernel(ids, source, out, sem):
        copy = pltpu.make_async_copy(source.at[pl.ds(pl.multiple_of(ids[1] * rows, 16), rows), :], out, sem)
        copy.start()
        copy.wait()

    (out,), token = call(
        kernel,
        "extract",
        [(ids, smem()), (block, anywhere())],
        [(shape((rows, block.shape[1])), vmem())],
        scratch=[pltpu.SemaphoreType.DMA],
        after=after,
    )
    return out, token


def cut(lay, arrays, axis, after, name):
    n, rows, columns = arrays[0].shape
    rows, columns = (rows // 2, columns) if axis == 1 else (rows, columns // 2)
    kind = shape((n, rows, columns))

    def spec(i):
        return pl.BlockSpec((1, rows, columns), lambda k: (k, i, 0) if axis == 1 else (k, 0, i))

    def kernel(a, b, left, right):
        left[...] = a[...]
        right[...] = b[...]

    out = pl.BlockSpec((1, rows, columns), lambda k: (k, 0, 0))
    return call(
        kernel, name, [(arrays[0], spec(0)), (arrays[1], spec(1))], [(kind, out)] * 2, grid=(n,), after=after
    )


def join(arrays, after, name):
    rows = sum(a.shape[0] for a in arrays)

    def kernel(*refs):
        at = 0
        for ref in refs[:-1]:
            refs[-1][at : at + ref.shape[0]] = ref[...]
            at += ref.shape[0]

    (out,), token = call(
        kernel, name, [(a, vmem()) for a in arrays], [(shape((rows, *arrays[0].shape[1:])), vmem())], after=after
    )
    return out, token


class Gathered:
    def __init__(self, lay, piece, axis, name, at_once):
        self.lay, self.axis, self.name = lay, axis, name
        piece = piece[None]
        if at_once:
            self.z_offsets = list(range(1, lay.R))
            self.got = [swap(piece, "row", lay.R, k) for k in self.z_offsets]
            self.bits = []
        else:
            self.bits = list(reversed(lay.row_bits))
            self.held, self.held_offsets = [piece], [0]
            self.got, self.z_offsets = [], []
            self.step()

    def step(self):
        bit = self.bits.pop(0)
        sent = self.held[0]
        self.got.append(swap(sent, "row", self.lay.R, bit))
        self.z_offsets += [o ^ bit for o in self.held_offsets]
        self.held_offsets = self.held_offsets + [o ^ bit for o in self.held_offsets]

    def double(self, after):
        token = after[0]
        while self.bits:
            self.held[0], token = join([self.held[0], self.got[-1]], (token, *after[1:]), self.name + "_double")
            self.step()
        return token

    def spread(self, after):
        lay = self.lay
        self.others, token = join(self.got, after, self.name + "_join")
        self.size = self.others.shape[self.axis]
        self.pieces = [(self.others, 0, 0, self.size)]
        for i in range(min(2, len(lay.split_bits))):
            self.pieces.append((swap(self.others, "dp", lay.Q, lay.split_bits[i]), 1 << i, 0, self.size))
        return token

    def forward(self, after):
        lay, half = self.lay, self.size // 2
        if len(lay.split_bits) < 2:
            return after[0]
        (left, right), token = cut(
            lay, [self.pieces[1][0], self.pieces[2][0]], self.axis, after, self.name
        )
        self.pieces.append((swap(left, "dp", lay.Q, lay.split_bits[1]), 3, 0, half))
        self.pieces.append((swap(right, "dp", lay.Q, lay.split_bits[0]), 3, half, half))
        for i, bit in list(enumerate(lay.split_bits))[2:]:
            self.pieces += [(swap(a, "dp", lay.Q, bit), q | 1 << i, f, n) for a, q, f, n in self.pieces]
        return token

    def sources(self, ids, refs, first=0):
        at = 0
        for _, qo, begin, size in self.pieces:
            if begin + size <= first:
                continue
            for k, zo in enumerate(self.z_offsets):
                yield refs[at].at[k], begin, size, ids[1] ^ qo, ids[0] ^ zo
            at += 1

    def arrays(self, first=0):
        return [a for a, _, begin, size in self.pieces if begin + size > first]


class Weight:
    def __init__(self, gathered, block, dims, pairs, first=0):
        self.block, self.dims, self.pairs = block, dims, pairs
        arrays = gathered.arrays(first)
        self.operands = [(a, anywhere()) for a in arrays] + [(block, anywhere())]
        self.n = len(self.operands)

        class Fake:
            def __getitem__(self, i):
                return self

            @property
            def at(self):
                return self

        fake = Fake()
        copies_n = len(list(pairs([1, 0], [fake] * self.n, fake)))
        self.scratch = [pltpu.VMEM(dims, BF), pltpu.SemaphoreType.DMA((copies_n,))]

    def copies(self, ids, refs, target, sems):
        return [
            pltpu.make_async_copy(a, b, sems.at[i])
            for i, (a, b) in enumerate(self.pairs(ids, refs, target))
        ]


def start_all(copies):
    for copy in copies:
        copy.start()


def wait_all(copies):
    for copy in copies:
        copy.wait()


def aligned(value, multiple):
    return value * multiple if isinstance(value, int) else pl.multiple_of(value * multiple, multiple)


def joint_weight_of(gathered, block):
    lay = gathered.lay
    width = block.shape[1]

    def pairs(ids, refs, target):
        for source, first, size, q, z in gathered.sources(ids, refs):
            n = min(first + size, width) - first
            rows = pl.ds(aligned(z * lay.s + q, lay.piece), lay.piece)
            yield source.at[:, :n], target.at[rows, first : first + n]
        yield refs[-1], target.at[pl.ds(aligned(ids[0], lay.block), lay.block), :]

    return Weight(gathered, block, (D, width), pairs)


def output_weight_of(gathered, block, column):
    lay = gathered.lay
    rows = block.shape[0]
    per = rows // lay.s

    def pairs(ids, refs, target):
        for source, first, _, q, z in gathered.sources(ids, refs, column):
            for b in range(per // lay.piece):
                at = column + b * lay.block - first
                yield (
                    source.at[:, at : at + lay.block],
                    target.at[
                        pl.ds(aligned(q * (per // lay.piece) + b, lay.piece), lay.piece),
                        pl.ds(aligned(z, lay.block), lay.block),
                    ],
                )
        yield refs[-1], target.at[:, pl.ds(aligned(ids[0], lay.block), lay.block)]

    return Weight(gathered, block, (rows, D), pairs, column)


def up_weight_of(gathered, block):
    lay = gathered.lay

    def pairs(ids, refs, target):
        for source, first, size, q, z in gathered.sources(ids, refs):
            rows = pl.ds(aligned(z * lay.s + q, lay.piece), lay.piece)
            yield source, target.at[rows, first : first + size]
        yield refs[-1], target.at[pl.ds(aligned(ids[0], lay.block), lay.block), :]

    return Weight(gathered, block, (D, block.shape[1]), pairs)


def down_weight_of(gathered, block):
    lay = gathered.lay
    rows = block.shape[0]
    per = rows // lay.s

    def pairs(ids, refs, target):
        for source, first, size, q, z in gathered.sources(ids, refs):
            row = aligned(q * (per // size) + first // size, size)
            yield source, target.at[pl.ds(row, size), pl.ds(aligned(z, lay.block), lay.block)]
        yield refs[-1], target.at[:, pl.ds(aligned(ids[0], lay.block), lay.block)]

    return Weight(gathered, block, (rows, D), pairs)


def store_piece(ids, keep, send, bit, q, value):
    spot = ((q >> (bit + 1)) << bit) + (q & ((1 << bit) - 1))
    mine = ((ids[1] >> bit) & 1) == ((q >> bit) & 1)
    pl.when(mine)(lambda: keep.__setitem__(spot, value))
    pl.when(jnp.logical_not(mine))(lambda: send.__setitem__(spot, value))


def small_chunks(refs):
    two, joint_a, joint_b, up, first = refs
    for row in range(4):
        yield from (two[row : row + 1, i : i + HDIM] for i in range(0, HALF, HDIM))
    for ref in (joint_a, joint_b):
        for head in range(ref.shape[0]):
            yield from (ref[head, :, i : i + HDIM] for i in range(0, ref.shape[2], HDIM))
    yield from (up[:, i : i + HDIM] for i in range(0, up.shape[1], HDIM))
    for begin in (0, HALF):
        for row in range(2):
            yield from (first[row : row + 1, i : i + HDIM] for i in range(begin, begin + HALF, HDIM))


def weight_grad(lay, ids, parts, orders, name, smalls, after=()):
    ins, widths = [(ids, smem())], []
    for sides in parts:
        for left, right in sides:
            ins.append((left, pl.BlockSpec((LEN, lay.block), lambda z: (0, z))))
            ins.append((right, whole(*right.shape)))
        widths.append(sum(right.shape[1] for _, right in sides))
    widths[0] += HDIM
    ins.extend((v, whole(*v.shape)) for v in smalls)
    n_out = 2 * len(orders)

    def kernel(ids, *refs):
        ins, outs, rows_ref = list(refs[: -n_out - 1]), refs[-n_out - 1 : -1], refs[-1]
        small_refs = ins[-len(smalls) :]

        def fill():
            rows_ref[...] = jnp.zeros_like(rows_ref)
            for i, chunk in enumerate(small_chunks(small_refs)):
                rows_ref[i : i + 1, :] = chunk

        pl.when(pl.program_id(0) == 0)(fill)
        for i, order in enumerate(orders):
            values = []
            for _ in parts[i]:
                left, right = ins.pop(0), ins.pop(0)
                values.append(dot(left[...], right[...], TN).astype(BF))
            if i == 0:
                values.append(rows_ref[...].astype(BF))
            block = jnp.concatenate(values, axis=1)
            for q in range(lay.s):
                part = block[q * lay.piece : (q + 1) * lay.piece]
                store_piece(ids, outs[2 * i], outs[2 * i + 1], order[0], q, part)

    outs = []
    for width in widths:
        out = pl.BlockSpec((lay.s // 2, lay.piece, width), lambda z: (z, 0, 0))
        outs += [(shape((lay.R * lay.s // 2, lay.piece, width)), out)] * 2
    return call(
        kernel, name, ins, outs, grid=(lay.R,), scratch=[pltpu.VMEM((lay.block, HDIM), F32)], after=after
    )


def output_grad(lay, ids, left, rights, orders, name, after):
    width = rights[0].shape[1]
    n_out = 2 * len(orders)
    if len(rights) != len(orders):
        return halves_grad(lay, ids, left, jnp.concatenate(rights, axis=1), orders, name, after)

    def kernel(ids, left_ref, *refs):
        for i, order in enumerate(orders):
            block = dot(left_ref[...], refs[i][...], TN).astype(BF)
            keep, send = refs[len(rights) + 2 * i : len(rights) + 2 * i + 2]
            for q in range(lay.s):
                store_piece(ids, keep, send, order[0], q, block[q * lay.piece : (q + 1) * lay.piece])

    out = pl.BlockSpec((lay.s // 2, lay.piece, width), lambda z: (z, 0, 0))
    return call(
        kernel,
        name,
        [(ids, smem()), (left, pl.BlockSpec((LEN, lay.block), lambda z: (0, z)))]
        + [(r, whole(*r.shape)) for r in rights],
        [(shape((lay.R * lay.s // 2, lay.piece, width)), out)] * n_out,
        grid=(lay.R,),
        after=after,
        mib=12,
    )


def halves_grad(lay, ids, left, right, orders, name, after):
    width = right.shape[1] // len(orders)
    n_out = 2 * len(orders)

    def kernel(ids, left_ref, right_ref, *outs):
        block = dot(left_ref[...], right_ref[...], TN).astype(BF)
        for i, order in enumerate(orders):
            for q in range(lay.s):
                keep, send, bit = outs[2 * i], outs[2 * i + 1], order[0]
                part = block[q * lay.piece : (q + 1) * lay.piece, i * width : (i + 1) * width]
                store_piece(ids, keep, send, bit, q, part)

    out = pl.BlockSpec((lay.s // 2, lay.piece, width), lambda z: (z, 0, 0))
    return call(
        kernel,
        name,
        [(ids, smem()), (left, pl.BlockSpec((LEN, lay.block), lambda z: (0, z))), (right, whole(*right.shape))],
        [(shape((lay.R * lay.s // 2, lay.piece, width)), out)] * n_out,
        grid=(lay.R,),
        after=after,
    )


class Reduction:
    def __init__(self, lay, ids, orders, parts):
        self.lay, self.ids, self.orders, self.step = lay, ids, orders, 0
        k = len(lay.split_bits)
        self.left = [sorted(set(range(k)) - {order[0]}, reverse=True) for order in orders]
        self.send(parts)

    def send(self, parts):
        self.keep, self.got = list(parts[0::2]), []
        for order, part in zip(self.orders, parts[1::2]):
            self.got.append(swap(part, "dp", self.lay.Q, self.lay.split_bits[order[self.step]]))
        self.step += 1

    def advance(self, after, name, passing=(), joined=()):
        lay, n = self.lay, len(self.orders)
        bits = [order[self.step] for order in self.orders]
        ins, outs = [(self.ids, smem())], []
        reds = [self, *joined]
        for i, bit in enumerate(bits):
            groups = lay.R * 2 ** self.left[i].index(bit)
            rows = 2 ** (len(self.left[i]) - 1 - self.left[i].index(bit)) * lay.piece
            width = sum(r.keep[i].shape[-1] for r in reds)
            for value in [v for r in reds for v in (r.keep[i], r.got[i])]:
                columns = value.shape[-1]
                ins.append(
                    (value.reshape(groups, 2, rows, columns), pl.BlockSpec((1, 2, rows, columns), lambda g: (g, 0, 0, 0)))
                )
            outs += [(shape((groups, rows, width)), pl.BlockSpec((1, rows, width), lambda g: (g, 0, 0)))] * 2

        def kernel(ids, *refs):
            ins, outs = list(refs[: 2 * n * len(reds)]), refs[2 * n * len(reds) :]
            for i, bit in enumerate(bits):
                mine = (ids[1] >> bit) & 1
                first = 0
                for _ in reds:
                    a, b = ins.pop(0), ins.pop(0)
                    last = first + a.shape[3]
                    for target, which in ((outs[2 * i], mine), (outs[2 * i + 1], 1 - mine)):
                        target[0, :, first:last] = (a[0, which].astype(F32) + b[0, which].astype(F32)).astype(BF)
                    first = last

        parts, token = call(kernel, name, ins, outs, grid=(groups,), after=after, passing=passing)
        self.left = [[b for b in left if b != bit] for left, bit in zip(self.left, bits)]
        self.send(parts[: 2 * n])
        return parts[2 * n :], token


def first_rows(reduction, after, name, passing=()):
    lay, ids, n = reduction.lay, reduction.ids, len(reduction.orders)
    ins = [(ids, smem())]
    widths = [keep.shape[-1] for keep in reduction.keep]
    starts = [sum(widths[:i]) for i in range(n)]
    columns = sum(widths)
    for i, width in enumerate(widths):
        for value in (reduction.keep[i], reduction.got[i]):
            value = value.reshape(lay.R // 2, 2, lay.piece, width)
            ins.append((value, pl.BlockSpec((1, 2, lay.piece, width), lambda g: (g, 0, 0, 0))))
    out = pl.BlockSpec((1, lay.piece, columns), lambda g: (g, 0, 0))

    def kernel(ids, *refs):
        ins, (keep, send) = refs[:-2], refs[-2:]
        mine = ids[0] & 1
        for target, bit in ((keep, mine), (send, 1 - mine)):
            for i in range(n):
                a, b = ins[2 * i], ins[2 * i + 1]
                total = (a[0, bit].astype(F32) + b[0, bit].astype(F32)).astype(BF)
                target[0, :, starts[i] : starts[i] + widths[i]] = total

    kind = shape((lay.R // 2, lay.piece, columns))
    (keep, send, *passed), token = call(
        kernel, name, ins, [(kind, out)] * 2, grid=(lay.R // 2,), after=after, passing=passing
    )
    return ((keep, swap(send, "row", lay.R, 1)), *passed), token


def next_rows(lay, ids, pair, after, name):
    token = after[0]
    for i, bit in list(enumerate(lay.row_bits))[1:]:
        keep, got = pair
        groups = keep.shape[0] // 2
        columns = keep.shape[-1]
        ins = [(ids, smem())]
        for value in pair:
            value = value.reshape(groups, 2, lay.piece, columns)
            ins.append((value, pl.BlockSpec((1, 2, lay.piece, columns), lambda g: (g, 0, 0, 0))))
        out = pl.BlockSpec((1, lay.piece, columns), lambda g: (g, 0, 0))

        def kernel(ids, a, b, keep, send, i=i):
            mine = (ids[0] >> i) & 1
            for target, which in ((keep, mine), (send, 1 - mine)):
                target[0] = (a[0, which].astype(F32) + b[0, which].astype(F32)).astype(BF)

        kind = shape((groups, lay.piece, columns))
        (keep, send), token = call(kernel, name, ins, [(kind, out)] * 2, grid=(groups,), after=(token, *after[1:]))
        pair = (keep, swap(send, "row", lay.R, bit))
    return pair, token


def row_total(lay, pair, after, name, ready=(), passing=()):
    width = pair[0].shape[-1]
    columns = width + sum(r.shape[1] for r in ready)

    def kernel(*refs):
        (*others, a, b), out = refs[:-1], refs[-1]
        column = 0
        for ref in others:
            out[:, column : column + ref.shape[1]] = ref[...]
            column += ref.shape[1]
        out[:, column:] = (a[...].astype(F32) + b[...].astype(F32)).astype(BF)

    (total, *passed), token = call(
        kernel,
        name,
        [(v, vmem()) for v in ready] + [(v.reshape(lay.piece, width), vmem()) for v in pair],
        [(shape((lay.piece, columns)), vmem())],
        after=after,
        passing=passing,
    )
    return (total, *passed), token


def rest_sum(lay, total):
    for bit in lay.rest_bits:
        total = (total.astype(F32) + swap(total, "dp", lay.Q, bit).astype(F32)).astype(BF)
    return total


def spread(lay, total):
    got = [total]
    for offset in range(1, lay.s):
        mask = sum(bit for i, bit in enumerate(lay.split_bits) if (offset >> i) & 1)
        got.append(swap(total, "dp", lay.Q, mask))
    return got


class Spread:
    def __init__(self, lay, total):
        self.lay = lay
        self.pieces = {0: total}
        for i in range(min(2, len(lay.split_bits))):
            self.pieces[1 << i] = swap(total, "dp", lay.Q, lay.split_bits[i])

    def forward(self, after, name):
        lay, token = self.lay, after[0]
        if len(lay.split_bits) >= 2:
            (left, right), token = cut(lay, [self.pieces[1][None], self.pieces[2][None]], 2, after, name)
            self.pieces[3] = (
                swap(left[0], "dp", lay.Q, lay.split_bits[1]),
                swap(right[0], "dp", lay.Q, lay.split_bits[0]),
            )
        for i, bit in list(enumerate(lay.split_bits))[2:]:
            for q, piece in list(self.pieces.items()):
                self.pieces[q | 1 << i] = jax.tree.map(lambda v: swap(v, "dp", lay.Q, bit), piece)
        return token

    def all(self):
        return [self.pieces[q] for q in range(self.lay.s)]


def finish(lay, ids, pieces, plan, name, after=(), small=None):
    outs = []
    for spans, transposed in plan:
        n = sum(c for _, c in spans)
        outs.append((shape((n, lay.block) if transposed else (lay.block, n), F32), vmem()))
    if small:
        outs += [(shape((rows, HDIM), F32), vmem()) for rows in small[1]]
    arrays = jax.tree.leaves(pieces)
    n_in = len(arrays)
    widest = max([HDIM] + [sum(c for _, c in spans) for spans, t in plan if t])

    def kernel(ids, *refs):
        ins, results, scratch = list(refs[:n_in]), refs[n_in:-1], refs[-1]
        values = []
        for piece in pieces:
            if isinstance(piece, tuple):
                values.append(jnp.concatenate([ins.pop(0)[...], ins.pop(0)[...]], axis=1))
            else:
                values.append(ins.pop(0))
        for (spans, transposed), result in zip(plan, results):
            column = 0
            for first, n in spans:
                for offset in range(lay.s):
                    rows = pl.ds(aligned(ids[1] ^ offset, lay.piece), lay.piece)
                    value = values[offset][:, first : first + n].astype(F32)
                    if transposed:
                        scratch[rows, column : column + n] = value
                    else:
                        result[rows, column : column + n] = value
                column += n
            if transposed:
                result[...] = scratch[:, :column].T
        if small:
            for offset in range(lay.s):
                rows = pl.ds(aligned(ids[1] ^ offset, lay.piece), lay.piece)
                scratch[rows, :HDIM] = values[offset][:, small[0] : small[0] + HDIM].astype(F32)
            row = 0
            for count, result in zip(small[1], results[len(plan) :]):
                result[...] = scratch[row : row + count, :HDIM]
                row += count

    return call(
        kernel,
        name,
        [(ids, smem())] + [(p, vmem()) for p in arrays],
        outs,
        scratch=[pltpu.VMEM((lay.block, widest), F32)],
        after=after,
        mib=12,
    )


def both(own, other):
    return jnp.concatenate([own, other], axis=1)


def row_stats(values):
    average = jnp.mean(values, axis=1, keepdims=True)
    square = jnp.mean(values * values, axis=1, keepdims=True)
    return average, lax.rsqrt(square - average * average + EPSILON)


def norm_grad(gradient, centered, factor, gain):
    scaled = gradient * gain
    first = jnp.mean(scaled, axis=1, keepdims=True)
    second = jnp.mean(scaled * centered, axis=1, keepdims=True)
    return factor * (scaled - first - centered * second)


V_GAIN1, V_SHIFT1, V_GAIN2, V_SHIFT2, V_OBIAS = range(5)


def pair_row(own_ref, other_ref, i):
    return both(own_ref[i : i + 1, :], other_ref[i : i + 1, :])


def branch_sum(own, other):
    return own[...].astype(F32) + both(other[:, HALF:], other[:, :HALF]).astype(F32)


def pair_up(pairs, after):
    def kernel(*refs):
        n = len(pairs)
        for i in range(n):
            refs[2 * n + i][:, :HALF] = refs[2 * i][...]
            refs[2 * n + i][:, HALF:] = refs[2 * i + 1][...]

    return call(
        kernel,
        "pair_up",
        [(v, row_tile(HALF)) for pair in pairs for v in pair],
        [(shape((LEN, D)), row_tile(D))] * len(pairs),
        grid=ROW_GRID,
        after=after,
    )


def first_norm_project(ids, x, vecs, bias, joint, after):
    width = bias.shape[1]

    def kernel(ids, x_ref, vo, vt, bias, *refs):
        pieces, full, qkv, weight, sems = refs[: joint.n], *refs[joint.n :]
        copies = joint.copies(ids, pieces, weight, sems)
        first = pl.program_id(0) == 0
        pl.when(first)(lambda: start_all(copies))
        values = x_ref[...].astype(F32)
        average, factor = row_stats(values)
        normed = (values - average) * factor * pair_row(vo, vt, V_GAIN1) + pair_row(vo, vt, V_SHIFT1)
        low = normed.astype(BF)
        full[...] = low
        pl.when(first)(lambda: wait_all(copies))
        qkv[...] = (dot(low, weight[...]) + bias[...]).astype(BF)

    return call(
        kernel,
        "first_norm_project",
        [(ids, smem()), (x, row_tile(D)), *[(v, whole(8, HALF)) for v in vecs], (bias, whole(1, width))]
        + joint.operands,
        [(hbm((LEN, D)), row_tile(D)), (shape((LEN, width)), row_tile(width))],
        grid=ROW_GRID,
        scratch=joint.scratch,
        after=after,
    )


def visible_mask(lo, rows, queries, prefix):
    key_id = lax.broadcasted_iota(jnp.int32, (rows, queries), 0) + lo
    query_id = lax.broadcasted_iota(jnp.int32, (rows, queries), 1) + lo
    return (key_id <= query_id) | (key_id < prefix)


def attend(prefix_ref, qkv_ref, out_ref, log_ref):
    bq = 512
    prefix_end = prefix_ref[0]
    for h in range(log_ref.shape[0]):
        base = h * 3 * HDIM
        keys = qkv_ref[:, base + HDIM : base + 2 * HDIM]
        values_t = qkv_ref[:, base + 2 * HDIM : base + 3 * HDIM].T
        for lo in range(0, LEN, bq):
            n = max(MAX_PREFIX, lo + bq)
            query = qkv_ref[lo : lo + bq, base : base + HDIM]
            scores = dot(keys[:n], query, NT)
            tail = jnp.where(visible_mask(lo, n - lo, bq, prefix_end), scores[lo:], NEGATIVE)
            scores = tail if lo == 0 else jnp.concatenate([scores[:lo], tail], axis=0)
            top = jnp.max(scores, axis=0, keepdims=True) * (SCALE * LOG2E)
            weights = jnp.exp2(scores * (SCALE * LOG2E) - top)
            total = jnp.sum(weights, axis=0, keepdims=True)
            mixed = dot(values_t[:, :n], weights.astype(BF)) * (1.0 / total)
            out_ref[lo : lo + bq, h * HDIM : (h + 1) * HDIM] = mixed.T.astype(BF)
            log_ref[h, :, lo : lo + bq] = top + jnp.log2(total)


def attention_first(prefix, qkv, heads, after):
    return call(
        attend,
        "attention_first",
        [(prefix, smem()), (qkv, pl.BlockSpec((LEN, 3 * HDIM * heads), lambda i: (0, 0)))],
        [
            (shape((LEN, HDIM * heads)), whole(LEN, HDIM * heads)),
            (shape((heads, 1, LEN), F32), whole(heads, 1, LEN)),
        ],
        grid=(1,),
        after=after,
    )


def attention_second(ids, prefix, qkv, heads, attended_first, output, after):
    width = HDIM * heads

    def kernel(ids, prefix_ref, qkv_ref, first_ref, *refs):
        pieces, (out_ref, log_ref, branch, weight, sems) = refs[: output.n], refs[output.n :]
        copies = output.copies(ids, pieces, weight, sems)
        start_all(copies)
        attend(prefix_ref, qkv_ref, out_ref, log_ref)
        wait_all(copies)
        for lo in range(0, LEN, TILE):
            rows = slice(lo, lo + TILE)
            branch[rows, :] = dot(both(first_ref[rows, :], out_ref[rows, :]), weight[...]).astype(BF)

    return call(
        kernel,
        "attention_second",
        [(ids, smem()), (prefix, smem()), (qkv, pl.BlockSpec((LEN, 3 * HDIM * heads), lambda i: (0, 1))),
         (attended_first, whole(LEN, width))]
        + output.operands,
        [
            (shape((LEN, width)), whole(LEN, width)),
            (shape((heads, 1, LEN), F32), whole(heads, 1, LEN)),
            (shape((LEN, D)), whole(LEN, D)),
        ],
        grid=(1,),
        scratch=output.scratch,
        after=after,
    )


def second_norm_up(ids, x, parts, vecs, bias, up, after):
    width = bias.shape[1]

    def kernel(ids, x_ref, po, pt, vo, vt, bias, *refs):
        pieces = refs[: up.n]
        residual, centered, factor_ref, full, active, slope, weight, sems = refs[up.n :]
        copies = up.copies(ids, pieces, weight, sems)
        first = pl.program_id(0) == 0
        pl.when(first)(lambda: start_all(copies))
        res = x_ref[...].astype(F32) + (branch_sum(po, pt) + pair_row(vo, vt, V_OBIAS))
        residual[...] = res[:, :HALF]
        average, factor = row_stats(res)
        cent = (res - average) * factor
        centered[...] = cent.astype(BF)
        factor_ref[...] = factor
        low = (cent * pair_row(vo, vt, V_GAIN2) + pair_row(vo, vt, V_SHIFT2)).astype(BF)
        full[...] = low
        pl.when(first)(lambda: wait_all(copies))
        hidden = dot(low, weight[...]) + bias[...]
        bell = jnp.exp(-0.5 * hidden * hidden) * (1.0 / math.sqrt(2.0 * math.pi))
        phi = 0.5 * (1.0 + lax.erf(hidden * 2.0**-0.5))
        active[...] = (hidden * phi).astype(BF)
        slope[...] = (phi + hidden * bell).astype(BF)

    return call(
        kernel,
        "second_norm_up",
        [(ids, smem()), (x, row_tile(D)), *[(p, row_tile(D)) for p in parts], *[(v, whole(8, HALF)) for v in vecs],
         (bias, whole(1, width))]
        + up.operands,
        [
            (hbm((LEN, HALF), F32), row_tile(HALF)),
            (hbm((LEN, D)), row_tile(D)),
            (hbm((LEN, 1), F32), row_tile(1)),
            (hbm((LEN, D)), row_tile(D)),
            (shape((LEN, width)), row_tile(width)),
            (shape((LEN, width)), row_tile(width)),
        ],
        grid=ROW_GRID,
        scratch=up.scratch,
        after=after,
    )


def hidden_backward(ids, cot, slope, up, down, after):
    width = slope.shape[1]

    def kernel(ids, cot_ref, slope_ref, *refs):
        up_pieces, refs = refs[: up.n], refs[up.n :]
        down_pieces, refs = refs[: down.n], refs[down.n :]
        hidden_grad, partial, bias_grad, up_full, up_sems, down_full, down_sems = refs
        down_copies = down.copies(ids, down_pieces, down_full, down_sems)
        up_copies = up.copies(ids, up_pieces, up_full, up_sems)
        first = pl.program_id(0) == 0

        def begin():
            start_all(down_copies)
            start_all(up_copies)
            bias_grad[...] = jnp.zeros_like(bias_grad)
            wait_all(down_copies)

        pl.when(first)(begin)
        grad = dot(cot_ref[...], down_full[...], NT) * slope_ref[...].astype(F32)
        low = grad.astype(BF)
        hidden_grad[...] = low
        bias_grad[...] += jnp.sum(low.astype(F32), axis=0, keepdims=True)
        pl.when(first)(lambda: wait_all(up_copies))
        partial[...] = dot(low, up_full[...], NT).astype(BF)

    return call(
        kernel,
        "hidden_backward",
        [(ids, smem()), (cot, row_tile(D)), (slope, row_tile(width))] + up.operands + down.operands,
        [(hbm((LEN, width)), row_tile(width)), (shape((LEN, D)), row_tile(D)), (shape((1, width), F32), whole(1, width))],
        grid=ROW_GRID,
        scratch=up.scratch + down.scratch,
        after=after,
    )


def second_norm_backward(ids, cot, parts, centered, factor, vecs, output, after):
    width = output.dims[0]

    def kernel(ids, cot_ref, po, pt, cent_ref, factor_ref, vo, vt, *refs):
        pieces, (branch, res_grad, att_grad, sums_ref, weight, sems) = refs[: output.n], refs[output.n :]
        copies = output.copies(ids, pieces, weight, sems)
        first = pl.program_id(0) == 0

        def begin():
            start_all(copies)
            sums_ref[...] = jnp.zeros_like(sums_ref)

        pl.when(first)(begin)
        grad = branch_sum(po, pt)
        cent = cent_ref[...].astype(F32)
        cot = cot_ref[...].astype(F32)
        total = cot + norm_grad(grad, cent, factor_ref[...], pair_row(vo, vt, V_GAIN2))
        low = total.astype(BF)
        branch[...] = low
        res_grad[...] = total[:, :HALF]
        news = (grad[:, :HALF] * cent[:, :HALF], grad[:, :HALF], low[:, :HALF].astype(F32), cot[:, :HALF])
        for i, value in enumerate(news):
            sums_ref[i : i + 1, :] += jnp.sum(value, axis=0, keepdims=True)
        pl.when(first)(lambda: wait_all(copies))
        att_grad[...] = dot(low, weight[...], NT).astype(BF)

    return call(
        kernel,
        "second_norm_backward",
        [(ids, smem()), (cot, row_tile(D)), *[(p, row_tile(D)) for p in parts], (centered, row_tile(D)),
         (factor, row_tile(1)), *[(v, whole(8, HALF)) for v in vecs]]
        + output.operands,
        [
            (shape((LEN, D)), row_tile(D)),
            (shape((LEN, HALF), F32), row_tile(HALF)),
            (shape((LEN, width)), row_tile(width)),
            (shape((4, HALF), F32), whole(4, HALF)),
        ],
        grid=ROW_GRID,
        scratch=output.scratch,
        after=after,
    )


def attention_backward(prefix, qkv, grads, logs, attended, first_head, heads, after):
    bq = 256

    def kernel(prefix_ref, qkv_ref, grad_ref, log_ref, att_ref, out_ref, sums_ref, key_sum, value_sum):
        prefix_end = prefix_ref[0]
        keys = qkv_ref[:, HDIM : 2 * HDIM]
        values = qkv_ref[:, 2 * HDIM : 3 * HDIM]
        keys_t = keys.T
        query_total = jnp.zeros((1, HDIM), F32)
        for lo in reversed(range(0, LEN, bq)):
            n = max(MAX_PREFIX, lo + bq)
            query = qkv_ref[lo : lo + bq, 0:HDIM]
            grad = grad_ref[lo : lo + bq, :]
            scores = dot(keys[:n], query, NT) * (SCALE * LOG2E)
            weights = jnp.exp2(scores - log_ref[0, :, lo : lo + bq])
            tail = jnp.where(visible_mask(lo, n - lo, bq, prefix_end), weights[lo:], 0.0)
            weights = tail if lo == 0 else jnp.concatenate([weights[:lo], tail], axis=0)
            weight_grad_t = dot(values[:n], grad, NT)
            mixed = grad.astype(F32) * att_ref[lo : lo + bq, :].astype(F32)
            delta = jnp.sum(mixed.T, axis=0, keepdims=True)
            score_grad = (weights * (weight_grad_t - delta)).astype(BF)
            value_part = dot(weights.astype(BF), grad)
            key_part = dot(score_grad, query)
            if lo + bq == LEN:
                value_sum[...] = value_part
                key_sum[...] = key_part
            else:
                value_sum[:n, :] += value_part
                key_sum[:n, :] += key_part
            query_part = (dot(keys_t[:, :n], score_grad).T * SCALE).astype(BF)
            out_ref[lo : lo + bq, 0:HDIM] = query_part
            query_total = query_total + jnp.sum(query_part.astype(F32), axis=0, keepdims=True)
        out_ref[:, HDIM : 2 * HDIM] = (key_sum[...] * SCALE).astype(BF)
        value_low = value_sum[...].astype(BF)
        out_ref[:, 2 * HDIM : 3 * HDIM] = value_low
        sums_ref[0] = both(query_total, jnp.sum(value_low.astype(F32), axis=0, keepdims=True))

    return call(
        kernel,
        "attention_backward",
        [
            (prefix, smem()),
            (qkv, pl.BlockSpec((LEN, 3 * HDIM), lambda h: (0, h + first_head))),
            (grads, pl.BlockSpec((LEN, HDIM), lambda h: (0, h + first_head))),
            (logs, pl.BlockSpec((1, 1, LEN), lambda h: (h, 0, 0))),
            (attended, pl.BlockSpec((LEN, HDIM), lambda h: (0, h))),
        ],
        [
            (shape((LEN, 3 * HDIM * heads)), pl.BlockSpec((LEN, 3 * HDIM), lambda h: (0, h))),
            (shape((heads, 1, 2 * HDIM), F32), pl.BlockSpec((1, 1, 2 * HDIM), lambda h: (h, 0, 0))),
        ],
        grid=(heads,),
        scratch=[pltpu.VMEM((LEN, HDIM), F32), pltpu.VMEM((LEN, HDIM), F32)],
        after=after,
    )


def project_backward(ids, grads, x, vecs, joint, after):
    widths = [g.shape[1] for g in grads]

    def kernel(ids, x_ref, vo, vt, *refs):
        grad_refs, refs = refs[: len(grads)], refs[len(grads) :]
        pieces, (own, other, sums, columns, weight, sems) = refs[: joint.n], refs[joint.n :]
        copies = joint.copies(ids, pieces, weight, sems)
        first = pl.program_id(0) == 0

        def begin():
            start_all(copies)
            columns[...] = jnp.zeros_like(columns)

        pl.when(first)(begin)
        values = x_ref[...].astype(F32)
        average, factor = row_stats(values)
        pl.when(first)(lambda: wait_all(copies))
        total, column = 0.0, 0
        for ref, width in zip(grad_refs, widths):
            total = total + dot(ref[...], weight[:, column : column + width], NT)
            column += width
        own[...] = total[:, :HALF].astype(BF)
        other[:, :HALF] = total[:, HALF:].astype(BF)
        gain = pair_row(vo, vt, V_GAIN1)
        product = total * ((values - average) * factor)
        columns[0:1, :] += jnp.sum(product, axis=0, keepdims=True)
        columns[1:2, :] += jnp.sum(total, axis=0, keepdims=True)
        lane = lax.broadcasted_iota(jnp.int32, (TILE, HDIM), 1)
        packed = jnp.zeros((TILE, HDIM), F32)
        parts = jnp.zeros((TILE, HDIM), F32)
        for i, value in enumerate((total * gain, product * gain)):
            row_sum = jnp.sum(value, axis=1, keepdims=True)
            high = row_sum.astype(BF).astype(F32)
            packed = jnp.where(lane == 2 * i, high, jnp.where(lane == 2 * i + 1, row_sum - high, packed))
            parts = jnp.where(lane == i, row_sum, parts)
        other[:, HALF:] = packed.astype(BF)
        sums[...] = parts

    return call(
        kernel,
        "project_backward",
        [(ids, smem()), (x, row_tile(D)), *[(v, whole(8, HALF)) for v in vecs]]
        + [(g, row_tile(g.shape[1])) for g in grads]
        + joint.operands,
        [
            (shape((LEN, HALF)), row_tile(HALF)),
            (shape((LEN, HALF + HDIM)), row_tile(HALF + HDIM)),
            (shape((LEN, HDIM), F32), row_tile(HDIM)),
            (shape((8, D), F32), whole(8, D)),
        ],
        grid=ROW_GRID,
        scratch=joint.scratch,
        after=after,
    )


MOST = LEN // 2


def most_tiles(width):
    return [
        pl.BlockSpec((TILE, width), lambda i: (jnp.minimum(i, MOST // TILE - 1), 0)),
        pl.BlockSpec((TILE, width), lambda i: (jnp.maximum(i - MOST // TILE, 0), 0)),
    ]


def in_most():
    return pl.program_id(0) < MOST // TILE


def down_project(ids, active, down, after):
    def kernel(ids, a_ref, *refs):
        pieces, (own, other, rest, weight, sems) = refs[: down.n], refs[down.n :]
        copies = down.copies(ids, pieces, weight, sems)

        def begin():
            start_all(copies)
            wait_all(copies)

        pl.when(pl.program_id(0) == 0)(begin)
        value = dot(a_ref[...], weight[...]).astype(BF)
        own[...] = value[:, :HALF]
        pl.when(in_most())(lambda: other.__setitem__(..., value[:, HALF:]))
        pl.when(jnp.logical_not(in_most()))(lambda: rest.__setitem__(..., value[:, HALF:]))

    return call(
        kernel,
        "down_project",
        [(ids, smem()), (active, row_tile(active.shape[1]))] + down.operands,
        [(shape((LEN, HALF)), row_tile(HALF))]
        + [(shape((n, HALF)), spec) for n, spec in zip((MOST, LEN - MOST), most_tiles(HALF))],
        grid=ROW_GRID,
        scratch=down.scratch,
        after=after,
    )


def add_output(residual, own, got, bias, after):
    def kernel(res, a, most, rest, bias, out):
        b = jnp.where(in_most(), most[...], rest[...])
        out[...] = (res[...] + (a[...].astype(F32) + b.astype(F32) + bias[...])).astype(BF)

    return call(
        kernel,
        "add_output",
        [(residual, row_tile(HALF)), (own, row_tile(HALF)), *zip(got, most_tiles(HALF)), (bias, whole(1, HALF))],
        [(shape((LEN, HALF)), row_tile(HALF))],
        grid=ROW_GRID,
        after=after,
    )


def first_norm_backward(x, own, other, sums, vecs, res_grad, after):
    def kernel(x_ref, po, pt, so, vo, res_ref, out):
        values = x_ref[...].astype(F32)
        average, factor = row_stats(values)
        cent = (values[:, :HALF] - average) * factor
        grad = po[...].astype(F32) + pt[:, :HALF].astype(F32)
        got = pt[:, HALF:].astype(F32)
        first = (so[:, 0:1] + (got[:, 0:1] + got[:, 1:2])) * (1.0 / D)
        second = (so[:, 1:2] + (got[:, 2:3] + got[:, 3:4])) * (1.0 / D)
        back = factor * (grad * vo[V_GAIN1 : V_GAIN1 + 1, :] - first - cent * second)
        out[...] = (res_ref[...] + back).astype(BF)

    return call(
        kernel,
        "first_norm_backward",
        [(x, row_tile(D)), (own, row_tile(HALF)), (other, row_tile(HALF + HDIM)), (sums, row_tile(HDIM)),
         (vecs[0], whole(8, HALF)), (res_grad, row_tile(HALF))],
        [(shape((LEN, HALF)), row_tile(HALF))],
        grid=ROW_GRID,
        after=after,
    )


def layer(lay, tokens_in, cotangent, prefix_length, first_gain, first_shift, joint_weight, joint_bias,
          output_weight, output_bias, second_gain, second_shift, up_weight, up_bias, down_weight, down_bias):
    heads = joint_bias.shape[0] // (2 * HDIM)
    ids = device_ids(lay)

    j_width, o_rows, ff = joint_weight.shape[1], output_weight.shape[0], down_weight.shape[0]
    per = o_rows // lay.s
    jo_piece = own_pieces(
        ids, [(joint_weight, lay.piece, 0), *[(output_weight, per, b * lay.piece) for b in range(per // lay.piece)]], lay.piece
    )
    jo = Gathered(lay, jo_piece, 2, "joint_pieces", True)

    zero_row = jnp.zeros_like(first_gain)
    vec_own = jnp.stack(
        [first_gain, first_shift, second_gain, second_shift, output_bias, zero_row, zero_row, zero_row]
    )
    vecs = (vec_own, swap_cores(vec_own))
    bias_rows = joint_bias.reshape(heads, 2, HDIM)
    joint_row = jnp.stack([bias_rows[:, 0], jnp.zeros_like(bias_rows[:, 0]), bias_rows[:, 1]], axis=1).reshape(1, -1)
    (x, cot), token = pair_up(
        [(tokens_in, swap_cores(tokens_in)), (cotangent, swap_cores(cotangent))], (*vecs, joint_row)
    )

    token = jo.spread((token,))
    up_piece, up_token = extract(lay, ids, up_weight, lay.piece, (token,))
    up = Gathered(lay, up_piece, 2, "up_pieces", False)
    token = up.double((up_token,))
    token = jo.forward((token,))
    down_piece, down_token = extract(lay, ids, down_weight, ff // lay.s, (token, *up.got))
    down = Gathered(lay, down_piece, 1, "down_pieces", False)
    token = up.spread((token, *jo.arrays()))
    joint_w = joint_weight_of(jo, joint_weight)
    output_w = output_weight_of(jo, output_weight, j_width)

    (full_one, qkv), token = first_norm_project(
        ids, x, vecs, joint_row, joint_w, (up.others, down_token)
    )
    pair = heads // 2
    token = down.double((token,))
    (attended_a, logs_a), token = attention_first(prefix_length, qkv, pair, (token,))
    token = up.forward((token,))
    up_w = up_weight_of(up, up_weight)
    (attended_b, logs_b, branch), token = attention_second(
        ids, prefix_length, qkv, pair, attended_a, output_w, (token,)
    )
    token = down.spread((token,))
    (branch,), token = hold([branch], (token, *up.arrays()), "hold_branch")
    (residual, centered, factor, full_two, active, slope), token = second_norm_up(
        ids, x, (branch, swap_cores(branch)), vecs, up_bias.reshape(1, -1), up_w, (token,)
    )
    token = down.forward((token,))
    down_w = down_weight_of(down, down_weight)
    both_orders = [lay.order_a, lay.order_b]
    later_steps = range(len(lay.split_bits) - 1)
    down_parts, token = halves_grad(lay, ids, cot, active, both_orders, "down_grad", (token,))
    down_parts, token = hold(down_parts, (token, *down.arrays()), "hold_down")
    down_red = Reduction(lay, ids, both_orders, down_parts)

    (hidden_grad, norm_part, up_bias_grad), token = hidden_backward(ids, cot, slope, up_w, down_w, (token,))
    passed, token = halves_grad(lay, ids, full_two, hidden_grad, both_orders, "up_grad", (token,))
    passed = [norm_part, *passed]
    for _ in later_steps:
        passed, token = down_red.advance((token,), "down_sum", passed)
    norm_part, *up_parts = passed
    up_red = Reduction(lay, ids, both_orders, up_parts)
    norm_parts = (norm_part, swap_cores(norm_part))
    (branch_grad, res_grad, att_grad, sums_two), token = second_norm_backward(
        ids, cot, norm_parts, centered, factor, vecs, output_w, (token,)
    )
    (qkv_grad_a, joint_sums_a), token = attention_backward(
        prefix_length, qkv, att_grad, logs_a, attended_a, 0, pair, (token,)
    )
    (qkv_grad_b, joint_sums_b), token = attention_backward(
        prefix_length, qkv, att_grad, logs_b, attended_b, pair, pair, (token,)
    )
    (down_rows,), token = first_rows(down_red, (token,), "down_rows")
    output_parts, token = output_grad(lay, ids, branch_grad, (attended_a, attended_b), both_orders, "output_grad", (token,))
    output_red = Reduction(lay, ids, both_orders, output_parts)
    (first_own, first_send, row_sums, first_sums), token = project_backward(
        ids, [qkv_grad_a, qkv_grad_b], x, vecs, joint_w, (token,)
    )
    down_rows, token = next_rows(lay, ids, down_rows, (token,), "down_rows_2")
    for i in later_steps:
        _, token = up_red.advance((token,), "up_sum", (), (output_red,) if i == 0 else ())
    joint_parts, token = weight_grad(
        lay,
        ids,
        [[(full_one, qkv_grad_a)], [(full_one, qkv_grad_b)]],
        both_orders,
        "joint_grad",
        (sums_two, joint_sums_a, joint_sums_b, up_bias_grad, first_sums),
        (token,),
    )
    joint_red = Reduction(lay, ids, both_orders, joint_parts)
    (down_own, *down_send), token = down_project(ids, active, down_w, (token,))
    (down_total,), token = row_total(lay, down_rows, (token,), "down_total")
    (up_rows, *down_send), token = first_rows(up_red, (token,), "up_rows", down_send)
    (layer_out,), token = add_output(
        residual, down_own, [swap_cores(p) for p in down_send], down_bias.reshape(1, -1), (token,)
    )
    up_rows, token = next_rows(lay, ids, up_rows, (token,), "up_rows_2")
    passed = [first_send]
    for _ in later_steps:
        passed, token = joint_red.advance((token,), "joint_sum", passed)
    (tokens_grad,), token = first_norm_backward(
        x, first_own, swap_cores(passed[0]), row_sums, vecs, res_grad, (token,)
    )
    (joint_rows,), token = first_rows(joint_red, (token,), "joint_rows")
    (ffn_total,), token = row_total(lay, up_rows, (token,), "up_total", [down_total])
    ffn = Spread(lay, rest_sum(lay, ffn_total))
    joint_rows, token = next_rows(lay, ids, joint_rows, (token,), "joint_rows_2")
    token = ffn.forward((token,), "ffn_pieces")
    (joint_total,), token = row_total(lay, joint_rows, (token,), "joint_total")
    joint_pieces = spread(lay, rest_sum(lay, joint_total))
    up_mid, o_mid = ff // 2, o_rows // 2
    up_half = up_mid + o_mid
    (grad_down, grad_up, grad_output), token = finish(
        lay,
        ids,
        ffn.all(),
        [
            ([(0, ff)], True),
            ([(ff, up_mid), (ff + up_half, up_mid)], False),
            ([(ff + up_mid, o_mid), (ff + up_half + up_mid, o_mid)], True),
        ],
        "finish_ffn",
        (token,),
    )
    mid = j_width // 2
    counts = [HALF] * 4 + [joint_bias.shape[0], up_bias.shape[0], 2 * HALF, 2 * HALF]
    (grad_joint, *small), token = finish(
        lay,
        ids,
        joint_pieces,
        [([(0, mid), (mid + HDIM, mid)], False)],
        "finish_attention",
        (token,),
        (mid, [n // HDIM for n in counts]),
    )
    sums_one = (small[6] + swap_cores(small[7])).reshape(-1)
    second_gain_grad, second_shift_grad, output_bias_grad, down_bias_grad, joint_bias_grad, up_bias_grad = [
        v.reshape(-1) for v in small[:6]
    ]
    return (
        layer_out,
        tokens_grad,
        sums_one[:HALF],
        sums_one[HALF:],
        grad_joint,
        joint_bias_grad,
        grad_output,
        output_bias_grad,
        second_gain_grad,
        second_shift_grad,
        grad_up,
        up_bias_grad,
        grad_down,
        down_bias_grad,
    )


def solution(mesh):
    lay = Layout(mesh)
    vec, rows, cols, flat = P("col"), P("row", "col"), P("col", "row"), P(("dp", "row"), "col")

    def shards(*args):
        return layer(lay, *args)

    return jax.shard_map(
        shards,
        mesh=mesh,
        in_specs=(flat, flat, P(("dp", "row")), vec, vec, rows, vec, cols, vec, vec, vec, rows, vec, cols, vec),
        out_specs=(flat, flat, vec, vec, rows, vec, cols, vec, vec, vec, rows, vec, cols, vec),
        check_vma=False,
    )
```
